128 devices in a mesh: ctx: 4 (over z), fsdp: 32 (over y, x, core).
Axes of the slice: x: 4, y: 4, z: 4, core: 2. Of those that a mesh axis runs over, the one named last changes fastest.
Arguments:
- tokens: bfloat16 [32, 512, 1024], P('fsdp', 'ctx'), may hold values from -6 to 6
- segments: int32 [32, 512], P('fsdp'), may hold values from 0 to 4, as said below
- cotangent: bfloat16 [32, 512, 1024], P('fsdp', 'ctx'), may hold values from -6 to 6
- gain_in: float32 [1024], P(('ctx', 'fsdp')), may hold values from 0.5 to 1.5
- mamba_in: float32 [1024, 3072], P(('ctx', 'fsdp')), may hold values from -0.1875 to 0.1875
- mamba_bc: float32 [1024, 256], P(('ctx', 'fsdp')), may hold values from -0.1875 to 0.1875
- mamba_step: float32 [1024, 24], P(('ctx', 'fsdp')), may hold values from -0.1875 to 0.1875
- in_query: float32 [1024, 512], P(('ctx', 'fsdp')), may hold values from -0.1875 to 0.1875
- in_key: float32 [1024, 128], P(('ctx', 'fsdp')), may hold values from -0.1875 to 0.1875
- in_value: float32 [1024, 128], P(('ctx', 'fsdp')), may hold values from -0.1875 to 0.1875
- mamba_out: float32 [1536, 1024], P(('ctx', 'fsdp')), may hold values from -0.15625 to 0.15625
- attn_out: float32 [512, 1024], P(('ctx', 'fsdp')), may hold values from -1 to 1
- gain_mid: float32 [1024], P(('ctx', 'fsdp')), may hold values from 0.5 to 1.5
- ffn_gate: float32 [1024, 2048], P(('ctx', 'fsdp')), may hold values from -0.1875 to 0.1875
- ffn_up: float32 [1024, 2048], P(('ctx', 'fsdp')), may hold values from -0.1875 to 0.1875
- ffn_down: float32 [2048, 1024], P(('ctx', 'fsdp')), may hold values from -0.125 to 0.125
- conv_taps: float32 [4, 1792], replicated, may hold values from -0.5 to 0.5
- conv_bias: float32 [1792], replicated, may hold values from -0.5 to 0.5
- step_bias: float32 [24], replicated, may hold values from -1 to 1
- decay_log: float32 [24], replicated, may hold values from -6.9 to -2.8
- skip_gain: float32 [24], replicated, may hold values from 0.5 to 1.5
Outputs:
- output: bfloat16 [32, 512, 1024], P('fsdp', 'ctx')
- grad_tokens: bfloat16 [32, 512, 1024], P('fsdp', 'ctx')
- grad_gain_in: float32 [1024], P(('ctx', 'fsdp'))
- grad_mamba_in: float32 [1024, 3072], P(('ctx', 'fsdp'))
- grad_mamba_bc: float32 [1024, 256], P(('ctx', 'fsdp'))
- grad_mamba_step: float32 [1024, 24], P(('ctx', 'fsdp'))
- grad_query: float32 [1024, 512], P(('ctx', 'fsdp'))
- grad_key: float32 [1024, 128], P(('ctx', 'fsdp'))
- grad_value: float32 [1024, 128], P(('ctx', 'fsdp'))
- grad_mamba_out: float32 [1536, 1024], P(('ctx', 'fsdp'))
- grad_attn_out: float32 [512, 1024], P(('ctx', 'fsdp'))
- grad_gain_mid: float32 [1024], P(('ctx', 'fsdp'))
- grad_ffn_gate: float32 [1024, 2048], P(('ctx', 'fsdp'))
- grad_ffn_up: float32 [1024, 2048], P(('ctx', 'fsdp'))
- grad_ffn_down: float32 [2048, 1024], P(('ctx', 'fsdp'))
- grad_conv_taps: float32 [4, 1792], replicated
- grad_conv_bias: float32 [1792], replicated
- grad_step_bias: float32 [24], replicated
- grad_decay_log: float32 [24], replicated
- grad_skip_gain: float32 [24], replicated
The draws below stay inside these ranges and needn't reach their ends.
Inputs may be any that keep to these rules, and one draw needn't show every extreme that they name: `segments`: document numbers never fall along a sequence; each sequence holds five documents, one of which has positions in every block of 128.
All inputs are finite; a program needn't handle non-finite values.
Results may differ from the reference program's by a relative error of at most 0.018.
Values may be sent and summed in bfloat16 or wider, within the bound.
A program may use at most 192 MiB of HBM per device.

```python
import jax
import jax.numpy as jnp
from jax import lax

D = 1024
SSM_HEADS = 24
SSM_HEAD = 64
STATE = 128
CONV = 4
Q_HEADS = 8
KV_HEADS = 2
HEAD_DIM = 64
FF = 2048
TOK_DEV = 128
SPAN = 128
SSM_WIDTH = 1536
CONV_CH = 1792
LEN = 512
SEQS = 32


def draw_segments(key, part):
    key = jax.random.fold_in(key, 5)
    pieces = jax.random.split(key, 4)
    doc_start = jax.random.randint(pieces[0], (SEQS,), 2, TOK_DEV)
    doc_first = jax.random.randint(pieces[1], (SEQS,), 1, doc_start)
    doc_finish = jax.random.randint(pieces[2], (SEQS,), LEN - TOK_DEV + 1, LEN - 1)
    doc_last = jax.random.randint(pieces[3], (SEQS,), doc_finish + 1, LEN)
    order = jnp.arange(LEN, dtype=jnp.int32)[None, :]
    total = (order >= doc_first[:, None]).astype(jnp.int32) + (order >= doc_start[:, None]).astype(jnp.int32)
    total = total + (order >= doc_finish[:, None]).astype(jnp.int32) + (order >= doc_last[:, None]).astype(jnp.int32)
    return total.astype(jnp.int32)


def draw_decay_log(key, part):
    key = jax.random.fold_in(key, 11)
    return jax.random.uniform(key, (SSM_HEADS,), jnp.float32, -6.2, -2.8)


def level_of(stream_key, extent, cuts, smallest, top_value):
    gain = 1.0
    for axis_at, blocks in cuts:
        heights = jax.random.uniform(jax.random.fold_in(jax.random.fold_in(stream_key, 6), axis_at), (blocks,), jnp.float32, smallest / len(cuts), top_value / len(cuts))
        gain = gain * jnp.repeat(jnp.exp(heights), extent[axis_at] // blocks).reshape((-1,) + (1,) * (len(extent) - 1 - axis_at))
    return gain


def gaussian(rng, shape, scale, bound, cuts=(), kind=jnp.bfloat16):
    drawn = scale * jax.random.normal(rng, shape, jnp.float32)
    if cuts:
        drawn = drawn * level_of(rng, shape, cuts, -0.22, 0.18)
    return jnp.clip(drawn, -bound, bound).astype(kind)


def setup_inputs(seed: int = 0) -> dict:
    arg_keys = jax.random.split(jax.random.key(seed), 22)
    tokens = gaussian(arg_keys[0], (SEQS, LEN, D), 1.0, 6.0, ((0, 32), (1, 4)))
    segments = draw_segments(jax.random.fold_in(arg_keys[21], 71), 0)
    cotangent = gaussian(arg_keys[2], (SEQS, LEN, D), 1.0, 6.0, ((0, 32), (1, 4)))
    gain_in = jnp.clip(1.0 + 0.1 * jax.random.normal(arg_keys[3], (D,), jnp.float32), 0.5, 1.5)
    mamba_in = gaussian(arg_keys[4], (D, 2 * SSM_WIDTH), D ** -0.5, 0.1875, ((0, 128),), jnp.float32)
    mamba_bc = gaussian(arg_keys[5], (D, 2 * STATE), D ** -0.5, 0.1875, ((0, 128),), jnp.float32)
    mamba_step = gaussian(arg_keys[6], (D, SSM_HEADS), D ** -0.5, 0.1875, ((0, 128),), jnp.float32)
    in_query = gaussian(arg_keys[7], (D, Q_HEADS * HEAD_DIM), D ** -0.5, 0.1875, ((0, 128),), jnp.float32)
    in_key = gaussian(arg_keys[8], (D, KV_HEADS * HEAD_DIM), D ** -0.5, 0.1875, ((0, 128),), jnp.float32)
    in_value = gaussian(arg_keys[9], (D, KV_HEADS * HEAD_DIM), D ** -0.5, 0.1875, ((0, 128),), jnp.float32)
    mamba_out = gaussian(arg_keys[10], (SSM_WIDTH, D), SSM_WIDTH ** -0.5, 0.15625, ((0, 128),), jnp.float32)
    attn_out = gaussian(arg_keys[11], (Q_HEADS * HEAD_DIM, D), (Q_HEADS * HEAD_DIM // 16) ** -0.5, 1.0, ((0, 128),), jnp.float32)
    gain_mid = jnp.clip(1.0 + 0.1 * jax.random.normal(arg_keys[12], (D,), jnp.float32), 0.5, 1.5)
    ffn_gate = gaussian(arg_keys[13], (D, FF), D ** -0.5, 0.1875, ((0, 128),), jnp.float32)
    ffn_up = gaussian(arg_keys[14], (D, FF), D ** -0.5, 0.1875, ((0, 128),), jnp.float32)
    ffn_down = gaussian(arg_keys[15], (FF, D), FF ** -0.5, 0.125, ((0, 128),), jnp.float32)
    conv_taps = jnp.clip(jax.random.uniform(arg_keys[16], (CONV, CONV_CH), jnp.float32, -0.5, 0.5), -0.5, 0.5)
    conv_bias = jnp.clip(jax.random.uniform(arg_keys[17], (CONV_CH,), jnp.float32, -0.5, 0.5), -0.5, 0.5)
    step_bias = jnp.clip(jax.random.uniform(arg_keys[18], (SSM_HEADS,), jnp.float32, -1.0, 1.0), -1.0, 1.0)
    decay_log = draw_decay_log(jax.random.fold_in(arg_keys[21], 71), 0)
    skip_gain = jnp.clip(jax.random.uniform(arg_keys[20], (SSM_HEADS,), jnp.float32, 0.5, 1.5), 0.5, 1.5)
    return {"tokens": tokens, "segments": segments, "cotangent": cotangent, "gain_in": gain_in, "mamba_in": mamba_in, "mamba_bc": mamba_bc, "mamba_step": mamba_step, "in_query": in_query, "in_key": in_key, "in_value": in_value, "mamba_out": mamba_out, "attn_out": attn_out, "gain_mid": gain_mid, "ffn_gate": ffn_gate, "ffn_up": ffn_up, "ffn_down": ffn_down, "conv_taps": conv_taps, "conv_bias": conv_bias, "step_bias": step_bias, "decay_log": decay_log, "skip_gain": skip_gain}


eps = 1e-06
rope_base = 100000000000.0
highest = lax.Precision.HIGHEST

@jax.custom_vjp
def low(v):
    return lax.optimization_barrier(v.astype(jnp.bfloat16)).astype(jnp.float32)

@jax.custom_vjp
def low_back(v):
    return v

def low_keep(v):
    return (low(v), None)

def low_pass(kept, grad):
    return (grad,)

def back_keep(v):
    return (v, None)

def back_low(kept, grad):
    return (low(grad),)
low.defvjp(low_keep, low_pass)
low_back.defvjp(back_keep, back_low)

def matmul(left_side, right_side):
    return jnp.dot(left_side, right_side, precision=highest)

def rms_scale(values, scales):
    return values * lax.rsqrt(lax.optimization_barrier(jnp.mean(values * values, axis=-1, keepdims=True)) + eps) * scales

def rotate(values, positions):
    half_dim = values.shape[-1] // 2
    frequency = rope_base ** (-2.0 * jnp.arange(half_dim, dtype=jnp.float32) / values.shape[-1])
    angles = positions.astype(jnp.float32)[:, None] * frequency[None, :]
    cosine = jnp.cos(angles)[:, None, :]
    sine_part = jnp.sin(angles)[:, None, :]
    front_part = values[..., :half_dim]
    back_part = values[..., half_dim:]
    return jnp.concatenate([front_part * cosine - back_part * sine_part, front_part * sine_part + back_part * cosine], axis=-1)

def attend(queries, keys, values, query_seg, key_seg, query_pos):
    group_size = queries.shape[1] // keys.shape[1]
    key_rep = jnp.repeat(keys, group_size, axis=1)
    value_rep = jnp.repeat(values, group_size, axis=1)
    row_count = queries.shape[0]
    block_rows = min(row_count, 512)
    scale_factor = queries.shape[2] ** (-0.5)
    key_pos = jnp.arange(keys.shape[0], dtype=jnp.int32)

    def one_block(start_row):
        block_query = lax.dynamic_slice_in_dim(queries, start_row, block_rows, 0)
        block_seg = lax.dynamic_slice_in_dim(query_seg, start_row, block_rows, 0)
        block_pos = lax.dynamic_slice_in_dim(query_pos, start_row, block_rows, 0)
        scores = low_back(jnp.einsum('qhd,khd->hqk', block_query, key_rep, precision=highest) * scale_factor)
        allowed = (block_seg[:, None] == key_seg[None, :]) & (key_pos[None, :] <= block_pos[:, None])
        scores = jnp.where(allowed[None], scores, -1e+30)
        shifted = jnp.exp(scores - lax.optimization_barrier(jnp.max(scores, axis=-1, keepdims=True)))
        weights = low(shifted / lax.optimization_barrier(jnp.sum(shifted, axis=-1, keepdims=True)))
        return jnp.einsum('hqk,khd->qhd', weights, value_rep, precision=highest)
    start_rows = jnp.arange(row_count // block_rows, dtype=jnp.int32) * block_rows
    return lax.map(jax.checkpoint(one_block), start_rows).reshape(row_count, -1)

def conv_rows(extended, ext_seg, row_seg, conv_taps, conv_bias):
    row_count = row_seg.shape[0]
    kernel = conv_taps.shape[0]
    total = jnp.zeros((row_count, extended.shape[1]), extended.dtype) + conv_bias[None, :]
    for tap_index in range(kernel):
        offset = kernel - 1 - tap_index
        same_doc = (ext_seg[offset:offset + row_count] == row_seg).astype(extended.dtype)
        total = total + conv_taps[tap_index][None, :] * extended[offset:offset + row_count] * same_doc[:, None]
    return jax.nn.silu(total)

def span_parts(heads_x, write_rows, read_rows, step_size, log_decay, span_seg, seg_before):
    size_rows = heads_x.shape[0]
    running = jnp.cumsum(log_decay, axis=0)
    order = jnp.arange(size_rows, dtype=jnp.int32)
    same_doc = (span_seg[:, None] == span_seg[None, :]) & (order[None, :] <= order[:, None])
    spread = running[:, None, :] - running[None, :, :]
    mixing = jnp.exp(jnp.where(same_doc[:, :, None], spread, -10000.0))
    intersection = jnp.dot(read_rows, write_rows.T, precision=highest)
    weights = mixing * intersection[:, :, None] * step_size[None, :, :]
    intra = jnp.einsum('tsh,shp->thp', weights, heads_x, precision=highest)
    inlet = (span_seg == seg_before).astype(heads_x.dtype)[:, None] * jnp.exp(running)
    tail = (span_seg == span_seg[-1]).astype(heads_x.dtype)[:, None] * jnp.exp(running[-1][None, :] - running) * step_size
    local_end = jnp.einsum('sh,shp,sn->hpn', tail, heads_x, write_rows, precision=highest)
    factor = jnp.exp(running[-1]) * (span_seg[-1] == seg_before).astype(heads_x.dtype)
    return (intra, inlet, local_end, factor)

def ssm_sequence(heads_x, write_rows, read_rows, step_size, log_decay, seq_seg):
    row_count = heads_x.shape[0]
    blocks = row_count // SPAN
    items = (heads_x.reshape(blocks, SPAN, SSM_HEADS, SSM_HEAD), write_rows.reshape(blocks, SPAN, STATE), read_rows.reshape(blocks, SPAN, STATE), step_size.reshape(blocks, SPAN, SSM_HEADS), log_decay.reshape(blocks, SPAN, SSM_HEADS), seq_seg.reshape(blocks, SPAN))

    def advance(carry, item):
        state, seg_before = carry
        intra, inlet, local_end, factor = span_parts(item[0], item[1], item[2], item[3], item[4], item[5], seg_before)
        result = intra + inlet[:, :, None] * jnp.einsum('tn,hpn->thp', item[2], state, precision=highest)
        state = factor[:, None, None] * state + local_end
        return ((state, item[5][-1]), result)
    start = (jnp.zeros((SSM_HEADS, SSM_HEAD, STATE), jnp.float32), jnp.int32(-1))
    unused, results = lax.scan(jax.checkpoint(advance), start, items)
    return results.reshape(row_count, SSM_HEADS, SSM_HEAD)

def layer(inputs, seq_seg, big, little):
    gain_in, mamba_in, mamba_bc, mamba_step, in_query, in_key, in_value, mamba_out, attn_out, gain_mid, ffn_gate, ffn_up, ffn_down = big
    conv_taps, conv_bias, step_bias, decay_log, skip_gain = little
    row_count = inputs.shape[0]
    first_norm = low(rms_scale(inputs, gain_in))
    proj_zx = low_back(matmul(first_norm, mamba_in))
    proj_bc = low_back(matmul(first_norm, mamba_bc))
    proj_step = low_back(matmul(first_norm, mamba_step))
    raw_rows = low(jnp.concatenate([proj_zx[:, SSM_WIDTH:], proj_bc], axis=1))
    pad_rows = jnp.zeros((CONV - 1, CONV_CH), jnp.float32)
    pad_seg = jnp.full((CONV - 1,), -1, jnp.int32)
    mixed = conv_rows(jnp.concatenate([pad_rows, raw_rows], 0), jnp.concatenate([pad_seg, seq_seg], 0), seq_seg, conv_taps, conv_bias)
    heads_x = mixed[:, :SSM_WIDTH].reshape(row_count, SSM_HEADS, SSM_HEAD)
    write_rows = mixed[:, SSM_WIDTH:SSM_WIDTH + STATE]
    read_rows = mixed[:, SSM_WIDTH + STATE:]
    step_size = jax.nn.softplus(proj_step + step_bias)
    log_decay = -jnp.exp(decay_log) * step_size
    ssm_rows = ssm_sequence(heads_x, write_rows, read_rows, step_size, log_decay, seq_seg)
    ssm_rows = ssm_rows + skip_gain[None, :, None] * heads_x
    gated = low(ssm_rows.reshape(row_count, SSM_WIDTH) * jax.nn.silu(proj_zx[:, :SSM_WIDTH]))
    mamba_branch = low_back(matmul(gated, mamba_out))
    positions = jnp.arange(row_count, dtype=jnp.int32)
    queries = low(rotate(low_back(matmul(first_norm, in_query)).reshape(row_count, Q_HEADS, HEAD_DIM), positions))
    keys = low(rotate(low_back(matmul(first_norm, in_key)).reshape(row_count, KV_HEADS, HEAD_DIM), positions))
    values = low(low_back(matmul(first_norm, in_value)).reshape(row_count, KV_HEADS, HEAD_DIM))
    heads = attend(queries, keys, values, seq_seg, seq_seg, positions)
    merged = low(low_back(heads))
    attn_branch = low_back(matmul(merged, attn_out))
    middle = inputs + mamba_branch + attn_branch
    second_norm = low(rms_scale(middle, gain_mid))
    gate_proj = low_back(matmul(second_norm, ffn_gate))
    up_proj = low_back(matmul(second_norm, ffn_up))
    hidden = low(jax.nn.silu(gate_proj) * up_proj)
    return middle + low_back(matmul(hidden, ffn_down))

def reference(tokens, segments, cotangent, gain_in, mamba_in, mamba_bc, mamba_step, in_query, in_key, in_value, mamba_out, attn_out, gain_mid, ffn_gate, ffn_up, ffn_down, conv_taps, conv_bias, step_bias, decay_log, skip_gain):
    sharded = (gain_in, mamba_in, mamba_bc, mamba_step, in_query, in_key, in_value, mamba_out, attn_out, gain_mid, ffn_gate, ffn_up, ffn_down)
    small = (conv_taps, conv_bias, step_bias, decay_log, skip_gain)

    def forward(inputs, big, little):
        rounded = tuple((low(member) for member in big))

        def one_sequence(item):
            return layer(item[0], item[1], rounded, little)
        return lax.map(jax.checkpoint(one_sequence), (inputs, segments))
    outputs, pull = jax.vjp(forward, tokens.astype(jnp.float32), sharded, small)
    grad_inputs, grad_big, grad_small = pull(cotangent.astype(jnp.float32))
    return (outputs.astype(jnp.bfloat16), grad_inputs.astype(jnp.bfloat16), grad_big[0], grad_big[1], grad_big[2], grad_big[3], grad_big[4], grad_big[5], grad_big[6], grad_big[7], grad_big[8], grad_big[9], grad_big[10], grad_big[11], grad_big[12], grad_small[0], grad_small[1], grad_small[2], grad_small[3], grad_small[4])
```

```python
import types

import jax
import jax.numpy as jnp
import numpy as np
from jax import lax
from jax.experimental import pallas as pl
from jax.experimental.pallas import tpu as pltpu
from jax.sharding import PartitionSpec as P

BF = jnp.bfloat16
F32 = jnp.float32
MESH = pl.DeviceIdType.MESH
HI = lax.Precision.HIGHEST
EPS = 1e-06
ROPE = 100000000000.0

D = 1024
LEN = 512
ROWS = 128
HEADS = 6
XW = 384
CW = 640
GW = 384
PK = 3584
FW = 512


def mm(a, b):
    return lax.dot_general(a, b, (((1,), (0,)), ((), ())), preferred_element_type=F32)


def mm_nt(a, b):
    return lax.dot_general(a, b, (((1,), (1,)), ((), ())), preferred_element_type=F32)


def mm_tn(a, b):
    return lax.dot_general(a, b, (((0,), (0,)), ((), ())), preferred_element_type=F32)


def mm_exact(a, b):
    return lax.dot_general(
        a, b, (((1,), (0,)), ((), ())), precision=HI, preferred_element_type=F32
    )


def iota(shape, dim):
    return lax.broadcasted_iota(jnp.int32, shape, dim)


def lane_low(shape):
    return iota(shape, 1) % 128 < 64


def roll(v, shift, axis):
    size = v.shape[axis]
    return pltpu.roll(v, shift % size, axis)


def swap_halves(v):
    lanes = v.shape[1]
    first = iota(v.shape, 1) % 64 < 32
    return jnp.where(first, roll(v, lanes - 32, 1), roll(v, 32, 1))


def sigmoid(v):
    return 1.0 / (1.0 + jnp.exp(-v))


def softplus(v):
    return jnp.maximum(v, 0.0) + jnp.log1p(jnp.exp(-jnp.abs(v)))


def spread_heads(v):
    rows = v.shape[0]
    low = lane_low((rows, 128))
    tiles = []
    for pair in range(HEADS // 2):
        a = jnp.broadcast_to(v[:, 2 * pair : 2 * pair + 1], (rows, 128))
        b = jnp.broadcast_to(v[:, 2 * pair + 1 : 2 * pair + 2], (rows, 128))
        tiles.append(jnp.where(low, a, b))
    return jnp.concatenate(tiles, axis=1)


def mm_terms(a, b, count):
    side = 0 if a.dtype == F32 else 1
    rest, total = (a, b)[side], None
    for _ in range(count):
        term = rest.astype(BF)
        rest = rest - term.astype(F32)
        one = mm(term, b) if side == 0 else mm(a, term)
        total = one if total is None else total + one
    return total


def sum_heads(v):
    pick = (iota((XW, 128), 0) // 64 == iota((XW, 128), 1)).astype(BF)
    return mm_terms(v, pick, 2)


def lower_ones():
    return (iota((ROWS, ROWS), 1) <= iota((ROWS, ROWS), 0)).astype(BF)


LATE, EARLY, OUT = (0, 2 * GW), (2 * GW, 2 * GW), (4 * GW, 512)
FIN, FOUT = (2048, 2 * FW), (2048 + 2 * FW, 512)
FFN = (FIN[0], FIN[1] + FOUT[1])


def chunk(R, core, kind, k, lo=0, width=GW):
    v = R.win[core, k // 2, :, :, :, pl.ds(kind[0] + GW * (k % 2) + lo, width)]
    return v.reshape(256, width)


def group_weight(R, core, kind):
    return jnp.concatenate([chunk(R, core, kind, k) for k in range(4)], axis=0)


def out_weight(R, kind=OUT):
    parts = []
    for core in range(2):
        rows = [R.win[core, d, :, :, :, pl.ds(kind[0], 512)].reshape(256, 512) for d in range(2)]
        parts.append(jnp.concatenate(rows, axis=0))
    return jnp.concatenate(parts, axis=1)


def seg_mask(R, k):
    seg = R.segc[...]
    return jnp.where(
        (seg == roll(seg, k, 0)) & (iota((LEN, 128), 0) >= k), 1.0, 0.0
    ).astype(F32)


def gains(R):
    pick = (iota((8, 128), 1) == iota((8, 128), 0) + 24).astype(BF)
    for k in range(4):
        R.gain[:, pl.ds(256 * k, 256)] = mm_nt(pick, chunk(R, 1, LATE, k, 256, 128))


def norm_first(R):
    gain = R.gain[0:1, :]

    def block(b, carry):
        x = R.xall[b].astype(F32)
        inv = lax.rsqrt(jnp.mean(x * x, axis=-1, keepdims=True) + EPS)
        R.first[pl.ds(pl.multiple_of(b * ROWS, ROWS), ROWS), :] = (x * inv * gain).astype(BF)
        return carry

    lax.fori_loop(0, 4, block, 0)


def project_late(R):
    first = R.first[...]
    out = mm(first, group_weight(R, 0, LATE))
    R.raw[:, 0:384] = out.astype(BF)
    out = mm(first, group_weight(R, 1, LATE))
    R.raw[:, 384:640] = out[:, 0:256].astype(BF)
    R.pm[...] = out[:, 256:384]


def project_early(R):
    first = R.first[...]
    out = mm(first, group_weight(R, 1, EARLY))
    R.pq[...] = out[:, 0:128]
    R.pkv[...] = out[:, 128:256]
    R.gate[...] = mm(first, group_weight(R, 0, EARLY))


def convolve(R):
    masks = [seg_mask(R, k) for k in range(1, 4)]
    for t in range(CW // 128):
        cols = slice(128 * t, 128 * t + 128)
        raw = R.raw[:, cols].astype(F32)
        total = R.cpar[4:5, cols] + R.cpar[0:1, cols] * raw
        for k in range(1, 4):
            total = total + R.cpar[k : k + 1, cols] * (roll(raw, k, 0) * masks[k - 1])
        R.pre[:, cols] = total
        R.mixed[:, cols] = total * sigmoid(total)


def steps(R):
    step = softplus(R.pm[...] + R.hpar[0:1, :])
    R.step[...] = step
    decay = -jnp.exp(R.hpar[1:2, :])
    ones = lower_ones()
    for b in range(4):
        rows = slice(b * ROWS, b * ROWS + ROWS)
        R.run[rows, :] = mm_terms(ones, decay * step[rows, :], 3)


def span(R, b):
    s = types.SimpleNamespace()
    s.at = pl.multiple_of(b * ROWS, ROWS)
    s.rows = pl.ds(s.at, ROWS)
    s.xs = R.mixed[s.rows, 0:384]
    s.xs_low = s.xs.astype(BF)
    s.wr_low = R.mixed[s.rows, 384:512].astype(BF)
    s.rd_low = R.mixed[s.rows, 512:640].astype(BF)
    s.step = R.step[s.rows, :]
    return s


def recurrence(R, begin, end):
    low = lane_low((ROWS, 128))

    def block(b, carry):
        s = span(R, b)
        run = R.run[s.rows, :]
        run_t = run.T
        seg = R.segc[s.rows, :]
        last = jnp.broadcast_to(seg[ROWS - 1 : ROWS, :], (ROWS, ROWS))
        earlier = R.segc[pl.ds(pl.multiple_of(jnp.maximum(s.at - 8, 0), 8), 8), :][7:8, :]
        earlier = jnp.where(jnp.broadcast_to(b, (1, 128)) == 0, -1.0, earlier)
        causal = (iota((ROWS, ROWS), 1) <= iota((ROWS, ROWS), 0)) & (
            seg == R.segr[0:1, s.rows]
        )
        inlet = jnp.where(seg == earlier, jnp.exp(run), 0.0)
        stop = run[ROWS - 1 : ROWS, :]
        tail0 = jnp.where(seg == last, jnp.exp(stop - run), 0.0)
        factor = jnp.where(last[0:1, :] == earlier, jnp.exp(stop), 0.0)
        inlet_x = spread_heads(inlet)
        step_x = spread_heads(s.step)
        tail_x = spread_heads(tail0)
        xstep = step_x * s.xs
        xstep_low = xstep.astype(BF)
        factor_x = spread_heads(jnp.broadcast_to(factor, (8, 128)))
        R.step_x[s.rows, :] = step_x
        R.factor[b] = jnp.broadcast_to(factor, (8, 128))
        R.inlet_x[s.rows, :] = inlet_x
        R.tail_x[s.rows, :] = tail_x
        R.factor_x[b] = factor_x
        cross = mm_nt(s.rd_low, s.wr_low)
        state = R.state[b]
        inflow = mm(s.rd_low, state.astype(BF))
        tiles = []
        for pair in range(HEADS // 2):
            xp = xstep_low[:, 128 * pair : 128 * pair + 128]
            both = []
            for h in (2 * pair, 2 * pair + 1):
                spread = run[:, h : h + 1] - run_t[h : h + 1, :]
                mix = jnp.exp(jnp.where(causal, spread, -10000.0))
                weights = (mix * cross).astype(BF)
                R.mix[b, h] = mix.astype(BF)
                R.weights[b, h] = weights
                both.append(mm(weights, xp))
            tiles.append(jnp.where(low, both[0], both[1]))
        R.ssm[s.rows, :] = (
            jnp.concatenate(tiles, axis=1) + inlet_x * inflow + R.cpar[5:6, 0:384] * s.xs
        )
        R.state[b + 1] = factor_x[0:1, :] * state + mm_tn(
            s.wr_low, (tail_x * xstep).astype(BF)
        )
        return carry

    lax.fori_loop(begin, end, block, 0)


def rotate(v, cosr, sinr):
    return v * cosr + swap_halves(v) * sinr


def rotated(R):
    low = lane_low((LEN, 128))
    R.q[...] = rotate(R.pq[...], R.cosr[...], R.sinr[...]).astype(BF)
    pkv = R.pkv[...]
    k = rotate(pkv, R.cosr[...], R.sinr[...])
    R.kk[...] = jnp.where(low, k, roll(k, 64, 1)).astype(BF)
    R.vv[...] = jnp.where(low, roll(pkv, 64, 1), pkv).astype(BF)


def half_only(v, e):
    low = lane_low(v.shape)
    return jnp.where(low if e == 0 else ~low, v, jnp.zeros_like(v))


def attend(R, begin, end):
    low = lane_low((ROWS, 128))
    for i in range(begin, end):
        rows = slice(i * ROWS, i * ROWS + ROWS)
        n = (i + 1) * ROWS
        seg_row = R.segr[0:1, 0:n]
        seg_col = jnp.broadcast_to(R.segc[rows, 0:1], (ROWS, n))
        allowed = (iota((ROWS, n), 1) <= iota((ROWS, n), 0) + i * ROWS) & (seg_col == seg_row)
        outs = []
        for e in range(2):
            scores = mm_nt(half_only(R.q[rows, :], e), R.kk[0:n, :]) * 0.125
            scores = jnp.where(allowed, scores, -1e30)
            shifted = jnp.exp(scores - jnp.max(scores, axis=-1, keepdims=True))
            probs = (shifted / jnp.sum(shifted, axis=-1, keepdims=True)).astype(BF)
            R.probs[e, rows, 0:n] = probs
            outs.append(mm(probs, R.vv[0:n, :]))
        R.left[rows, 384:512] = jnp.where(low, outs[0], outs[1]).astype(BF)


def out_project(R, h):
    rows = slice(256 * h, 256 * h + 256)
    gate = R.gate[rows, :]
    R.left[rows, 0:384] = (R.ssm[rows, :] * (gate * sigmoid(gate))).astype(BF)
    left = mm(R.left[rows, :], R.perm5[...]).astype(BF)
    R.left_p[rows, :] = left
    out = mm(left, out_weight(R))
    for j in range(4):
        R.branch[h, j] = out[64 * j : 64 * j + 64, :].astype(BF)


def unit_chunk(R, core, k):
    lo = FIN[0] + FW * (k % 2)
    return R.win[core, k // 2, :, :, :, lo : lo + FW].reshape(256, FW)


def ffn(R, h):
    second = R.secall[h].reshape(256, D)
    cot = R.cotall[2 * h : 2 * h + 2].reshape(256, D)
    rows = slice(256 * h, 256 * h + 256)
    for d in range(2):
        cols = slice(256 * d, 256 * d + 256)
        weights = []
        for core in range(2):
            parts = [unit_chunk(R, core, k)[:, cols] for k in range(4)]
            weights.append(jnp.concatenate(parts, axis=0))
        a = mm(second, weights[0])
        b = mm(second, weights[1])
        down = jnp.concatenate(
            [R.win[core, d, :, :, :, FOUT[0] : PK].reshape(256, 512) for core in range(2)], axis=1
        )
        ghid = mm_nt(cot, down)
        sig = sigmoid(a)
        act = a * sig
        R.hid[rows, cols] = (act * b).astype(BF)
        R.gab[rows, cols] = (ghid * b * (sig + act * (1.0 - sig))).astype(BF)
        R.gab[rows, FW + 256 * d : FW + 256 * d + 256] = (ghid * act).astype(BF)
    for k in range(4):
        weights = jnp.concatenate([unit_chunk(R, core, k) for core in range(2)], axis=1)
        out = mm_nt(R.gab[rows, :], weights)
        for j in range(4):
            R.gsec[h, j, :, 256 * k : 256 * k + 256] = out[64 * j : 64 * j + 64, :].astype(BF)


def ffn_out(R, L):
    out = mm(R.hid[...], out_weight(R, FOUT))
    for b in range(4):
        R.fout[b] = out[b * ROWS : b * ROWS + ROWS, :].astype(BF)
    for h in range(2):
        block, rows = mid_rows(L, h)
        R.fout[block, rows, :] = (
            R.fout[block, rows, :].astype(F32) + R.middle[h]
        ).astype(BF)


def ffn_grads(R):
    second = R.secall[...].reshape(LEN, D)
    for k in range(4):
        out = mm_tn(second[:, 256 * k : 256 * k + 256], R.gab[...]).astype(BF)
        lo = FIN[0] + FW * (k % 2)
        for core in range(2):
            part = out[:, FW * core : FW * core + FW]
            R.win[core, k // 2, :, :, :, lo : lo + FW] = part.reshape(4, 4, 16, FW)
    put_out_grad(R.win, FOUT, mm_tn(R.hid[...], R.cotall[...].reshape(LEN, D)))


def norm_back(x, gain, grad):
    inv = lax.rsqrt(jnp.mean(x * x, axis=-1, keepdims=True) + EPS)
    unit = x * inv
    scaled = grad * gain
    return inv * (scaled - unit * jnp.mean(scaled * unit, axis=-1, keepdims=True))


def mid_rows(L, h):
    return 2 * h + lax.div(L.z, 2), pl.ds(pl.multiple_of(64 * lax.rem(L.z, 2), 64), 64)


def back_out(R, h):
    rows = slice(256 * h, 256 * h + 256)
    raw = mm_nt(R.gball[h].reshape(256, D), out_weight(R))
    perm = R.perm5[...]
    hi = raw.astype(BF)
    rest = raw - hi.astype(F32)
    R.gleft[rows, :] = mm_nt(hi, perm) + mm_nt(rest.astype(BF), perm)


def back_gate(R):
    def block(b, carry):
        rows = pl.ds(pl.multiple_of(b * ROWS, ROWS), ROWS)
        gate = R.gate[rows, :]
        sig = sigmoid(gate)
        grad = R.gleft[rows, 0:384] * R.ssm[rows, :]
        R.gproj[rows, 768:1152] = (grad * (sig + gate * sig * (1.0 - sig))).astype(BF)
        return carry

    lax.fori_loop(0, 4, block, 0)


def back_attend(R, begin, end):
    low = lane_low((ROWS, 128))
    for i in range(begin, end):
        rows = slice(i * ROWS, i * ROWS + ROWS)
        n = (i + 1) * ROWS
        go = R.gleft[rows, 384:512].astype(BF)
        outs = []
        for e in range(2):
            probs = R.probs[e, rows, 0:n]
            pf = probs.astype(F32)
            go_e = half_only(go, e)
            dp = mm_nt(go_e, R.vv[0:n, :])
            ds = (pf * (dp - jnp.sum(pf * dp, axis=-1, keepdims=True))).astype(BF)
            outs.append(mm(ds, R.kk[0:n, :]))
            R.gk[0:n, :] += mm_tn(ds, half_only(R.q[rows, :], e))
            R.gv[0:n, :] += mm_tn(probs, go_e)
        R.gq[rows, :] = jnp.where(low, outs[0], outs[1]) * 0.125


def back_rotated(R):
    cosr, sinr = R.cosr[...], R.sinr[...]
    gq = rotate(R.gq[...], cosr, -sinr)
    R.gproj[:, 1152:1280] = gq.astype(BF)
    gk = R.gk[...] * 0.125
    gk = rotate(gk + roll(gk, 64, 1), cosr, -sinr)
    gv = R.gv[...]
    gv = gv + roll(gv, 64, 1)
    R.gproj[:, 1280:1408] = jnp.where(lane_low((LEN, 128)), gk, gv).astype(BF)
    R.gproj[:, 1408:1536] = jnp.zeros((LEN, 128), BF)


def back_recurrence(R):
    R.gstate[...] = jnp.zeros((128, XW), F32)
    R.hsum[...] = jnp.zeros((8, 128), F32)
    low = lane_low((ROWS, 128))
    lane = iota((ROWS, 128), 1)
    sub = iota((ROWS, 128), 0)
    upper = (iota((ROWS, ROWS), 1) >= iota((ROWS, ROWS), 0)).astype(BF)

    def block(i, carry):
        b = 3 - i
        s = span(R, b)
        state = R.state[b]
        state_low = state.astype(BF)
        gstate = R.gstate[...]
        gstate_low = gstate.astype(BF)
        gate = R.gate[s.rows, :]
        gy = R.gleft[s.rows, 0:384] * (gate * sigmoid(gate))
        gy_low = gy.astype(BF)
        step_x = R.step_x[s.rows, :]
        tail_x = R.tail_x[s.rows, :]
        xstep = step_x * s.xs
        xstep_low = xstep.astype(BF)
        skip = R.cpar[5:6, 0:384]
        gcross = jnp.zeros((ROWS, ROWS), F32)
        tiles = []
        for pair in range(HEADS // 2):
            cols = slice(128 * pair, 128 * pair + 128)
            gp = gy_low[:, cols]
            both = []
            for e in range(2):
                h = 2 * pair + e
                both.append(mm_tn(R.weights[b, h], gp))
                gm = mm_nt(half_only(gp, e), xstep_low[:, cols])
                gcross = gcross + gm * R.mix[b, h].astype(F32)
            tiles.append(jnp.where(low, both[0], both[1]))
        inside = jnp.concatenate(tiles, axis=1)
        outflow = tail_x * mm(s.wr_low, gstate_low)
        flow_low = (R.inlet_x[s.rows, :] * gy).astype(BF)
        gcross_low = gcross.astype(BF)
        R.gmix[s.rows, 0:384] = (inside + outflow) * step_x + skip * gy
        R.gmix[s.rows, 384:512] = mm_tn(gcross_low, s.rd_low) + mm_nt(
            (tail_x * xstep).astype(BF), gstate_low
        )
        R.gmix[s.rows, 512:640] = mm(gcross_low, s.wr_low) + mm_nt(flow_low, state_low)
        ends = jnp.concatenate(
            [
                jnp.sum(gstate * state, axis=0, keepdims=True),
                jnp.sum(gy * s.xs, axis=0, keepdims=True),
                jnp.zeros((6, XW), F32),
            ],
            axis=0,
        )
        sums = sum_heads(
            jnp.concatenate(
                [
                    gy * (R.ssm[s.rows, :] - skip * s.xs),
                    inside * s.xs,
                    outflow * s.xs,
                    ends,
                ],
                axis=0,
            )
        )
        row_part = sums[0:ROWS, :]
        col_part = sums[ROWS : 2 * ROWS, :]
        through = sums[2 * ROWS : 3 * ROWS, :]
        gfactor = sums[3 * ROWS : 3 * ROWS + 1, :]
        grun = row_part - (col_part + through) * s.step
        at_end = (
            jnp.sum(through * s.step, axis=0, keepdims=True) + gfactor * R.factor[b, 0:1, :]
        )
        grun = grun + jnp.where(sub == ROWS - 1, at_end, 0.0)
        glog = mm_terms(upper, grun, 3)
        decay = -jnp.exp(R.hpar[1:2, :])
        gstep = col_part + through + glog * decay
        drive = R.pm[s.rows, :] + R.hpar[0:1, :]
        gdrive = jnp.where(lane < HEADS, gstep * sigmoid(drive), 0.0)
        R.gproj[s.rows, 640:768] = gdrive.astype(BF)
        R.hsum[0:1, :] += jnp.sum(gdrive, axis=0, keepdims=True)
        R.hsum[1:2, :] += jnp.sum(glog * decay * s.step, axis=0, keepdims=True)
        R.hsum[2:3, :] += sums[3 * ROWS + 1 : 3 * ROWS + 2, :]
        R.gstate[...] = R.factor_x[b, 0:1, :] * gstate + mm_tn(s.rd_low, flow_low)
        return carry

    lax.fori_loop(0, 4, block, 0)


def back_convolve(R):
    masks = [seg_mask(R, k) for k in range(1, 4)]
    for t in range(CW // 128):
        cols = slice(128 * t, 128 * t + 128)
        pre = R.pre[:, cols]
        raw = R.raw[:, cols].astype(F32)
        sig = sigmoid(pre)
        gpre = R.gmix[:, cols] * (sig + pre * sig * (1.0 - sig))
        graw = R.cpar[0:1, cols] * gpre
        R.small[0:1, cols] = jnp.sum(gpre * raw, axis=0, keepdims=True)
        for k in range(1, 4):
            masked = gpre * masks[k - 1]
            graw = graw + R.cpar[k : k + 1, cols] * roll(masked, LEN - k, 0)
            R.small[k : k + 1, cols] = jnp.sum(masked * roll(raw, k, 0), axis=0, keepdims=True)
        R.small[4:5, cols] = jnp.sum(gpre, axis=0, keepdims=True)
        R.gproj[:, cols] = graw.astype(BF)


def back_first(R, L):
    places = ((0, LATE), (1, LATE), (0, EARLY), (1, EARLY))
    gain = R.gain[0:1, :]
    moves = []
    for n, k in enumerate((2, 1, 3, 0)):
        b = L.around("z", k)
        rows = pl.ds(pl.multiple_of(b * ROWS, ROWS), ROWS)
        grads = R.gproj[rows, :]
        for q in range(4):
            weights = jnp.concatenate([chunk(R, core, kind, q) for core, kind in places], axis=1)
            R.gsum[:, 256 * q : 256 * q + 256] = mm_nt(grads, weights)
        R.gfirst[b] = norm_back(R.xall[b].astype(F32), gain, R.gsum[...]).astype(BF)
        for h in range(2):
            block, rows = mid_rows(L, h)

            @pl.when(block == b)
            def _():
                mine = R.gfirst[b, rows, :].astype(F32) + R.gmid[h]
                R.gfirst[b, rows, :] = mine.astype(BF)

        if k:
            moves.append(L.copy(R.gfirst.at[b], R.hrecv.at[n], L.device(z=b)))
        yield
    for one in moves:
        one.wait_recv()
    add_blocks(())(R.gfirst.at[L.z], [R.hrecv.at[n] for n in range(3)])


def put_out_grad(buf, kind, out):
    out = out.astype(BF)
    for core in range(2):
        for d in range(2):
            part = out[256 * d : 256 * d + 256, 512 * core : 512 * core + 512]
            buf[core, d, :, :, :, kind[0] : kind[0] + 512] = part.reshape(4, 4, 16, 512)


def out_grad(R):
    put_out_grad(R.dwin, OUT, mm_tn(R.left_p[...], R.gball[...].reshape(LEN, D)))


def put_grad(R, core, kind, k, value):
    lo = kind[0] + GW * (k % 2)
    R.dwin[core, k // 2, :, :, :, lo : lo + GW] = value.astype(BF).reshape(4, 4, 16, GW)


def early_grads(R):
    for k in range(4):
        out = mm_tn(R.first[:, 256 * k : 256 * k + 256], R.gproj[:, 768:1536])
        for core in range(2):
            put_grad(R, core, EARLY, k, out[:, GW * core : GW * core + GW])


def late_grads(R):
    for k in range(4):
        out = mm_tn(R.first[:, 256 * k : 256 * k + 256], R.gproj[:, 0:768])
        for core in range(2):
            put_grad(R, core, LATE, k, out[:, GW * core : GW * core + GW])


class Move:
    def __init__(self, one):
        self.one, self.came, self.went = one, False, False

    def wait_recv(self):
        if not self.came:
            self.one.wait_recv()
            self.came = True

    def wait_send(self):
        if not self.went:
            self.one.wait_send()
            self.went = True


class Links:
    def __init__(self, send, recv):
        self.send, self.recv, self.moves = send, recv, []
        self.z = lax.axis_index("ctx")
        place = lax.axis_index("fsdp")
        self.c = lax.rem(place, 2)
        self.x = lax.rem(lax.div(place, 2), 4)
        self.y = lax.div(place, 8)
        self.at = {"z": self.z, "y": self.y, "x": self.x}
        self.sibling = self.device(c=1 - self.c)

    def device(self, **moved):
        p = dict(z=self.z, y=self.y, x=self.x, c=self.c)
        p.update(moved)
        return (p["z"], (p["y"] * 4 + p["x"]) * 2 + p["c"])

    def copy(self, src, dst, device):
        k = len(self.moves)
        one = pltpu.make_async_remote_copy(
            src_ref=src,
            dst_ref=dst,
            send_sem=self.send.at[k],
            recv_sem=self.recv.at[k],
            device_id=device,
            device_id_type=MESH,
        )
        one.start()
        self.moves.append(Move(one))
        return self.moves[-1]

    def around(self, axis, k):
        return lax.rem(self.at[axis] + k, 4)

    def slab(self):
        for dz in range(4):
            for flip in range(2):
                if dz or flip:
                    yield self.around("z", dz), self.c if flip == 0 else 1 - self.c

    def greet(self):
        barrier = pltpu.get_barrier_semaphore()
        to = [self.device(z=j, c=h) for j, h in self.slab()]
        for axis in ("x", "y"):
            to += [self.device(**{axis: self.around(axis, k)}) for k in range(1, 4)]
        for one in to:
            pl.semaphore_signal(barrier, inc=1, device_id=one, device_id_type=MESH)
        return lambda: pl.semaphore_wait(barrier, len(to))

    def settle(self):
        for one in self.moves:
            one.wait_send()

    def finish(self):
        for one in self.moves:
            one.wait_recv()
            one.wait_send()


def gather(L, axis, slot, arrived=None, log=None):
    me = L.at[axis]
    moves = [
        (k, L.copy(slot(me), slot(me), L.device(**{axis: L.around(axis, k)}))) for k in (2, 1, 3)
    ]
    if log is not None:
        log.extend(one for _, one in moves)
    if arrived:
        arrived(me)
    yield
    for k, one in moves[1:] + moves[:1]:
        one.wait_recv()
        if arrived:
            arrived(L.around(axis, 4 - k))


def reduce(L, axis, src, bufs, add):
    moves = []
    for buf, k in zip(bufs, (2, 1, 3)):
        j = L.around(axis, k)
        moves.append(L.copy(src(j), buf, L.device(**{axis: j})))
    yield
    for one in moves:
        one.wait_recv()
    add(src(L.at[axis]), bufs)


def add_blocks(lead):
    count = int(np.prod(lead)) if lead else 1

    def add(dst, srcs):
        def body(n, carry):
            where = []
            for size in reversed(lead):
                where.append(lax.rem(n, size))
                n = lax.div(n, size)
            where = tuple(reversed(where)) + (slice(None), slice(None))
            total = dst[where].astype(F32)
            for one in srcs:
                total = total + one[where].astype(F32)
            dst[where] = total.astype(BF)
            return carry

        lax.fori_loop(0, count, body, 0)

    return add


def columns(ref, lead, lo, width):
    return ref.at[(slice(None),) * (lead + 1) + (pl.ds(lo, width),)]


def step(*gens):
    for g in gens:
        next(g, None)


def together(*gens):
    gens = list(gens)
    while gens:
        alive = []
        for g in gens:
            try:
                next(g)
                alive.append(g)
            except StopIteration:
                pass
        gens = alive
        if gens:
            yield


def drain(*gens):
    for _ in together(*gens):
        pass


def mixer_slot(L, buf, sub, stage, lo, width):
    ref = buf.at[L.c, sub]
    axis = ("xy" if sub == 0 else "yx")[stage]

    def slot(j):
        if stage == 0:
            block = ref.at[L.y, j] if axis == "x" else ref.at[j, L.x]
        else:
            block = ref.at[j] if axis == "y" else ref.at[:, j]
        return columns(block, stage, lo, width)

    return axis, slot


def gather_mixer(L, R, sub, lo, width, log=None):
    sent = []
    for stage in range(2):
        axis, slot = mixer_slot(L, R.win, sub, stage, lo, width)

        def arrived(j, slot=slot):
            sent.append(L.copy(slot(j), slot(j), L.sibling))

        yield from gather(L, axis, slot, arrived if stage == 1 else None, log)
    if log is not None:
        log.extend(sent)
    yield
    for one in sent:
        one.wait_recv()


def reduce_mixer(L, R, buf, lo, width):
    moves = []
    for sub in range(2):
        theirs = columns(buf.at[1 - L.c, sub], 2, lo, width)
        moves.append(L.copy(theirs, columns(R.wsib.at[sub], 2, lo, width), L.sibling))
    yield
    gens = []
    for sub in range(2):
        moves[sub].wait_recv()
        mine = columns(buf.at[L.c, sub], 2, lo, width)
        add_blocks((4, 4))(mine, [columns(R.wsib.at[sub], 2, lo, width)])
        gens.append(reduce_chips(L, R, buf, sub, lo, width))
        next(gens[-1])
    yield
    yield from together(*gens)


def reduce_chips(L, R, buf, sub, lo, width):
    for stage in (1, 0):
        axis, slot = mixer_slot(L, buf, sub, stage, lo, width)
        bufs = [columns(one.at[sub], stage, lo, width) for one in R.mbufs[stage]]
        yield from reduce(L, axis, slot, bufs, add_blocks((4,) * stage))


def deal_rows(L, buf, kind, width, fin, rfin, place):
    for sub in range(2):
        for k in range(2):
            lo = kind[0] + width * k
            both = buf[L.c, sub, L.y, L.x, :, lo : lo + width].astype(F32)
            for core in range(2):
                fin[2 * sub + k, core, :, place : place + width] = both[8 * core : 8 * core + 8, :]
    cols = pl.ds(place, width)
    moves = [
        L.copy(fin.at[j, h, :, cols], rfin.at[L.z, L.c, :, cols], L.device(z=j, c=h))
        for j, h in L.slab()
    ]
    rfin[L.z, L.c, :, cols] = fin[L.z, L.c, :, cols]
    return moves


def deal_halves(L, buf, kind, fin, rfin):
    for d in range(2):
        fin[d] = buf[L.c, d, L.y, L.x, :, kind[0] : kind[0] + 512].astype(F32)
    return L.copy(fin.at[1 - L.c], rfin, L.sibling)


def reduce_inputs(L, R, kind, place):
    yield from reduce_mixer(L, R, R.dwin, *kind)
    moves = deal_rows(L, R.dwin, kind, GW, R.fin, R.rfin, place)
    yield
    for one in moves:
        one.wait_recv()


def reduce_outputs(L, R):
    yield from reduce_mixer(L, R, R.dwin, *OUT)
    move = deal_halves(L, R.dwin, OUT, R.ofin, R.orfin)
    yield
    move.wait_recv()
    lo, hi = in_core_order(L, R.ofin[L.c], R.orfin[...])
    R.o_mo[:, 0:512] = lo[0:12, :]
    R.o_mo[:, 512:1024] = hi[0:12, :]
    R.o_ao[:, 0:512] = lo[12:16, :]
    R.o_ao[:, 512:1024] = hi[12:16, :]
    R.send_out("o_mo", "o_ao")


def reduce_ffn(L, R):
    yield from reduce_mixer(L, R, R.win, *FFN)
    moves = deal_rows(L, R.win, FIN, FW, R.ffin, R.frfin, 0)
    moves.append(deal_halves(L, R.win, FOUT, R.dfin, R.drfin))
    yield
    for one in moves:
        one.wait_recv()
    lo, hi = in_core_order(L, R.dfin[L.c], R.drfin[...])
    R.o_fd[:, 0:512] = lo
    R.o_fd[:, 512:1024] = hi
    turn = (iota((FW, FW), 1) == deal(iota((FW, FW), 0))).astype(F32)
    rows = [R.frfin[j, core] for core in range(2) for j in range(4)]
    out = mm_exact(jnp.concatenate(rows, axis=0), turn)
    for j in range(4):
        R.o_fg[:, FW * j : FW * j + FW] = out[8 * j : 8 * j + 8, :]
        R.o_fu[:, FW * j : FW * j + FW] = out[32 + 8 * j : 40 + 8 * j, :]
    R.gcol[0] = gain_column([(R.w_fg, R.o_fg), (R.w_fu, R.o_fu)], R.gain_mid)
    R.send_out("o_fd", "o_fg", "o_fu")


def reduce_blocks(L, ref, recv):
    return reduce(L, "z", lambda j: ref.at[j], [recv.at[n] for n in range(3)], add_blocks(()))


def gather_blocks(L, ref):
    return gather(L, "z", lambda j: ref.at[j])


def reduce_small(L, R):
    for part in range(3):
        R.small[5:6, 128 * part : 128 * part + 128] = R.hsum[part : part + 1, :]
    R.smc[L.c] = R.small[...]
    move = L.copy(R.smc.at[L.c], R.smc.at[L.c], L.sibling)
    yield
    move.wait_recv()
    R.smx[L.x] = R.smc[0] + R.smc[1]
    yield from gather(L, "x", lambda j: R.smx.at[j])
    R.smy[L.y] = (R.smx[0] + R.smx[1]) + (R.smx[2] + R.smx[3])
    yield from gather(L, "y", lambda j: R.smy.at[j])
    R.smz[L.z] = (R.smy[0] + R.smy[1]) + (R.smy[2] + R.smy[3])
    yield from gather(L, "z", lambda j: R.smz.at[j])
    for j in range(4):
        R.o_conv[:, 384 * j : 384 * j + 384] = R.smz[j, :, 0:384]
    total = (R.smz[0] + R.smz[1]) + (R.smz[2] + R.smz[3])
    R.o_conv[:, 1536:1792] = total[:, 384:640]
    lane = iota((8, 128), 1)
    for part in range(3):
        heads = jnp.zeros((8, 128), F32)
        for j in range(4):
            one = jnp.where(lane < HEADS, R.smz[j, :, 128 * part : 128 * part + 128], 0.0)
            heads = heads + (one if j == 0 else roll(one, HEADS * j, 1))
        R.o_head[part : part + 1, :] = heads[5:6, :]


def setup(L, R):
    lane = iota((1, 128), 1)
    first = HEADS * L.z
    for row, ref in enumerate((R.step_bias, R.decay_log)):
        total = jnp.zeros((1, 128), F32)
        for h in range(HEADS):
            total = jnp.where(lane == h, ref[first + h], total)
        R.hpar[row : row + 1, :] = total
    cols = pl.ds(pl.multiple_of(XW * L.z, 128), XW)
    R.cpar[0:4, 0:384] = R.taps[:, cols]
    R.cpar[0:4, 384:640] = R.taps[:, 1536:1792]
    R.cpar[4:5, 0:384] = R.bias[:, cols]
    R.cpar[4:5, 384:640] = R.bias[:, 1536:1792]
    lane = iota((1, XW), 1) // 64
    total = jnp.zeros((1, XW), F32)
    for h in range(HEADS):
        total = jnp.where(lane == h, R.skip_gain[first + h], total)
    R.cpar[5:6, 0:384] = total
    seg = R.seg[...].astype(F32)
    R.segr[0:1, :] = seg
    for b in range(4):
        row = seg[:, b * ROWS : b * ROWS + ROWS]
        R.segc[b * ROWS : b * ROWS + ROWS, :] = jnp.broadcast_to(row, (ROWS, ROWS)).T


def pack_weights(L, R):
    shape8 = (8, 128)
    low = lane_low(shape8)
    lane = iota(shape8, 1)
    sub = iota(shape8, 0)
    k, v = R.w_k[...], R.w_v[...]
    k_up, v_up = roll(k, 64, 1), roll(v, 64, 1)
    R.misc[...] = jnp.zeros(shape8, F32)
    R.misc[:, 0:24] = R.w_step[...]
    misc = R.misc[...]
    for row in range(8):
        misc = jnp.where((lane == 24) & (sub == row), R.gain_in[row], misc)
        misc = jnp.where((lane == 25) & (sub == row), R.gain_mid[row], misc)
    for j in range(4):
        R.pack[j, 0, :, 0:384] = R.w_min[:, 1536 + 384 * j : 1920 + 384 * j]
        R.pack[j, 0, :, 384:768] = R.w_min[:, 384 * j : 384 * j + 384]
        R.pack[j, 1, :, 0:256] = R.w_bc[...]
        mine = misc if j == 0 else roll(misc, 128 - HEADS * j, 1)
        R.pack[j, 1, :, 256:384] = jnp.where(
            lane < HEADS, mine, jnp.where((lane >= 24) & (lane < 26), misc, 0.0)
        )
        R.pack[j, 1, :, 384:512] = R.w_q[:, 128 * j : 128 * j + 128]
        R.pack[j, 1, :, 512:640] = jnp.where(low, k, v_up) if j < 2 else jnp.where(low, k_up, v)
        R.pack[j, 1, :, 640:768] = jnp.zeros(shape8, F32)
    for h in range(2):
        R.opack[h, 0:12, :] = R.w_mo[:, 512 * h : 512 * h + 512]
        R.opack[h, 12:16, :] = R.w_ao[:, 512 * h : 512 * h + 512]


def deal(n):
    return 32 * ((n % 256) // 16) + 16 * (n // 256) + n % 16


def pack_ffn(L, R):
    turn = (iota((FW, FW), 0) == deal(iota((FW, FW), 1))).astype(BF)
    rows = [ref[:, FW * j : FW * j + FW] for ref in (R.w_fg, R.w_fu) for j in range(4)]
    out = mm(jnp.concatenate(rows, axis=0).astype(BF), turn)
    for j in range(4):
        R.fpack[j, 0] = out[8 * j : 8 * j + 8, :]
        R.fpack[j, 1] = out[32 + 8 * j : 40 + 8 * j, :]
    for h in range(2):
        R.dpack[h] = R.w_fd[:, 512 * h : 512 * h + 512]


def gain_column(pairs, scalars):
    total = jnp.zeros((8, 1), F32)
    for weight, grad in pairs:
        weight = weight[...].astype(BF).astype(F32)
        total = total + jnp.sum(weight * grad[...], axis=1, keepdims=True)
    sub = iota((8, 128), 0)
    gain = jnp.ones((8, 128), F32)
    for row in range(8):
        gain = jnp.where(sub == row, scalars[row], gain)
    return total / gain.astype(BF).astype(F32)


def unpack_inputs(R):
    lane = iota((8, 128), 1)
    low = lane_low((8, 128))
    misc = jnp.zeros((8, 128), F32)
    for j in range(4):
        R.o_min[:, 384 * j : 384 * j + 384] = R.rfin[j, 0, :, 384:768]
        R.o_min[:, 1536 + 384 * j : 1920 + 384 * j] = R.rfin[j, 0, :, 0:384]
        R.o_q[:, 128 * j : 128 * j + 128] = R.rfin[j, 1, :, 384:512]
        part = R.rfin[j, 1, :, 256:384]
        own = jnp.where(lane < HEADS, part, 0.0)
        misc = misc + (own if j == 0 else roll(own, HEADS * j, 1))
    R.o_misc[...] = misc
    R.o_bc[...] = (R.rfin[0, 1, :, 0:256] + R.rfin[1, 1, :, 0:256]) + (
        R.rfin[2, 1, :, 0:256] + R.rfin[3, 1, :, 0:256]
    )
    kv0 = R.rfin[0, 1, :, 512:640] + R.rfin[1, 1, :, 512:640]
    kv1 = R.rfin[2, 1, :, 512:640] + R.rfin[3, 1, :, 512:640]
    R.o_k[...] = jnp.where(low, kv0, roll(kv1, 64, 1))
    R.o_v[...] = jnp.where(low, roll(kv0, 64, 1), kv1)
    pairs = [(R.w_min, R.o_min), (R.w_bc, R.o_bc), (R.w_step, R.o_misc.at[:, 0:24])]
    pairs += [(R.w_q, R.o_q), (R.w_k, R.o_k), (R.w_v, R.o_v)]
    first = gain_column(pairs, R.gain_in)
    both = jnp.where(iota((8, 128), 1) == 0, first, R.gcol[0])
    turned = jnp.concatenate([both, jnp.zeros((120, 128), F32)], axis=0).T
    R.o_head[3:5, :] = turned[0:2, :]


def in_core_order(L, mine, other):
    first = L.c == 0
    return jnp.where(first, mine, other), jnp.where(first, other, mine)


def own_rows(L, R, exch, kinds, width):
    for sub in range(2):
        for k in range(2):
            both = jnp.concatenate([exch[2 * sub + k, d] for d in range(2)], axis=0).astype(BF)
            for n, kind in enumerate(kinds):
                lo = kind[0] + width * k
                R.win[L.c, sub, L.y, L.x, :, lo : lo + width] = both[:, width * n : width * n + width]


def own_halves(L, R, pack, other, kind):
    for d, part in enumerate(in_core_order(L, pack[L.c], other[...])):
        R.win[L.c, d, L.y, L.x, :, kind[0] : kind[0] + 512] = part.astype(BF)


def to_slab(L, pack, exch):
    moves = [L.copy(pack.at[j, h], exch.at[L.z, L.c], L.device(z=j, c=h)) for j, h in L.slab()]
    exch[L.z, L.c] = pack[L.z, L.c]
    return moves


def come(*moves):
    for one in moves:
        one.wait_recv()


def middle_rows(L, R, h):
    block, rows = mid_rows(L, h)
    total = R.xall[block, rows, :].astype(F32) + R.branch[h, L.z].astype(F32)
    for n in range(3):
        total = total + R.zrecv[h, n].astype(F32)
    R.middle[h] = total
    inv = lax.rsqrt(jnp.mean(total * total, axis=-1, keepdims=True) + EPS)
    R.secall[h, L.z] = (total * inv * R.gain[1:2, :]).astype(BF)


def back_middle(L, R, h):
    block, rows = mid_rows(L, h)
    total = R.gsec[h, L.z].astype(F32)
    for n in range(3):
        total = total + R.zrecv[2 + h, n].astype(F32)
    gmid = norm_back(R.middle[h], R.gain[1:2, :], total)
    gmid = gmid + R.cotall[block, rows, :].astype(F32)
    R.gmid[h] = gmid
    R.gball[h, L.z] = gmid.astype(BF)


def keep(dst, srcs):
    pass


def to_owner(L, R, ref, n):
    return reduce(L, "z", lambda j: ref.at[j], [R.zrecv.at[n, k] for k in range(3)], keep)


def kernel(R):
    L = Links(R.send, R.recv)
    greeted = L.greet()
    R.await_in(*WEIGHTS_IN)
    pack_weights(L, R)
    R.await_in("tok", "cot")
    R.xall[L.z] = R.tok[...]
    R.cotall[L.z] = R.cot[...]
    greeted()

    moves = to_slab(L, R.pack, R.exch)
    xgen = gather_blocks(L, R.xall)
    step(xgen)
    wo = L.copy(R.opack.at[1 - L.c], R.exo, L.sibling)
    R.await_in("seg", "taps", "bias")
    setup(L, R)
    come(*moves)
    own_rows(L, R, R.exch, (LATE, EARLY), GW)
    late = together(*[gather_mixer(L, R, sub, *LATE) for sub in range(2)])
    step(late)
    come(wo)
    own_halves(L, R, R.opack, R.exo, OUT)
    R.await_in("w_fg", "w_fu", "w_fd")
    pack_ffn(L, R)
    fmoves = to_slab(L, R.fpack, R.fexch)
    do = L.copy(R.dpack.at[1 - L.c], R.dexo, L.sibling)
    step(late)
    rest = together(
        *[gather_mixer(L, R, sub, EARLY[0], EARLY[1] + OUT[1]) for sub in range(2)]
    )
    step(rest)
    cgen = gather_blocks(L, R.cotall)
    R.small[...] = jnp.zeros((8, CW), F32)
    R.gk[...] = jnp.zeros((LEN, 128), F32)
    R.gv[...] = jnp.zeros((LEN, 128), F32)
    R.state[0] = jnp.zeros((128, XW), F32)
    step(late)
    step(rest)
    come(do, *fmoves)
    own_rows(L, R, R.fexch, (FIN,), FW)
    own_halves(L, R, R.dpack, R.dexo, FOUT)
    fsent = []
    fgen = together(*[gather_mixer(L, R, sub, *FFN, fsent) for sub in range(2)])
    step(fgen)
    drain(late)
    drain(xgen)
    step(cgen)

    gains(R)
    norm_first(R)
    project_late(R)
    convolve(R)
    steps(R)
    step(rest, fgen)
    recurrence(R, 0, 2)
    drain(rest)
    project_early(R)
    R.await_in("cosr", "sinr", "perm5")
    rotated(R)
    attend(R, 0, 2)
    out_project(R, 0)
    branch = [to_owner(L, R, R.branch.at[h], h) for h in range(2)]
    step(branch[0])
    step(fgen)
    recurrence(R, 2, 4)
    attend(R, 2, 4)
    out_project(R, 1)
    step(branch[1])
    second = [gather_blocks(L, R.secall.at[h]) for h in range(2)]
    for h in range(2):
        drain(branch[h])
        middle_rows(L, R, h)
        step(second[h])
    drain(cgen, fgen)
    gsec = [to_owner(L, R, R.gsec.at[h], 2 + h) for h in range(2)]
    for h in range(2):
        drain(second[h])
        ffn(R, h)
        step(gsec[h])
    gball = [gather_blocks(L, R.gball.at[h]) for h in range(2)]
    drain(gsec[0])
    back_middle(L, R, 0)
    step(gball[0])
    ffn_out(R, L)
    for one in fsent:
        one.wait_send()
    ffn_grads(R)
    wgen = reduce_ffn(L, R)
    step(wgen)
    drain(gsec[1])
    back_middle(L, R, 1)
    step(gball[1])
    step(wgen)
    drain(gball[0])
    back_out(R, 0)
    back_attend(R, 0, 2)
    step(wgen)
    drain(gball[1])
    fout = reduce_blocks(L, R.fout, R.frecv)
    step(fout)
    back_out(R, 1)
    out_grad(R)
    ogen = reduce_outputs(L, R)
    step(ogen)
    back_gate(R)
    back_attend(R, 2, 4)
    back_rotated(R)
    step(ogen, wgen)
    early_grads(R)
    egen = reduce_inputs(L, R, EARLY, GW)
    step(egen)
    back_recurrence(R)
    step(egen, ogen, wgen)
    back_convolve(R)
    late_grads(R)
    lgen = reduce_inputs(L, R, LATE, 0)
    step(lgen)
    mgen = reduce_small(L, R)
    step(mgen)
    hgen = back_first(R, L)
    step(hgen)
    step(lgen, mgen)
    step(hgen)
    step(egen, ogen, wgen)
    step(hgen)
    step(lgen, mgen)
    step(hgen)
    step(egen, ogen, wgen)
    drain(fout)
    R.o_out[...] = R.fout[L.z]
    R.send_out("o_out")
    step(lgen, mgen)
    step(egen, ogen, wgen)
    drain(ogen, egen, wgen)
    step(lgen, mgen)
    drain(mgen)
    drain(hgen)
    R.o_tok[...] = R.gfirst[L.z]
    R.send_out("o_tok")
    drain(lgen)
    unpack_inputs(R)
    R.send_out("o_min", "o_bc", "o_misc", "o_q", "o_k", "o_v", "o_conv", "o_head")
    L.finish()
    R.finish_out()


INS = dict(
    w_min=((8, 3072), F32),
    w_bc=((8, 256), F32),
    w_step=((8, 24), F32),
    w_q=((8, 512), F32),
    w_k=((8, 128), F32),
    w_v=((8, 128), F32),
    w_mo=((12, D), F32),
    w_ao=((4, D), F32),
    tok=((ROWS, D), BF),
    cot=((ROWS, D), BF),
    w_fg=((8, 2048), F32),
    w_fu=((8, 2048), F32),
    w_fd=((16, D), F32),
    seg=((1, LEN), jnp.int32),
    taps=((4, 1792), F32),
    bias=((1, 1792), F32),
    cosr=((LEN, 128), F32),
    sinr=((LEN, 128), F32),
    perm5=((512, 512), BF),
)
WEIGHTS_IN = list(INS)[:8]
SCALARS = ("gain_in", "gain_mid", "step_bias", "decay_log", "skip_gain")
OUTS = dict(
    o_out=((ROWS, D), BF),
    o_tok=((ROWS, D), BF),
    o_min=((8, 3072), F32),
    o_bc=((8, 256), F32),
    o_misc=((8, 128), F32),
    o_q=((8, 512), F32),
    o_k=((8, 128), F32),
    o_v=((8, 128), F32),
    o_mo=((12, D), F32),
    o_ao=((4, D), F32),
    o_fg=((8, 2048), F32),
    o_fu=((8, 2048), F32),
    o_fd=((16, D), F32),
    o_conv=((8, 1792), F32),
    o_head=((8, 128), F32),
)
SCRATCH = dict(
    xall=((4, ROWS, D), BF),
    segc=((LEN, 128), F32),
    segr=((8, LEN), F32),
    cpar=((8, CW), F32),
    hpar=((8, 128), F32),
    misc=((8, 128), F32),
    pack=((4, 2, 8, 768), F32),
    exch=((4, 2, 8, 768), F32),
    opack=((2, 16, 512), F32),
    exo=((16, 512), F32),
    fpack=((4, 2, 8, FW), F32),
    fexch=((4, 2, 8, FW), F32),
    dpack=((2, 16, 512), F32),
    dexo=((16, 512), F32),
    win=((2, 2, 4, 4, 16, PK), BF),
    dwin=((2, 2, 4, 4, 16, FIN[0]), BF),
    cotall=((4, ROWS, D), BF),
    secall=((2, 4, 64, D), BF),
    hid=((LEN, FW), BF),
    gab=((LEN, 2 * FW), BF),
    gsec=((2, 4, 64, D), BF),
    fout=((4, ROWS, D), BF),
    gain=((8, D), F32),
    gcol=((1, 8, 128), F32),
    first=((LEN, D), BF),
    gate=((LEN, XW), F32),
    raw=((LEN, CW), BF),
    pq=((LEN, 128), F32),
    pkv=((LEN, 128), F32),
    pm=((LEN, 128), F32),
    pre=((LEN, CW), F32),
    mixed=((LEN, CW), F32),
    step=((LEN, 128), F32),
    run=((LEN, 128), F32),
    state=((5, 128, XW), F32),
    ssm=((LEN, XW), F32),
    q=((LEN, 128), BF),
    kk=((LEN, 128), BF),
    vv=((LEN, 128), BF),
    probs=((2, LEN, LEN), BF),
    left=((LEN, 512), BF),
    left_p=((LEN, 512), BF),
    branch=((2, 4, 64, D), BF),
    zrecv=((4, 3, 64, D), BF),
    frecv=((3, ROWS, D), BF),
    hrecv=((3, ROWS, D), BF),
    middle=((2, 64, D), F32),
    gmid=((2, 64, D), F32),
    gsum=((ROWS, D), F32),
    gball=((2, 4, 64, D), BF),
    gleft=((LEN, 512), F32),
    gq=((LEN, 128), F32),
    gk=((LEN, 128), F32),
    gv=((LEN, 128), F32),
    gstate=((128, XW), F32),
    hsum=((8, 128), F32),
    gmix=((LEN, CW), F32),
    gproj=((LEN, 4 * GW), BF),
    small=((8, CW), F32),
    factor=((4, 8, 128), F32),
    inlet_x=((LEN, XW), F32),
    tail_x=((LEN, XW), F32),
    factor_x=((4, 8, XW), F32),
    step_x=((LEN, XW), F32),
    mix=((4, HEADS, ROWS, ROWS), BF),
    weights=((4, HEADS, ROWS, ROWS), BF),
    gfirst=((4, ROWS, D), BF),
    wsib=((2, 4, 4, 16, PK), BF),
    smc=((2, 8, CW), F32),
    smx=((4, 8, CW), F32),
    smy=((4, 8, CW), F32),
    smz=((4, 8, CW), F32),
    fin=((4, 2, 8, 768), F32),
    rfin=((4, 2, 8, 768), F32),
    ofin=((2, 16, 512), F32),
    orfin=((16, 512), F32),
    ffin=((4, 2, 8, FW), F32),
    frfin=((4, 2, 8, FW), F32),
    dfin=((2, 16, 512), F32),
    drfin=((16, 512), F32),
)
COPIES = 250


def ring_buffers(parts, width, stages):
    shapes = {}
    for stage in range(stages):
        for n in range(3):
            shapes[(stage, n)] = ((parts,) + (4,) * stage + (16, width), BF)
    return shapes


MBUFS = ring_buffers(2, PK, 2)


def entry(*refs):
    refs = list(refs)
    take = lambda names: [(name, refs.pop(0)) for name in names]
    given, scalars, results = dict(take(INS)), take(SCALARS), dict(take(OUTS))
    inside = take(INS)
    R = types.SimpleNamespace(**dict(scalars + inside + take(OUTS) + take(SCRATCH)))
    bufs = dict(take(MBUFS))
    R.mbufs = [[bufs[key] for key in MBUFS if key[0] == stage] for stage in range(2)]
    R.send, R.recv, came, left = refs
    loads = {}
    for n, name in enumerate(INS):
        loads[name] = pltpu.make_async_copy(given[name], getattr(R, name), came.at[n])
        loads[name].start()
    stores = []

    def await_in(*names):
        for name in names:
            loads[name].wait()

    def send_out(*names):
        for name in names:
            n = len(stores)
            stores.append(pltpu.make_async_copy(getattr(R, name), results[name], left.at[n]))
            stores[-1].start()

    def finish_out():
        for one in stores:
            one.wait()

    R.await_in, R.send_out, R.finish_out = await_in, send_out, finish_out
    kernel(R)


def layer(*args):
    anywhere = pl.BlockSpec(memory_space=pl.ANY)
    smem = pl.BlockSpec(memory_space=pltpu.SMEM)
    shapes = [*INS.values(), *OUTS.values(), *SCRATCH.values(), *MBUFS.values()]
    scratch = [pltpu.VMEM(shape, kind) for shape, kind in shapes]
    scratch += [pltpu.SemaphoreType.DMA((n,)) for n in (COPIES, COPIES, len(INS), len(OUTS))]
    return pl.pallas_call(
        entry,
        out_shape=[jax.ShapeDtypeStruct(shape, kind) for shape, kind in OUTS.values()],
        in_specs=[anywhere] * len(INS) + [smem] * len(SCALARS),
        out_specs=[anywhere] * len(OUTS),
        scratch_shapes=scratch,
        compiler_params=pltpu.CompilerParams(
            collective_id=0, has_side_effects=True, vmem_limit_bytes=63 * 2**20
        ),
    )(*args)


SAME = [name for name in OUTS if name not in ("o_misc", "o_conv", "o_head")]
RESULTS = {name: OUTS[name] for name in SAME}
RESULTS.update(
    step=((8, 24), F32),
    taps=((4, 1792), F32),
    bias=((1, 1792), F32),
    gain_in=((1, 8), F32),
    gain_mid=((1, 8), F32),
    step_bias=((1, 24), F32),
    decay_log=((1, 24), F32),
    skip_gain=((1, 24), F32),
)


def deliver_kernel(*refs):
    given = dict(zip(OUTS, refs))
    result = dict(zip(RESULTS, refs[len(OUTS) :]))
    for name in SAME:
        result[name][...] = given[name][...]
    result["step"][...] = given["o_misc"][:, 0:24]
    result["taps"][...] = given["o_conv"][0:4, :]
    result["bias"][...] = given["o_conv"][4:5, :]
    head = given["o_head"]
    for row, name in enumerate(("step_bias", "decay_log", "skip_gain")):
        result[name][...] = head[row : row + 1, 0:24]
    result["gain_in"][...] = head[3:4, 0:8]
    result["gain_mid"][...] = head[4:5, 0:8]


def deliver(outs):
    vmem = pl.BlockSpec(memory_space=pltpu.VMEM)
    results = pl.pallas_call(
        deliver_kernel,
        out_shape=[jax.ShapeDtypeStruct(shape, kind) for shape, kind in RESULTS.values()],
        in_specs=[vmem] * len(OUTS),
        out_specs=[vmem] * len(RESULTS),
    )(*outs)
    return dict(zip(RESULTS, results))


def rotary_tables():
    lane = np.arange(128)
    power = (-2.0 * (lane % 32).astype(np.float32) / np.float32(64)).astype(np.float32)
    frequency = np.power(np.float32(ROPE), power).astype(np.float32)
    angles = np.arange(LEN, dtype=np.float32)[:, None] * frequency[None, :]
    sign = np.where(lane % 64 < 32, -1.0, 1.0)
    cosine = np.cos(angles.astype(np.float64)).astype(np.float32)
    sine = (np.sin(angles.astype(np.float64)) * sign).astype(np.float32)
    return cosine, sine


def out_order():
    n = np.arange(512)
    device = np.where(n < 384, n // 12, (n - 384) // 4)
    row = np.where(n < 384, n % 12, 12 + (n - 384) % 4)
    to = (device % 2) * 256 + (device // 2) * 16 + row
    table = np.zeros((512, 512), np.float32)
    table[n, to] = 1.0
    return table


def shards(
    tokens,
    segments,
    cotangent,
    gain_in,
    mamba_in,
    mamba_bc,
    mamba_step,
    in_query,
    in_key,
    in_value,
    mamba_out,
    attn_out,
    gain_mid,
    ffn_gate,
    ffn_up,
    ffn_down,
    conv_taps,
    conv_bias,
    step_bias,
    decay_log,
    skip_gain,
):
    cosine, sine = rotary_tables()
    outs = layer(
        mamba_in,
        mamba_bc,
        mamba_step,
        in_query,
        in_key,
        in_value,
        mamba_out,
        attn_out,
        tokens[0],
        cotangent[0],
        ffn_gate,
        ffn_up,
        ffn_down,
        segments,
        conv_taps,
        conv_bias[None],
        jnp.asarray(cosine),
        jnp.asarray(sine),
        jnp.asarray(out_order(), BF),
        gain_in,
        gain_mid,
        step_bias,
        decay_log,
        skip_gain,
    )
    r = deliver(outs)
    return (
        r["o_out"][None],
        r["o_tok"][None],
        r["gain_in"][0],
        r["o_min"],
        r["o_bc"],
        r["step"],
        r["o_q"],
        r["o_k"],
        r["o_v"],
        r["o_mo"],
        r["o_ao"],
        r["gain_mid"][0],
        r["o_fg"],
        r["o_fu"],
        r["o_fd"],
        r["taps"],
        r["bias"][0],
        r["step_bias"][0],
        r["decay_log"][0],
        r["skip_gain"][0],
    )


def solution(mesh):
    one = P(("ctx", "fsdp"))
    rows = P(("ctx", "fsdp"), None)
    block = P("fsdp", "ctx", None)
    return jax.shard_map(
        shards,
        mesh=mesh,
        in_specs=(block, P("fsdp", None), block, one)
        + (rows,) * 8
        + (one,)
        + (rows,) * 3
        + (P(),) * 5,
        out_specs=(block, block, one) + (rows,) * 8 + (one,) + (rows,) * 3 + (P(),) * 5,
        check_vma=False,
    )
```

```python
import types

import jax
import jax.numpy as jnp
import numpy as np
from jax import lax
from jax.experimental import pallas as pl
from jax.experimental.pallas import tpu as pltpu
from jax.sharding import PartitionSpec as P

BF = jnp.bfloat16
F32 = jnp.float32
MESH = pl.DeviceIdType.MESH
HI = lax.Precision.HIGHEST
EPS = 1e-06
ROPE = 100000000000.0

D = 1024
LEN = 512
ROWS = 128
HEADS = 6
XW = 384
CW = 640
GW = 384
PK = 3584
FW = 512


def mm(a, b):
    return lax.dot_general(a, b, (((1,), (0,)), ((), ())), preferred_element_type=F32)


def mm_nt(a, b):
    return lax.dot_general(a, b, (((1,), (1,)), ((), ())), preferred_element_type=F32)


def mm_tn(a, b):
    return lax.dot_general(a, b, (((0,), (0,)), ((), ())), preferred_element_type=F32)


def mm_exact(a, b):
    return lax.dot_general(
        a, b, (((1,), (0,)), ((), ())), precision=HI, preferred_element_type=F32
    )


def iota(shape, dim):
    return lax.broadcasted_iota(jnp.int32, shape, dim)


def lane_low(shape):
    return iota(shape, 1) % 128 < 64


def roll(v, shift, axis):
    size = v.shape[axis]
    return pltpu.roll(v, shift % size, axis)


def swap_halves(v):
    lanes = v.shape[1]
    first = iota(v.shape, 1) % 64 < 32
    return jnp.where(first, roll(v, lanes - 32, 1), roll(v, 32, 1))


def sigmoid(v):
    return 1.0 / (1.0 + jnp.exp(-v))


def softplus(v):
    return jnp.maximum(v, 0.0) + jnp.log1p(jnp.exp(-jnp.abs(v)))


def spread_heads(v):
    rows = v.shape[0]
    low = lane_low((rows, 128))
    tiles = []
    for pair in range(HEADS // 2):
        a = jnp.broadcast_to(v[:, 2 * pair : 2 * pair + 1], (rows, 128))
        b = jnp.broadcast_to(v[:, 2 * pair + 1 : 2 * pair + 2], (rows, 128))
        tiles.append(jnp.where(low, a, b))
    return jnp.concatenate(tiles, axis=1)


def mm_terms(a, b, count):
    side = 0 if a.dtype == F32 else 1
    rest, total = (a, b)[side], None
    for _ in range(count):
        term = rest.astype(BF)
        rest = rest - term.astype(F32)
        one = mm(term, b) if side == 0 else mm(a, term)
        total = one if total is None else total + one
    return total


def sum_heads(v):
    pick = (iota((XW, 128), 0) // 64 == iota((XW, 128), 1)).astype(BF)
    return mm_terms(v, pick, 2)


def lower_ones():
    return (iota((ROWS, ROWS), 1) <= iota((ROWS, ROWS), 0)).astype(BF)


LATE, EARLY, OUT = (0, 2 * GW), (2 * GW, 2 * GW), (4 * GW, 512)
FIN, FOUT = (2048, 2 * FW), (2048 + 2 * FW, 512)
FFN = (FIN[0], FIN[1] + FOUT[1])


def chunk(R, core, kind, k, lo=0, width=GW):
    v = R.win[core, k // 2, :, :, :, pl.ds(kind[0] + GW * (k % 2) + lo, width)]
    return v.reshape(256, width)


def group_weight(R, core, kind):
    return jnp.concatenate([chunk(R, core, kind, k) for k in range(4)], axis=0)


def out_weight(R, kind=OUT):
    parts = []
    for core in range(2):
        rows = [R.win[core, d, :, :, :, pl.ds(kind[0], 512)].reshape(256, 512) for d in range(2)]
        parts.append(jnp.concatenate(rows, axis=0))
    return jnp.concatenate(parts, axis=1)


def seg_mask(R, k):
    seg = R.segc[...]
    return jnp.where(
        (seg == roll(seg, k, 0)) & (iota((LEN, 128), 0) >= k), 1.0, 0.0
    ).astype(F32)


def gains(R):
    pick = (iota((8, 128), 1) == iota((8, 128), 0) + 24).astype(BF)
    for k in range(4):
        R.gain[:, pl.ds(256 * k, 256)] = mm_nt(pick, chunk(R, 1, LATE, k, 256, 128))


def norm_first(R):
    gain = R.gain[0:1, :]

    def block(b, carry):
        x = R.xall[b].astype(F32)
        inv = lax.rsqrt(jnp.mean(x * x, axis=-1, keepdims=True) + EPS)
        R.first[pl.ds(pl.multiple_of(b * ROWS, ROWS), ROWS), :] = (x * inv * gain).astype(BF)
        return carry

    lax.fori_loop(0, 4, block, 0)


def project_late(R):
    first = R.first[...]
    out = mm(first, group_weight(R, 0, LATE))
    R.raw[:, 0:384] = out.astype(BF)
    out = mm(first, group_weight(R, 1, LATE))
    R.raw[:, 384:640] = out[:, 0:256].astype(BF)
    R.pm[...] = out[:, 256:384]


def project_early(R):
    first = R.first[...]
    out = mm(first, group_weight(R, 1, EARLY))
    R.pq[...] = out[:, 0:128]
    R.pkv[...] = out[:, 128:256]
    R.gate[...] = mm(first, group_weight(R, 0, EARLY))


def convolve(R):
    masks = [seg_mask(R, k) for k in range(1, 4)]
    for t in range(CW // 128):
        cols = slice(128 * t, 128 * t + 128)
        raw = R.raw[:, cols].astype(F32)
        total = R.cpar[4:5, cols] + R.cpar[0:1, cols] * raw
        for k in range(1, 4):
            total = total + R.cpar[k : k + 1, cols] * (roll(raw, k, 0) * masks[k - 1])
        R.pre[:, cols] = total
        R.mixed[:, cols] = total * sigmoid(total)


def steps(R):
    step = softplus(R.pm[...] + R.hpar[0:1, :])
    R.step[...] = step
    decay = -jnp.exp(R.hpar[1:2, :])
    ones = lower_ones()
    for b in range(4):
        rows = slice(b * ROWS, b * ROWS + ROWS)
        R.run[rows, :] = mm_terms(ones, decay * step[rows, :], 3)


def span(R, b):
    s = types.SimpleNamespace()
    s.at = pl.multiple_of(b * ROWS, ROWS)
    s.rows = pl.ds(s.at, ROWS)
    s.xs = R.mixed[s.rows, 0:384]
    s.xs_low = s.xs.astype(BF)
    s.wr_low = R.mixed[s.rows, 384:512].astype(BF)
    s.rd_low = R.mixed[s.rows, 512:640].astype(BF)
    s.step = R.step[s.rows, :]
    return s


def recurrence(R, begin, end):
    low = lane_low((ROWS, 128))

    def block(b, carry):
        s = span(R, b)
        run = R.run[s.rows, :]
        run_t = run.T
        seg = R.segc[s.rows, :]
        last = jnp.broadcast_to(seg[ROWS - 1 : ROWS, :], (ROWS, ROWS))
        earlier = R.segc[pl.ds(pl.multiple_of(jnp.maximum(s.at - 8, 0), 8), 8), :][7:8, :]
        earlier = jnp.where(jnp.broadcast_to(b, (1, 128)) == 0, -1.0, earlier)
        causal = (iota((ROWS, ROWS), 1) <= iota((ROWS, ROWS), 0)) & (
            seg == R.segr[0:1, s.rows]
        )
        inlet = jnp.where(seg == earlier, jnp.exp(run), 0.0)
        stop = run[ROWS - 1 : ROWS, :]
        tail0 = jnp.where(seg == last, jnp.exp(stop - run), 0.0)
        factor = jnp.where(last[0:1, :] == earlier, jnp.exp(stop), 0.0)
        inlet_x = spread_heads(inlet)
        step_x = spread_heads(s.step)
        tail_x = spread_heads(tail0)
        xstep = step_x * s.xs
        xstep_low = xstep.astype(BF)
        factor_x = spread_heads(jnp.broadcast_to(factor, (8, 128)))
        R.step_x[s.rows, :] = step_x
        R.factor[b] = jnp.broadcast_to(factor, (8, 128))
        R.inlet_x[s.rows, :] = inlet_x
        R.tail_x[s.rows, :] = tail_x
        R.factor_x[b] = factor_x
        cross = mm_nt(s.rd_low, s.wr_low)
        state = R.state[b]
        inflow = mm(s.rd_low, state.astype(BF))
        tiles = []
        for pair in range(HEADS // 2):
            xp = xstep_low[:, 128 * pair : 128 * pair + 128]
            both = []
            for h in (2 * pair, 2 * pair + 1):
                spread = run[:, h : h + 1] - run_t[h : h + 1, :]
                mix = jnp.exp(jnp.where(causal, spread, -10000.0))
                weights = (mix * cross).astype(BF)
                R.mix[b, h] = mix.astype(BF)
                R.weights[b, h] = weights
                both.append(mm(weights, xp))
            tiles.append(jnp.where(low, both[0], both[1]))
        R.ssm[s.rows, :] = (
            jnp.concatenate(tiles, axis=1) + inlet_x * inflow + R.cpar[5:6, 0:384] * s.xs
        )
        R.state[b + 1] = factor_x[0:1, :] * state + mm_tn(
            s.wr_low, (tail_x * xstep).astype(BF)
        )
        return carry

    lax.fori_loop(begin, end, block, 0)


def rotate(v, cosr, sinr):
    return v * cosr + swap_halves(v) * sinr


def rotated(R):
    low = lane_low((LEN, 128))
    R.q[...] = rotate(R.pq[...], R.cosr[...], R.sinr[...]).astype(BF)
    pkv = R.pkv[...]
    k = rotate(pkv, R.cosr[...], R.sinr[...])
    R.kk[...] = jnp.where(low, k, roll(k, 64, 1)).astype(BF)
    R.vv[...] = jnp.where(low, roll(pkv, 64, 1), pkv).astype(BF)


def half_only(v, e):
    low = lane_low(v.shape)
    return jnp.where(low if e == 0 else ~low, v, jnp.zeros_like(v))


def attend(R, begin, end):
    low = lane_low((ROWS, 128))
    for i in range(begin, end):
        rows = slice(i * ROWS, i * ROWS + ROWS)
        n = (i + 1) * ROWS
        seg_row = R.segr[0:1, 0:n]
        seg_col = jnp.broadcast_to(R.segc[rows, 0:1], (ROWS, n))
        allowed = (iota((ROWS, n), 1) <= iota((ROWS, n), 0) + i * ROWS) & (seg_col == seg_row)
        outs = []
        for e in range(2):
            scores = mm_nt(half_only(R.q[rows, :], e), R.kk[0:n, :]) * 0.125
            scores = jnp.where(allowed, scores, -1e30)
            shifted = jnp.exp(scores - jnp.max(scores, axis=-1, keepdims=True))
            probs = (shifted / jnp.sum(shifted, axis=-1, keepdims=True)).astype(BF)
            R.probs[e, rows, 0:n] = probs
            outs.append(mm(probs, R.vv[0:n, :]))
        R.left[rows, 384:512] = jnp.where(low, outs[0], outs[1]).astype(BF)


def out_project(R, h):
    rows = slice(256 * h, 256 * h + 256)
    gate = R.gate[rows, :]
    R.left[rows, 0:384] = (R.ssm[rows, :] * (gate * sigmoid(gate))).astype(BF)
    left = mm(R.left[rows, :], R.perm5[...]).astype(BF)
    R.left_p[rows, :] = left
    out = mm(left, out_weight(R))
    for j in range(4):
        R.branch[h, j] = out[64 * j : 64 * j + 64, :].astype(BF)


def unit_chunk(R, core, k):
    lo = FIN[0] + FW * (k % 2)
    return R.win[core, k // 2, :, :, :, lo : lo + FW].reshape(256, FW)


def ffn(R, h):
    second = R.secall[h].reshape(256, D)
    cot = R.cotall[2 * h : 2 * h + 2].reshape(256, D)
    rows = slice(256 * h, 256 * h + 256)
    for d in range(2):
        cols = slice(256 * d, 256 * d + 256)
        weights = []
        for core in range(2):
            parts = [unit_chunk(R, core, k)[:, cols] for k in range(4)]
            weights.append(jnp.concatenate(parts, axis=0))
        a = mm(second, weights[0])
        b = mm(second, weights[1])
        down = jnp.concatenate(
            [R.win[core, d, :, :, :, FOUT[0] : PK].reshape(256, 512) for core in range(2)], axis=1
        )
        ghid = mm_nt(cot, down)
        sig = sigmoid(a)
        act = a * sig
        R.hid[rows, cols] = (act * b).astype(BF)
        R.gab[rows, cols] = (ghid * b * (sig + act * (1.0 - sig))).astype(BF)
        R.gab[rows, FW + 256 * d : FW + 256 * d + 256] = (ghid * act).astype(BF)
    for k in range(4):
        weights = jnp.concatenate([unit_chunk(R, core, k) for core in range(2)], axis=1)
        out = mm_nt(R.gab[rows, :], weights)
        for j in range(4):
            R.gsec[h, j, :, 256 * k : 256 * k + 256] = out[64 * j : 64 * j + 64, :].astype(BF)


def ffn_out(R, L):
    out = mm(R.hid[...], out_weight(R, FOUT))
    for b in range(4):
        R.fout[b] = out[b * ROWS : b * ROWS + ROWS, :].astype(BF)
    for h in range(2):
        block, rows = mid_rows(L, h)
        R.fout[block, rows, :] = (
            R.fout[block, rows, :].astype(F32) + R.middle[h]
        ).astype(BF)


def ffn_grads(R):
    second = R.secall[...].reshape(LEN, D)
    for k in range(4):
        out = mm_tn(second[:, 256 * k : 256 * k + 256], R.gab[...]).astype(BF)
        lo = FIN[0] + FW * (k % 2)
        for core in range(2):
            part = out[:, FW * core : FW * core + FW]
            R.win[core, k // 2, :, :, :, lo : lo + FW] = part.reshape(4, 4, 16, FW)
    put_out_grad(R.win, FOUT, mm_tn(R.hid[...], R.cotall[...].reshape(LEN, D)))


def norm_back(x, gain, grad):
    inv = lax.rsqrt(jnp.mean(x * x, axis=-1, keepdims=True) + EPS)
    unit = x * inv
    scaled = grad * gain
    return inv * (scaled - unit * jnp.mean(scaled * unit, axis=-1, keepdims=True))


def mid_rows(L, h):
    return 2 * h + lax.div(L.z, 2), pl.ds(pl.multiple_of(64 * lax.rem(L.z, 2), 64), 64)


def back_out(R, h):
    rows = slice(256 * h, 256 * h + 256)
    raw = mm_nt(R.gball[h].reshape(256, D), out_weight(R))
    perm = R.perm5[...]
    hi = raw.astype(BF)
    rest = raw - hi.astype(F32)
    R.gleft[rows, :] = mm_nt(hi, perm) + mm_nt(rest.astype(BF), perm)


def back_gate(R):
    def block(b, carry):
        rows = pl.ds(pl.multiple_of(b * ROWS, ROWS), ROWS)
        gate = R.gate[rows, :]
        sig = sigmoid(gate)
        grad = R.gleft[rows, 0:384] * R.ssm[rows, :]
        R.gproj[rows, 768:1152] = (grad * (sig + gate * sig * (1.0 - sig))).astype(BF)
        return carry

    lax.fori_loop(0, 4, block, 0)


def back_attend(R, begin, end):
    low = lane_low((ROWS, 128))
    for i in range(begin, end):
        rows = slice(i * ROWS, i * ROWS + ROWS)
        n = (i + 1) * ROWS
        go = R.gleft[rows, 384:512].astype(BF)
        outs = []
        for e in range(2):
            probs = R.probs[e, rows, 0:n]
            pf = probs.astype(F32)
            go_e = half_only(go, e)
            dp = mm_nt(go_e, R.vv[0:n, :])
            ds = (pf * (dp - jnp.sum(pf * dp, axis=-1, keepdims=True))).astype(BF)
            outs.append(mm(ds, R.kk[0:n, :]))
            R.gk[0:n, :] += mm_tn(ds, half_only(R.q[rows, :], e))
            R.gv[0:n, :] += mm_tn(probs, go_e)
        R.gq[rows, :] = jnp.where(low, outs[0], outs[1]) * 0.125


def back_rotated(R):
    cosr, sinr = R.cosr[...], R.sinr[...]
    gq = rotate(R.gq[...], cosr, -sinr)
    R.gproj[:, 1152:1280] = gq.astype(BF)
    gk = R.gk[...] * 0.125
    gk = rotate(gk + roll(gk, 64, 1), cosr, -sinr)
    gv = R.gv[...]
    gv = gv + roll(gv, 64, 1)
    R.gproj[:, 1280:1408] = jnp.where(lane_low((LEN, 128)), gk, gv).astype(BF)
    R.gproj[:, 1408:1536] = jnp.zeros((LEN, 128), BF)


def back_recurrence(R, begin, end):
    low = lane_low((ROWS, 128))
    lane = iota((ROWS, 128), 1)
    sub = iota((ROWS, 128), 0)
    upper = (iota((ROWS, ROWS), 1) >= iota((ROWS, ROWS), 0)).astype(BF)

    def block(i, carry):
        b = 3 - i
        s = span(R, b)
        state = R.state[b]
        state_low = state.astype(BF)
        gstate = R.gstate[...]
        gstate_low = gstate.astype(BF)
        gate = R.gate[s.rows, :]
        gy = R.gleft[s.rows, 0:384] * (gate * sigmoid(gate))
        gy_low = gy.astype(BF)
        step_x = R.step_x[s.rows, :]
        tail_x = R.tail_x[s.rows, :]
        xstep = step_x * s.xs
        xstep_low = xstep.astype(BF)
        skip = R.cpar[5:6, 0:384]
        gcross = jnp.zeros((ROWS, ROWS), F32)
        tiles = []
        for pair in range(HEADS // 2):
            cols = slice(128 * pair, 128 * pair + 128)
            gp = gy_low[:, cols]
            both = []
            for e in range(2):
                h = 2 * pair + e
                both.append(mm_tn(R.weights[b, h], gp))
                gm = mm_nt(half_only(gp, e), xstep_low[:, cols])
                gcross = gcross + gm * R.mix[b, h].astype(F32)
            tiles.append(jnp.where(low, both[0], both[1]))
        inside = jnp.concatenate(tiles, axis=1)
        outflow = tail_x * mm(s.wr_low, gstate_low)
        flow_low = (R.inlet_x[s.rows, :] * gy).astype(BF)
        gcross_low = gcross.astype(BF)
        R.gmix[s.rows, 0:384] = (inside + outflow) * step_x + skip * gy
        R.gmix[s.rows, 384:512] = mm_tn(gcross_low, s.rd_low) + mm_nt(
            (tail_x * xstep).astype(BF), gstate_low
        )
        R.gmix[s.rows, 512:640] = mm(gcross_low, s.wr_low) + mm_nt(flow_low, state_low)
        ends = jnp.concatenate(
            [
                jnp.sum(gstate * state, axis=0, keepdims=True),
                jnp.sum(gy * s.xs, axis=0, keepdims=True),
                jnp.zeros((6, XW), F32),
            ],
            axis=0,
        )
        sums = sum_heads(
            jnp.concatenate(
                [
                    gy * (R.ssm[s.rows, :] - skip * s.xs),
                    inside * s.xs,
                    outflow * s.xs,
                    ends,
                ],
                axis=0,
            )
        )
        row_part = sums[0:ROWS, :]
        col_part = sums[ROWS : 2 * ROWS, :]
        through = sums[2 * ROWS : 3 * ROWS, :]
        gfactor = sums[3 * ROWS : 3 * ROWS + 1, :]
        grun = row_part - (col_part + through) * s.step
        at_end = (
            jnp.sum(through * s.step, axis=0, keepdims=True) + gfactor * R.factor[b, 0:1, :]
        )
        grun = grun + jnp.where(sub == ROWS - 1, at_end, 0.0)
        glog = mm_terms(upper, grun, 3)
        decay = -jnp.exp(R.hpar[1:2, :])
        gstep = col_part + through + glog * decay
        drive = R.pm[s.rows, :] + R.hpar[0:1, :]
        gdrive = jnp.where(lane < HEADS, gstep * sigmoid(drive), 0.0)
        R.gproj[s.rows, 640:768] = gdrive.astype(BF)
        R.hsum[0:1, :] += jnp.sum(gdrive, axis=0, keepdims=True)
        R.hsum[1:2, :] += jnp.sum(glog * decay * s.step, axis=0, keepdims=True)
        R.hsum[2:3, :] += sums[3 * ROWS + 1 : 3 * ROWS + 2, :]
        R.gstate[...] = R.factor_x[b, 0:1, :] * gstate + mm_tn(s.rd_low, flow_low)
        return carry

    lax.fori_loop(begin, end, block, 0)


def back_convolve(R):
    masks = [seg_mask(R, k) for k in range(1, 4)]
    for t in range(CW // 128):
        cols = slice(128 * t, 128 * t + 128)
        pre = R.pre[:, cols]
        raw = R.raw[:, cols].astype(F32)
        sig = sigmoid(pre)
        gpre = R.gmix[:, cols] * (sig + pre * sig * (1.0 - sig))
        graw = R.cpar[0:1, cols] * gpre
        R.small[0:1, cols] = jnp.sum(gpre * raw, axis=0, keepdims=True)
        for k in range(1, 4):
            masked = gpre * masks[k - 1]
            graw = graw + R.cpar[k : k + 1, cols] * roll(masked, LEN - k, 0)
            R.small[k : k + 1, cols] = jnp.sum(masked * roll(raw, k, 0), axis=0, keepdims=True)
        R.small[4:5, cols] = jnp.sum(gpre, axis=0, keepdims=True)
        R.gproj[:, cols] = graw.astype(BF)


def back_first(R, L):
    places = ((0, LATE), (1, LATE), (0, EARLY), (1, EARLY))
    gain = R.gain[0:1, :]
    moves = []
    for n, k in enumerate((2, 1, 3, 0)):
        b = L.around("z", k)
        rows = pl.ds(pl.multiple_of(b * ROWS, ROWS), ROWS)
        grads = R.gproj[rows, :]
        for q in range(4):
            weights = jnp.concatenate([chunk(R, core, kind, q) for core, kind in places], axis=1)
            R.gsum[:, 256 * q : 256 * q + 256] = mm_nt(grads, weights)
        R.gfirst[b] = norm_back(R.xall[b].astype(F32), gain, R.gsum[...]).astype(BF)
        for h in range(2):
            block, rows = mid_rows(L, h)

            @pl.when(block == b)
            def _():
                mine = R.gfirst[b, rows, :].astype(F32) + R.gmid[h]
                R.gfirst[b, rows, :] = mine.astype(BF)

        if k:
            moves.append(L.copy(R.gfirst.at[b], R.hrecv.at[n], L.device(z=b)))
        yield
    for one in moves:
        one.wait_recv()
    add_blocks(())(R.gfirst.at[L.z], [R.hrecv.at[n] for n in range(3)])


def put_out_grad(buf, kind, out):
    out = out.astype(BF)
    for core in range(2):
        for d in range(2):
            part = out[256 * d : 256 * d + 256, 512 * core : 512 * core + 512]
            buf[core, d, :, :, :, kind[0] : kind[0] + 512] = part.reshape(4, 4, 16, 512)


def out_grad(R):
    put_out_grad(R.dwin, OUT, mm_tn(R.left_p[...], R.gball[...].reshape(LEN, D)))


def put_grad(R, core, kind, k, value):
    lo = kind[0] + GW * (k % 2)
    R.dwin[core, k // 2, :, :, :, lo : lo + GW] = value.astype(BF).reshape(4, 4, 16, GW)


def early_grads(R):
    for k in range(4):
        out = mm_tn(R.first[:, 256 * k : 256 * k + 256], R.gproj[:, 768:1536])
        for core in range(2):
            put_grad(R, core, EARLY, k, out[:, GW * core : GW * core + GW])


def late_grads(R):
    for k in range(4):
        out = mm_tn(R.first[:, 256 * k : 256 * k + 256], R.gproj[:, 0:768])
        for core in range(2):
            put_grad(R, core, LATE, k, out[:, GW * core : GW * core + GW])


class Move:
    def __init__(self, one):
        self.one, self.came, self.went = one, False, False

    def wait_recv(self):
        if not self.came:
            self.one.wait_recv()
            self.came = True

    def wait_send(self):
        if not self.went:
            self.one.wait_send()
            self.went = True


class Links:
    def __init__(self, send, recv):
        self.send, self.recv, self.moves = send, recv, []
        self.z = lax.axis_index("ctx")
        place = lax.axis_index("fsdp")
        self.c = lax.rem(place, 2)
        self.x = lax.rem(lax.div(place, 2), 4)
        self.y = lax.div(place, 8)
        self.at = {"z": self.z, "y": self.y, "x": self.x}
        self.sibling = self.device(c=1 - self.c)

    def device(self, **moved):
        p = dict(z=self.z, y=self.y, x=self.x, c=self.c)
        p.update(moved)
        return (p["z"], (p["y"] * 4 + p["x"]) * 2 + p["c"])

    def copy(self, src, dst, device):
        k = len(self.moves)
        one = pltpu.make_async_remote_copy(
            src_ref=src,
            dst_ref=dst,
            send_sem=self.send.at[k],
            recv_sem=self.recv.at[k],
            device_id=device,
            device_id_type=MESH,
        )
        one.start()
        self.moves.append(Move(one))
        return self.moves[-1]

    def around(self, axis, k):
        return lax.rem(self.at[axis] + k, 4)

    def slab(self):
        for dz in range(4):
            for flip in range(2):
                if dz or flip:
                    yield self.around("z", dz), self.c if flip == 0 else 1 - self.c

    def greet(self):
        barrier = pltpu.get_barrier_semaphore()
        to = [self.device(z=j, c=h) for j, h in self.slab()]
        for axis in ("x", "y"):
            to += [self.device(**{axis: self.around(axis, k)}) for k in range(1, 4)]
        for one in to:
            pl.semaphore_signal(barrier, inc=1, device_id=one, device_id_type=MESH)
        return lambda: pl.semaphore_wait(barrier, len(to))

    def settle(self):
        for one in self.moves:
            one.wait_send()

    def finish(self):
        for one in self.moves:
            one.wait_recv()
            one.wait_send()


def gather(L, axis, slot, arrived=None, log=None):
    me = L.at[axis]
    moves = [
        (k, L.copy(slot(me), slot(me), L.device(**{axis: L.around(axis, k)}))) for k in (2, 1, 3)
    ]
    if log is not None:
        log.extend(one for _, one in moves)
    if arrived:
        arrived(me)
    yield
    for k, one in moves[1:] + moves[:1]:
        one.wait_recv()
        if arrived:
            arrived(L.around(axis, 4 - k))


def reduce(L, axis, src, bufs, add):
    moves = []
    for buf, k in zip(bufs, (2, 1, 3)):
        j = L.around(axis, k)
        moves.append(L.copy(src(j), buf, L.device(**{axis: j})))
    yield
    for one in moves:
        one.wait_recv()
    add(src(L.at[axis]), bufs)


def add_blocks(lead):
    count = int(np.prod(lead)) if lead else 1

    def add(dst, srcs):
        def body(n, carry):
            where = []
            for size in reversed(lead):
                where.append(lax.rem(n, size))
                n = lax.div(n, size)
            where = tuple(reversed(where)) + (slice(None), slice(None))
            total = dst[where].astype(F32)
            for one in srcs:
                total = total + one[where].astype(F32)
            dst[where] = total.astype(BF)
            return carry

        lax.fori_loop(0, count, body, 0)

    return add


def columns(ref, lead, lo, width):
    return ref.at[(slice(None),) * (lead + 1) + (pl.ds(lo, width),)]


def step(*gens):
    for g in gens:
        next(g, None)


def together(*gens):
    gens = list(gens)
    while gens:
        alive = []
        for g in gens:
            try:
                next(g)
                alive.append(g)
            except StopIteration:
                pass
        gens = alive
        if gens:
            yield


def drain(*gens):
    for _ in together(*gens):
        pass


def mixer_slot(L, buf, sub, stage, lo, width):
    ref = buf.at[L.c, sub]
    axis = ("xy" if sub == 0 else "yx")[stage]

    def slot(j):
        if stage == 0:
            block = ref.at[L.y, j] if axis == "x" else ref.at[j, L.x]
        else:
            block = ref.at[j] if axis == "y" else ref.at[:, j]
        return columns(block, stage, lo, width)

    return axis, slot


def gather_mixer(L, R, sub, lo, width, log=None):
    sent = []
    for stage in range(2):
        axis, slot = mixer_slot(L, R.win, sub, stage, lo, width)

        def arrived(j, slot=slot):
            sent.append(L.copy(slot(j), slot(j), L.sibling))

        yield from gather(L, axis, slot, arrived if stage == 1 else None, log)
    if log is not None:
        log.extend(sent)
    yield
    for one in sent:
        one.wait_recv()


def reduce_mixer(L, R, buf, lo, width):
    moves = []
    for sub in range(2):
        theirs = columns(buf.at[1 - L.c, sub], 2, lo, width)
        moves.append(L.copy(theirs, columns(R.wsib.at[sub], 2, lo, width), L.sibling))
    yield
    gens = []
    for sub in range(2):
        moves[sub].wait_recv()
        mine = columns(buf.at[L.c, sub], 2, lo, width)
        add_blocks((4, 4))(mine, [columns(R.wsib.at[sub], 2, lo, width)])
        gens.append(reduce_chips(L, R, buf, sub, lo, width))
        next(gens[-1])
    yield
    yield from together(*gens)


def reduce_chips(L, R, buf, sub, lo, width):
    for stage in (1, 0):
        axis, slot = mixer_slot(L, buf, sub, stage, lo, width)
        bufs = [columns(one.at[sub], stage, lo, width) for one in R.mbufs[stage]]
        yield from reduce(L, axis, slot, bufs, add_blocks((4,) * stage))


def deal_rows(L, buf, kind, width, fin, rfin, place):
    for sub in range(2):
        for k in range(2):
            lo = kind[0] + width * k
            both = buf[L.c, sub, L.y, L.x, :, lo : lo + width].astype(F32)
            for core in range(2):
                fin[2 * sub + k, core, :, place : place + width] = both[8 * core : 8 * core + 8, :]
    cols = pl.ds(place, width)
    moves = [
        L.copy(fin.at[j, h, :, cols], rfin.at[L.z, L.c, :, cols], L.device(z=j, c=h))
        for j, h in L.slab()
    ]
    rfin[L.z, L.c, :, cols] = fin[L.z, L.c, :, cols]
    return moves


def deal_halves(L, buf, kind, fin, rfin):
    for d in range(2):
        fin[d] = buf[L.c, d, L.y, L.x, :, kind[0] : kind[0] + 512].astype(F32)
    return L.copy(fin.at[1 - L.c], rfin, L.sibling)


def reduce_late(L, R):
    yield from reduce_mixer(L, R, R.dwin, *LATE)
    moves = deal_rows(L, R.dwin, LATE, GW, R.fin, R.rfin, 0)
    yield
    for one in moves:
        one.wait_recv()


def reduce_early(L, R):
    yield from reduce_mixer(L, R, R.dwin, EARLY[0], EARLY[1] + OUT[1])
    moves = deal_rows(L, R.dwin, EARLY, GW, R.fin, R.rfin, GW)
    moves.append(deal_halves(L, R.dwin, OUT, R.ofin, R.orfin))
    yield
    for one in moves:
        one.wait_recv()
    lo, hi = in_core_order(L, R.ofin[L.c], R.orfin[...])
    R.o_mo[:, 0:512] = lo[0:12, :]
    R.o_mo[:, 512:1024] = hi[0:12, :]
    R.o_ao[:, 0:512] = lo[12:16, :]
    R.o_ao[:, 512:1024] = hi[12:16, :]
    R.send_out("o_mo", "o_ao")


def reduce_ffn(L, R):
    yield from reduce_mixer(L, R, R.win, *FFN)
    moves = deal_rows(L, R.win, FIN, FW, R.ffin, R.frfin, 0)
    moves.append(deal_halves(L, R.win, FOUT, R.dfin, R.drfin))
    yield
    for one in moves:
        one.wait_recv()
    lo, hi = in_core_order(L, R.dfin[L.c], R.drfin[...])
    R.o_fd[:, 0:512] = lo
    R.o_fd[:, 512:1024] = hi
    turn = (iota((FW, FW), 1) == deal(iota((FW, FW), 0))).astype(F32)
    rows = [R.frfin[j, core] for core in range(2) for j in range(4)]
    out = mm_exact(jnp.concatenate(rows, axis=0), turn)
    for j in range(4):
        R.o_fg[:, FW * j : FW * j + FW] = out[8 * j : 8 * j + 8, :]
        R.o_fu[:, FW * j : FW * j + FW] = out[32 + 8 * j : 40 + 8 * j, :]
    R.gcol[0] = gain_column([(R.w_fg, R.o_fg), (R.w_fu, R.o_fu)], R.gain_mid)
    R.send_out("o_fd", "o_fg", "o_fu")


def reduce_blocks(L, ref, recv):
    return reduce(L, "z", lambda j: ref.at[j], [recv.at[n] for n in range(3)], add_blocks(()))


def gather_blocks(L, ref):
    return gather(L, "z", lambda j: ref.at[j])


def reduce_small(L, R):
    for part in range(3):
        R.small[5:6, 128 * part : 128 * part + 128] = R.hsum[part : part + 1, :]
    R.smc[L.c] = R.small[...]
    move = L.copy(R.smc.at[L.c], R.smc.at[L.c], L.sibling)
    yield
    move.wait_recv()
    R.smx[L.x] = R.smc[0] + R.smc[1]
    yield from gather(L, "x", lambda j: R.smx.at[j])
    R.smy[L.y] = (R.smx[0] + R.smx[1]) + (R.smx[2] + R.smx[3])
    yield from gather(L, "y", lambda j: R.smy.at[j])
    R.smz[L.z] = (R.smy[0] + R.smy[1]) + (R.smy[2] + R.smy[3])
    yield from gather(L, "z", lambda j: R.smz.at[j])
    for j in range(4):
        R.o_conv[:, 384 * j : 384 * j + 384] = R.smz[j, :, 0:384]
    total = (R.smz[0] + R.smz[1]) + (R.smz[2] + R.smz[3])
    R.o_conv[:, 1536:1792] = total[:, 384:640]
    lane = iota((8, 128), 1)
    for part in range(3):
        heads = jnp.zeros((8, 128), F32)
        for j in range(4):
            one = jnp.where(lane < HEADS, R.smz[j, :, 128 * part : 128 * part + 128], 0.0)
            heads = heads + (one if j == 0 else roll(one, HEADS * j, 1))
        R.o_head[part : part + 1, :] = heads[5:6, :]


def setup(L, R):
    lane = iota((1, 128), 1)
    first = HEADS * L.z
    for row, ref in enumerate((R.step_bias, R.decay_log)):
        total = jnp.zeros((1, 128), F32)
        for h in range(HEADS):
            total = jnp.where(lane == h, ref[first + h], total)
        R.hpar[row : row + 1, :] = total
    cols = pl.ds(pl.multiple_of(XW * L.z, 128), XW)
    R.cpar[0:4, 0:384] = R.taps[:, cols]
    R.cpar[0:4, 384:640] = R.taps[:, 1536:1792]
    R.cpar[4:5, 0:384] = R.bias[cols].reshape(1, 384)
    R.cpar[4:5, 384:640] = R.bias[1536:1792].reshape(1, 256)
    lane = iota((1, XW), 1) // 64
    total = jnp.zeros((1, XW), F32)
    for h in range(HEADS):
        total = jnp.where(lane == h, R.skip_gain[first + h], total)
    R.cpar[5:6, 0:384] = total
    seg = R.seg[...].astype(F32)
    R.segr[0:1, :] = seg
    for b in range(4):
        row = seg[:, b * ROWS : b * ROWS + ROWS]
        R.segc[b * ROWS : b * ROWS + ROWS, :] = jnp.broadcast_to(row, (ROWS, ROWS)).T


def pack_weights(L, R):
    shape8 = (8, 128)
    low = lane_low(shape8)
    lane = iota(shape8, 1)
    sub = iota(shape8, 0)
    k, v = R.w_k[...], R.w_v[...]
    k_up, v_up = roll(k, 64, 1), roll(v, 64, 1)
    R.misc[...] = jnp.zeros(shape8, F32)
    R.misc[:, 0:24] = R.w_step[...]
    misc = R.misc[...]
    for row in range(8):
        misc = jnp.where((lane == 24) & (sub == row), R.gain_in[row], misc)
        misc = jnp.where((lane == 25) & (sub == row), R.gain_mid[row], misc)
    for j in range(4):
        R.pack[j, 0, :, 0:384] = R.w_min[:, 1536 + 384 * j : 1920 + 384 * j]
        R.pack[j, 0, :, 384:768] = R.w_min[:, 384 * j : 384 * j + 384]
        R.pack[j, 1, :, 0:256] = R.w_bc[...]
        mine = misc if j == 0 else roll(misc, 128 - HEADS * j, 1)
        R.pack[j, 1, :, 256:384] = jnp.where(
            lane < HEADS, mine, jnp.where((lane >= 24) & (lane < 26), misc, 0.0)
        )
        R.pack[j, 1, :, 384:512] = R.w_q[:, 128 * j : 128 * j + 128]
        R.pack[j, 1, :, 512:640] = jnp.where(low, k, v_up) if j < 2 else jnp.where(low, k_up, v)
        R.pack[j, 1, :, 640:768] = jnp.zeros(shape8, F32)
    for h in range(2):
        R.opack[h, 0:12, :] = R.w_mo[:, 512 * h : 512 * h + 512]
        R.opack[h, 12:16, :] = R.w_ao[:, 512 * h : 512 * h + 512]


def deal(n):
    return 32 * ((n % 256) // 16) + 16 * (n // 256) + n % 16


def pack_ffn(L, R):
    turn = (iota((FW, FW), 0) == deal(iota((FW, FW), 1))).astype(BF)
    rows = [ref[:, FW * j : FW * j + FW] for ref in (R.w_fg, R.w_fu) for j in range(4)]
    out = mm(jnp.concatenate(rows, axis=0).astype(BF), turn)
    for j in range(4):
        R.fpack[j, 0] = out[8 * j : 8 * j + 8, :]
        R.fpack[j, 1] = out[32 + 8 * j : 40 + 8 * j, :]
    for h in range(2):
        R.dpack[h] = R.w_fd[:, 512 * h : 512 * h + 512]


def gain_column(pairs, scalars):
    total = jnp.zeros((8, 1), F32)
    for weight, grad in pairs:
        weight = weight[...].astype(BF).astype(F32)
        total = total + jnp.sum(weight * grad[...], axis=1, keepdims=True)
    sub = iota((8, 128), 0)
    gain = jnp.ones((8, 128), F32)
    for row in range(8):
        gain = jnp.where(sub == row, scalars[row], gain)
    return total / gain.astype(BF).astype(F32)


def unpack_inputs(R):
    lane = iota((8, 128), 1)
    low = lane_low((8, 128))
    misc = jnp.zeros((8, 128), F32)
    for j in range(4):
        R.o_min[:, 384 * j : 384 * j + 384] = R.rfin[j, 0, :, 384:768]
        R.o_min[:, 1536 + 384 * j : 1920 + 384 * j] = R.rfin[j, 0, :, 0:384]
        R.o_q[:, 128 * j : 128 * j + 128] = R.rfin[j, 1, :, 384:512]
        part = R.rfin[j, 1, :, 256:384]
        own = jnp.where(lane < HEADS, part, 0.0)
        misc = misc + (own if j == 0 else roll(own, HEADS * j, 1))
    R.o_misc[...] = misc
    R.o_bc[...] = (R.rfin[0, 1, :, 0:256] + R.rfin[1, 1, :, 0:256]) + (
        R.rfin[2, 1, :, 0:256] + R.rfin[3, 1, :, 0:256]
    )
    kv0 = R.rfin[0, 1, :, 512:640] + R.rfin[1, 1, :, 512:640]
    kv1 = R.rfin[2, 1, :, 512:640] + R.rfin[3, 1, :, 512:640]
    R.o_k[...] = jnp.where(low, kv0, roll(kv1, 64, 1))
    R.o_v[...] = jnp.where(low, roll(kv0, 64, 1), kv1)
    pairs = [(R.w_min, R.o_min), (R.w_bc, R.o_bc), (R.w_step, R.o_misc.at[:, 0:24])]
    pairs += [(R.w_q, R.o_q), (R.w_k, R.o_k), (R.w_v, R.o_v)]
    first = gain_column(pairs, R.gain_in)
    both = jnp.where(iota((8, 128), 1) == 0, first, R.gcol[0])
    turned = jnp.concatenate([both, jnp.zeros((120, 128), F32)], axis=0).T
    R.o_head[3:5, :] = turned[0:2, :]


def in_core_order(L, mine, other):
    first = L.c == 0
    return jnp.where(first, mine, other), jnp.where(first, other, mine)


def own_rows(L, R, exch, kinds, width):
    for sub in range(2):
        for k in range(2):
            both = jnp.concatenate([exch[2 * sub + k, d] for d in range(2)], axis=0).astype(BF)
            for n, kind in enumerate(kinds):
                lo = kind[0] + width * k
                R.win[L.c, sub, L.y, L.x, :, lo : lo + width] = both[:, width * n : width * n + width]


def own_halves(L, R, pack, other, kind):
    for d, part in enumerate(in_core_order(L, pack[L.c], other[...])):
        R.win[L.c, d, L.y, L.x, :, kind[0] : kind[0] + 512] = part.astype(BF)


def to_slab(L, pack, exch):
    moves = [L.copy(pack.at[j, h], exch.at[L.z, L.c], L.device(z=j, c=h)) for j, h in L.slab()]
    exch[L.z, L.c] = pack[L.z, L.c]
    return moves


def come(*moves):
    for one in moves:
        one.wait_recv()


def middle_rows(L, R, h):
    block, rows = mid_rows(L, h)
    total = R.xall[block, rows, :].astype(F32) + R.branch[h, L.z].astype(F32)
    for n in range(3):
        total = total + R.zrecv[h, n].astype(F32)
    R.middle[h] = total
    inv = lax.rsqrt(jnp.mean(total * total, axis=-1, keepdims=True) + EPS)
    R.secall[h, L.z] = (total * inv * R.gain[1:2, :]).astype(BF)


def back_middle(L, R, h):
    block, rows = mid_rows(L, h)
    total = R.gsec[h, L.z].astype(F32)
    for n in range(3):
        total = total + R.zrecv[2 + h, n].astype(F32)
    gmid = norm_back(R.middle[h], R.gain[1:2, :], total)
    gmid = gmid + R.cotall[block, rows, :].astype(F32)
    R.gmid[h] = gmid
    R.gball[h, L.z] = gmid.astype(BF)


def keep(dst, srcs):
    pass


def to_owner(L, R, ref, n):
    return reduce(L, "z", lambda j: ref.at[j], [R.zrecv.at[n, k] for k in range(3)], keep)


def kernel(R):
    L = Links(R.send, R.recv)
    greeted = L.greet()
    R.await_in(*WEIGHTS_IN)
    pack_weights(L, R)
    R.await_in("tok", "cot")
    R.xall[L.z] = R.tok[...]
    R.cotall[L.z] = R.cot[...]
    greeted()

    moves = to_slab(L, R.pack, R.exch)
    wo = L.copy(R.opack.at[1 - L.c], R.exo, L.sibling)
    R.await_in("seg", "taps", "bias")
    setup(L, R)
    R.await_in("w_fg", "w_fu", "w_fd")
    pack_ffn(L, R)
    come(*moves)
    own_rows(L, R, R.exch, (LATE, EARLY), GW)
    late = together(*[gather_mixer(L, R, sub, *LATE) for sub in range(2)])
    step(late)
    xgen = gather_blocks(L, R.xall)
    step(xgen)
    fmoves = to_slab(L, R.fpack, R.fexch)
    do = L.copy(R.dpack.at[1 - L.c], R.dexo, L.sibling)
    come(wo)
    own_halves(L, R, R.opack, R.exo, OUT)
    step(late)
    early = together(
        *[gather_mixer(L, R, sub, EARLY[0], EARLY[1] + OUT[1]) for sub in range(2)]
    )
    step(early)
    R.small[...] = jnp.zeros((8, CW), F32)
    R.gk[...] = jnp.zeros((LEN, 128), F32)
    R.gv[...] = jnp.zeros((LEN, 128), F32)
    R.state[0] = jnp.zeros((128, XW), F32)
    R.gstate[...] = jnp.zeros((128, XW), F32)
    R.hsum[...] = jnp.zeros((8, 128), F32)
    step(late)
    step(early)
    drain(late)
    gains(R)
    drain(xgen)
    cgen = gather_blocks(L, R.cotall)
    step(cgen)
    norm_first(R)
    project_late(R)
    convolve(R)
    come(do, *fmoves)
    own_rows(L, R, R.fexch, (FIN,), FW)
    own_halves(L, R, R.dpack, R.dexo, FOUT)
    fsent = []
    fgen = together(*[gather_mixer(L, R, sub, *FFN, fsent) for sub in range(2)])
    step(fgen)
    steps(R)
    recurrence(R, 0, 2)
    drain(early)
    step(fgen)
    project_early(R)
    R.await_in("cosr", "sinr", "perm5")
    rotated(R)
    attend(R, 0, 2)
    out_project(R, 0)
    branch = [to_owner(L, R, R.branch.at[h], h) for h in range(2)]
    step(branch[0])
    recurrence(R, 2, 4)
    attend(R, 2, 4)
    out_project(R, 1)
    step(branch[1])
    step(fgen)
    second = [gather_blocks(L, R.secall.at[h]) for h in range(2)]
    for h in range(2):
        drain(branch[h])
        middle_rows(L, R, h)
        step(second[h])
    drain(cgen, fgen)
    gsec = [to_owner(L, R, R.gsec.at[h], 2 + h) for h in range(2)]
    for h in range(2):
        drain(second[h])
        ffn(R, h)
        step(gsec[h])
    gball = [gather_blocks(L, R.gball.at[h]) for h in range(2)]
    for one in fsent:
        one.wait_send()
    ffn_out(R, L)
    drain(gsec[0])
    back_middle(L, R, 0)
    step(gball[0])
    ffn_grads(R)
    wgen = reduce_ffn(L, R)
    step(wgen)
    drain(gsec[1])
    back_middle(L, R, 1)
    step(gball[1])
    step(wgen)
    drain(gball[0])
    back_out(R, 0)
    back_attend(R, 0, 2)
    drain(gball[1])
    fout = reduce_blocks(L, R.fout, R.frecv)
    step(fout)
    back_out(R, 1)
    back_gate(R)
    back_attend(R, 2, 4)
    back_rotated(R)
    out_grad(R)
    early_grads(R)
    egen = reduce_early(L, R)
    step(egen)
    step(wgen)
    back_recurrence(R, 0, 2)
    step(egen)
    step(wgen)
    back_recurrence(R, 2, 4)
    back_convolve(R)
    step(wgen)
    late_grads(R)
    lgen = reduce_late(L, R)
    step(lgen)
    mgen = reduce_small(L, R)
    step(mgen)
    hgen = back_first(R, L)
    step(hgen)
    step(lgen, mgen)
    step(hgen)
    step(egen)
    step(hgen)
    step(mgen)
    step(hgen)
    step(lgen)
    step(egen)
    step(mgen)
    drain(wgen, fout)
    R.o_out[...] = R.fout[L.z]
    R.send_out("o_out")
    step(lgen)
    drain(egen)
    drain(mgen)
    drain(hgen)
    R.o_tok[...] = R.gfirst[L.z]
    R.send_out("o_tok")
    drain(lgen)
    unpack_inputs(R)
    R.send_out("o_min", "o_bc", "o_misc", "o_q", "o_k", "o_v", "o_conv", "o_head")
    L.finish()
    R.finish_out()


INS = dict(
    w_min=((8, 3072), F32),
    w_bc=((8, 256), F32),
    w_step=((8, 24), F32),
    w_q=((8, 512), F32),
    w_k=((8, 128), F32),
    w_v=((8, 128), F32),
    w_mo=((12, D), F32),
    w_ao=((4, D), F32),
    tok=((ROWS, D), BF),
    cot=((ROWS, D), BF),
    w_fg=((8, 2048), F32),
    w_fu=((8, 2048), F32),
    w_fd=((16, D), F32),
    seg=((1, LEN), jnp.int32),
    taps=((4, 1792), F32),
    bias=((1792,), F32),
    cosr=((LEN, 128), F32),
    sinr=((LEN, 128), F32),
    perm5=((512, 512), BF),
)
WEIGHTS_IN = list(INS)[:8]
SCALARS = ("gain_in", "gain_mid", "step_bias", "decay_log", "skip_gain")
OUTS = dict(
    o_out=((ROWS, D), BF),
    o_tok=((ROWS, D), BF),
    o_min=((8, 3072), F32),
    o_bc=((8, 256), F32),
    o_misc=((8, 128), F32),
    o_q=((8, 512), F32),
    o_k=((8, 128), F32),
    o_v=((8, 128), F32),
    o_mo=((12, D), F32),
    o_ao=((4, D), F32),
    o_fg=((8, 2048), F32),
    o_fu=((8, 2048), F32),
    o_fd=((16, D), F32),
    o_conv=((8, 1792), F32),
    o_head=((8, 128), F32),
)
SCRATCH = dict(
    xall=((4, ROWS, D), BF),
    segc=((LEN, 128), F32),
    segr=((8, LEN), F32),
    cpar=((8, CW), F32),
    hpar=((8, 128), F32),
    misc=((8, 128), F32),
    pack=((4, 2, 8, 768), F32),
    exch=((4, 2, 8, 768), F32),
    opack=((2, 16, 512), F32),
    exo=((16, 512), F32),
    fpack=((4, 2, 8, FW), F32),
    fexch=((4, 2, 8, FW), F32),
    dpack=((2, 16, 512), F32),
    dexo=((16, 512), F32),
    win=((2, 2, 4, 4, 16, PK), BF),
    dwin=((2, 2, 4, 4, 16, FIN[0]), BF),
    cotall=((4, ROWS, D), BF),
    secall=((2, 4, 64, D), BF),
    hid=((LEN, FW), BF),
    gab=((LEN, 2 * FW), BF),
    gsec=((2, 4, 64, D), BF),
    fout=((4, ROWS, D), BF),
    gain=((8, D), F32),
    gcol=((1, 8, 128), F32),
    first=((LEN, D), BF),
    gate=((LEN, XW), F32),
    raw=((LEN, CW), BF),
    pq=((LEN, 128), F32),
    pkv=((LEN, 128), F32),
    pm=((LEN, 128), F32),
    pre=((LEN, CW), F32),
    mixed=((LEN, CW), F32),
    step=((LEN, 128), F32),
    run=((LEN, 128), F32),
    state=((5, 128, XW), F32),
    ssm=((LEN, XW), F32),
    q=((LEN, 128), BF),
    kk=((LEN, 128), BF),
    vv=((LEN, 128), BF),
    probs=((2, LEN, LEN), BF),
    left=((LEN, 512), BF),
    left_p=((LEN, 512), BF),
    branch=((2, 4, 64, D), BF),
    zrecv=((4, 3, 64, D), BF),
    frecv=((3, ROWS, D), BF),
    hrecv=((3, ROWS, D), BF),
    middle=((2, 64, D), F32),
    gmid=((2, 64, D), F32),
    gsum=((ROWS, D), F32),
    gball=((2, 4, 64, D), BF),
    gleft=((LEN, 512), F32),
    gq=((LEN, 128), F32),
    gk=((LEN, 128), F32),
    gv=((LEN, 128), F32),
    gstate=((128, XW), F32),
    hsum=((8, 128), F32),
    gmix=((LEN, CW), F32),
    gproj=((LEN, 4 * GW), BF),
    small=((8, CW), F32),
    factor=((4, 8, 128), F32),
    inlet_x=((LEN, XW), F32),
    tail_x=((LEN, XW), F32),
    factor_x=((4, 8, XW), F32),
    step_x=((LEN, XW), F32),
    mix=((4, HEADS, ROWS, ROWS), BF),
    weights=((4, HEADS, ROWS, ROWS), BF),
    gfirst=((4, ROWS, D), BF),
    wsib=((2, 4, 4, 16, PK), BF),
    smc=((2, 8, CW), F32),
    smx=((4, 8, CW), F32),
    smy=((4, 8, CW), F32),
    smz=((4, 8, CW), F32),
    fin=((4, 2, 8, 768), F32),
    rfin=((4, 2, 8, 768), F32),
    ofin=((2, 16, 512), F32),
    orfin=((16, 512), F32),
    ffin=((4, 2, 8, FW), F32),
    frfin=((4, 2, 8, FW), F32),
    dfin=((2, 16, 512), F32),
    drfin=((16, 512), F32),
)
COPIES = 250


def ring_buffers(parts, width, stages):
    shapes = {}
    for stage in range(stages):
        for n in range(3):
            shapes[(stage, n)] = ((parts,) + (4,) * stage + (16, width), BF)
    return shapes


MBUFS = ring_buffers(2, PK, 2)


def entry(*refs):
    refs = list(refs)
    take = lambda names: [(name, refs.pop(0)) for name in names]
    given, scalars, results = dict(take(INS)), take(SCALARS), dict(take(OUTS))
    inside = take(INS)
    R = types.SimpleNamespace(**dict(scalars + inside + take(OUTS) + take(SCRATCH)))
    bufs = dict(take(MBUFS))
    R.mbufs = [[bufs[key] for key in MBUFS if key[0] == stage] for stage in range(2)]
    R.send, R.recv, came, left = refs
    loads = {}
    for n, name in enumerate(INS):
        loads[name] = pltpu.make_async_copy(given[name], getattr(R, name), came.at[n])
        loads[name].start()
    stores = []

    def await_in(*names):
        for name in names:
            loads[name].wait()

    def send_out(*names):
        for name in names:
            n = len(stores)
            stores.append(pltpu.make_async_copy(getattr(R, name), results[name], left.at[n]))
            stores[-1].start()

    def finish_out():
        for one in stores:
            one.wait()

    R.await_in, R.send_out, R.finish_out = await_in, send_out, finish_out
    kernel(R)


def layer(*args):
    anywhere = pl.BlockSpec(memory_space=pl.ANY)
    smem = pl.BlockSpec(memory_space=pltpu.SMEM)
    shapes = [*INS.values(), *OUTS.values(), *SCRATCH.values(), *MBUFS.values()]
    scratch = [pltpu.VMEM(shape, kind) for shape, kind in shapes]
    scratch += [pltpu.SemaphoreType.DMA((n,)) for n in (COPIES, COPIES, len(INS), len(OUTS))]
    return pl.pallas_call(
        entry,
        out_shape=[jax.ShapeDtypeStruct(shape, kind) for shape, kind in OUTS.values()],
        in_specs=[anywhere] * len(INS) + [smem] * len(SCALARS),
        out_specs=[anywhere] * len(OUTS),
        scratch_shapes=scratch,
        compiler_params=pltpu.CompilerParams(
            collective_id=0, has_side_effects=True, vmem_limit_bytes=63 * 2**20
        ),
    )(*args)


SAME = [name for name in OUTS if name not in ("o_misc", "o_conv", "o_head")]
RESULTS = {name: OUTS[name] for name in SAME}
RESULTS.update(
    step=((8, 24), F32),
    taps=((4, 1792), F32),
    bias=((1792,), F32),
    gain_in=((8,), F32),
    gain_mid=((8,), F32),
    step_bias=((24,), F32),
    decay_log=((24,), F32),
    skip_gain=((24,), F32),
)


def deliver_kernel(*refs):
    given = dict(zip(OUTS, refs))
    result = dict(zip(RESULTS, refs[len(OUTS) :]))
    for name in SAME:
        result[name][...] = given[name][...]
    result["step"][...] = given["o_misc"][:, 0:24]
    result["taps"][...] = given["o_conv"][0:4, :]
    result["bias"][...] = given["o_conv"][4, :]
    head = given["o_head"]
    for row, name in enumerate(("step_bias", "decay_log", "skip_gain")):
        result[name][...] = head[row, 0:24]
    result["gain_in"][...] = head[3, 0:8]
    result["gain_mid"][...] = head[4, 0:8]


def deliver(outs):
    vmem = pl.BlockSpec(memory_space=pltpu.VMEM)
    results = pl.pallas_call(
        deliver_kernel,
        out_shape=[jax.ShapeDtypeStruct(shape, kind) for shape, kind in RESULTS.values()],
        in_specs=[vmem] * len(OUTS),
        out_specs=[vmem] * len(RESULTS),
    )(*outs)
    return dict(zip(RESULTS, results))


def rotary_tables():
    lane = np.arange(128)
    power = (-2.0 * (lane % 32).astype(np.float32) / np.float32(64)).astype(np.float32)
    frequency = np.power(np.float32(ROPE), power).astype(np.float32)
    angles = np.arange(LEN, dtype=np.float32)[:, None] * frequency[None, :]
    sign = np.where(lane % 64 < 32, -1.0, 1.0)
    cosine = np.cos(angles.astype(np.float64)).astype(np.float32)
    sine = (np.sin(angles.astype(np.float64)) * sign).astype(np.float32)
    return cosine, sine


def out_order():
    n = np.arange(512)
    device = np.where(n < 384, n // 12, (n - 384) // 4)
    row = np.where(n < 384, n % 12, 12 + (n - 384) % 4)
    to = (device % 2) * 256 + (device // 2) * 16 + row
    table = np.zeros((512, 512), np.float32)
    table[n, to] = 1.0
    return table


def shards(
    tokens,
    segments,
    cotangent,
    gain_in,
    mamba_in,
    mamba_bc,
    mamba_step,
    in_query,
    in_key,
    in_value,
    mamba_out,
    attn_out,
    gain_mid,
    ffn_gate,
    ffn_up,
    ffn_down,
    conv_taps,
    conv_bias,
    step_bias,
    decay_log,
    skip_gain,
):
    cosine, sine = rotary_tables()
    outs = layer(
        mamba_in,
        mamba_bc,
        mamba_step,
        in_query,
        in_key,
        in_value,
        mamba_out,
        attn_out,
        tokens[0],
        cotangent[0],
        ffn_gate,
        ffn_up,
        ffn_down,
        segments,
        conv_taps,
        conv_bias,
        jnp.asarray(cosine),
        jnp.asarray(sine),
        jnp.asarray(out_order(), BF),
        gain_in,
        gain_mid,
        step_bias,
        decay_log,
        skip_gain,
    )
    r = deliver(outs)
    return (
        r["o_out"][None],
        r["o_tok"][None],
        r["gain_in"],
        r["o_min"],
        r["o_bc"],
        r["step"],
        r["o_q"],
        r["o_k"],
        r["o_v"],
        r["o_mo"],
        r["o_ao"],
        r["gain_mid"],
        r["o_fg"],
        r["o_fu"],
        r["o_fd"],
        r["taps"],
        r["bias"],
        r["step_bias"],
        r["decay_log"],
        r["skip_gain"],
    )


def solution(mesh):
    one = P(("ctx", "fsdp"))
    rows = P(("ctx", "fsdp"), None)
    block = P("fsdp", "ctx", None)
    return jax.shard_map(
        shards,
        mesh=mesh,
        in_specs=(block, P("fsdp", None), block, one)
        + (rows,) * 8
        + (one,)
        + (rows,) * 3
        + (P(),) * 5,
        out_specs=(block, block, one) + (rows,) * 8 + (one,) + (rows,) * 3 + (P(),) * 5,
        check_vma=False,
    )
```

```python
import types

import jax
import jax.numpy as jnp
import numpy as np
from jax import lax
from jax.experimental import pallas as pl
from jax.experimental.pallas import tpu as pltpu
from jax.sharding import PartitionSpec as P

BF = jnp.bfloat16
F32 = jnp.float32
MESH = pl.DeviceIdType.MESH
EPS = 1e-06
ROPE = 100000000000.0

D = 1024
LEN = 512
ROWS = 128
HEADS = 6
XW = 384
CW = 640
GW = 384
PK = 3584
FW = 512


def mm(a, b):
    return lax.dot_general(a, b, (((1,), (0,)), ((), ())), preferred_element_type=F32)


def mm_nt(a, b):
    return lax.dot_general(a, b, (((1,), (1,)), ((), ())), preferred_element_type=F32)


def mm_tn(a, b):
    return lax.dot_general(a, b, (((0,), (0,)), ((), ())), preferred_element_type=F32)


def iota(shape, dim):
    return lax.broadcasted_iota(jnp.int32, shape, dim)


def lane_low(shape):
    return iota(shape, 1) & 64 == 0


def roll(v, shift, axis):
    size = v.shape[axis]
    return pltpu.roll(v, shift % size, axis)


def swap_halves(v):
    lanes = v.shape[1]
    first = iota(v.shape, 1) & 32 == 0
    return jnp.where(first, roll(v, lanes - 32, 1), roll(v, 32, 1))


def sigmoid(v):
    return 1.0 / (1.0 + jnp.exp(-v))


def softplus(v):
    return jnp.maximum(v, 0.0) + jnp.log1p(jnp.exp(-jnp.abs(v)))


def spread_heads(v):
    rows = v.shape[0]
    low = lane_low((rows, 128))
    tiles = []
    for pair in range(HEADS // 2):
        a = jnp.broadcast_to(v[:, 2 * pair : 2 * pair + 1], (rows, 128))
        b = jnp.broadcast_to(v[:, 2 * pair + 1 : 2 * pair + 2], (rows, 128))
        tiles.append(jnp.where(low, a, b))
    return jnp.concatenate(tiles, axis=1)


def mm_terms(a, b, count):
    side = 0 if a.dtype == F32 else 1
    rest, total = (a, b)[side], None
    for _ in range(count):
        term = rest.astype(BF)
        rest = rest - term.astype(F32)
        one = mm(term, b) if side == 0 else mm(a, term)
        total = one if total is None else total + one
    return total


def sum_heads(v):
    pick = (iota((XW, 128), 0) >> 6 == iota((XW, 128), 1)).astype(BF)
    return mm_terms(v, pick, 2)


def lower_ones():
    return (iota((ROWS, ROWS), 1) <= iota((ROWS, ROWS), 0)).astype(BF)


LATE, EARLY, OUT = (0, 2 * GW), (2 * GW, 2 * GW), (4 * GW, 512)
FIN, FOUT = (2048, 2 * FW), (2048 + 2 * FW, 512)
FFN = (FIN[0], FIN[1] + FOUT[1])


def chunk(R, core, kind, k, lo=0, width=GW):
    v = R.win[core, k // 2, :, :, :, pl.ds(kind[0] + GW * (k % 2) + lo, width)]
    return v.reshape(256, width)


def group_weight(R, core, kind):
    return jnp.concatenate([chunk(R, core, kind, k) for k in range(4)], axis=0)


def out_weight(R, kind=OUT):
    parts = []
    for core in range(2):
        rows = [R.win[core, d, :, :, :, pl.ds(kind[0], 512)].reshape(256, 512) for d in range(2)]
        parts.append(jnp.concatenate(rows, axis=0))
    return jnp.concatenate(parts, axis=1)


def seg_mask(R, k):
    seg = R.segc[...]
    return jnp.where(
        (seg == roll(seg, k, 0)) & (iota((LEN, 128), 0) >= k), 1.0, 0.0
    ).astype(F32)


def gains(R):
    pick = (iota((8, 128), 1) == iota((8, 128), 0) + 24).astype(BF)
    for k in range(4):
        R.gain[:, pl.ds(256 * k, 256)] = mm_nt(pick, chunk(R, 1, LATE, k, 256, 128))


def norm_first(R):
    gain = R.gain[0:1, :]

    def block(b, carry):
        x = R.xall[b].astype(F32)
        inv = lax.rsqrt(jnp.mean(x * x, axis=-1, keepdims=True) + EPS)
        R.first[pl.ds(pl.multiple_of(b * ROWS, ROWS), ROWS), :] = (x * inv * gain).astype(BF)
        return carry

    lax.fori_loop(0, 4, block, 0)


def project_late(R):
    first = R.first[...]
    out = mm(first, group_weight(R, 0, LATE))
    R.raw[:, 0:384] = out.astype(BF)
    out = mm(first, group_weight(R, 1, LATE))
    R.raw[:, 384:640] = out[:, 0:256].astype(BF)
    R.pm[...] = out[:, 256:384]


def project_early(R):
    first = R.first[...]
    out = mm(first, group_weight(R, 1, EARLY))
    R.pq[...] = out[:, 0:128]
    R.pkv[...] = out[:, 128:256]
    R.gate[...] = mm(first, group_weight(R, 0, EARLY))


def convolve(R):
    masks = [seg_mask(R, k) for k in range(1, 4)]
    for t in range(CW // 128):
        cols = slice(128 * t, 128 * t + 128)
        raw = R.raw[:, cols].astype(F32)
        total = R.cpar[4:5, cols] + R.cpar[0:1, cols] * raw
        for k in range(1, 4):
            total = total + R.cpar[k : k + 1, cols] * (roll(raw, k, 0) * masks[k - 1])
        R.pre[:, cols] = total
        R.mixed[:, cols] = total * sigmoid(total)


def steps(R):
    step = softplus(R.pm[...] + R.hpar[0:1, :])
    R.step[...] = step
    decay = -jnp.exp(R.hpar[1:2, :])
    ones = lower_ones()
    for b in range(4):
        rows = slice(b * ROWS, b * ROWS + ROWS)
        R.run[rows, :] = mm_terms(ones, decay * step[rows, :], 3)


def span(R, b):
    s = types.SimpleNamespace()
    s.at = pl.multiple_of(b * ROWS, ROWS)
    s.rows = pl.ds(s.at, ROWS)
    s.xs = R.mixed[s.rows, 0:384]
    s.xs_low = s.xs.astype(BF)
    s.wr_low = R.mixed[s.rows, 384:512].astype(BF)
    s.rd_low = R.mixed[s.rows, 512:640].astype(BF)
    s.step = R.step[s.rows, :]
    return s


def recurrence(R, begin, end):
    low = lane_low((ROWS, 128))

    def block(b, carry):
        s = span(R, b)
        run = R.run[s.rows, :]
        run_t = run.T
        seg = R.segc[s.rows, :]
        last = jnp.broadcast_to(seg[ROWS - 1 : ROWS, :], (ROWS, ROWS))
        earlier = R.segc[pl.ds(pl.multiple_of(jnp.maximum(s.at - 8, 0), 8), 8), :][7:8, :]
        earlier = jnp.where(jnp.broadcast_to(b, (1, 128)) == 0, -1.0, earlier)
        causal = (iota((ROWS, ROWS), 1) <= iota((ROWS, ROWS), 0)) & (
            seg == R.segr[0:1, s.rows]
        )
        inlet = jnp.where(seg == earlier, jnp.exp(run), 0.0)
        stop = run[ROWS - 1 : ROWS, :]
        tail0 = jnp.where(seg == last, jnp.exp(stop - run), 0.0)
        factor = jnp.where(last[0:1, :] == earlier, jnp.exp(stop), 0.0)
        inlet_x = spread_heads(inlet)
        step_x = spread_heads(s.step)
        tail_x = spread_heads(tail0)
        xstep = step_x * s.xs
        xstep_low = xstep.astype(BF)
        factor_x = spread_heads(jnp.broadcast_to(factor, (8, 128)))
        R.step_x[s.rows, :] = step_x
        R.factor[b] = jnp.broadcast_to(factor, (8, 128))
        R.inlet_x[s.rows, :] = inlet_x
        R.tail_x[s.rows, :] = tail_x
        R.factor_x[b] = factor_x
        cross = mm_nt(s.rd_low, s.wr_low)
        state = R.state[b]
        inflow = mm(s.rd_low, state.astype(BF))
        tiles = []
        for pair in range(HEADS // 2):
            xp = xstep_low[:, 128 * pair : 128 * pair + 128]
            both = []
            for h in (2 * pair, 2 * pair + 1):
                spread = run[:, h : h + 1] - run_t[h : h + 1, :]
                mix = jnp.exp(jnp.where(causal, spread, -10000.0))
                weights = (mix * cross).astype(BF)
                R.mix[b, h] = mix.astype(BF)
                R.weights[b, h] = weights
                both.append(mm(weights, xp))
            tiles.append(jnp.where(low, both[0], both[1]))
        R.ssm[s.rows, :] = (
            jnp.concatenate(tiles, axis=1) + inlet_x * inflow + R.cpar[5:6, 0:384] * s.xs
        )
        R.state[b + 1] = factor_x[0:1, :] * state + mm_tn(
            s.wr_low, (tail_x * xstep).astype(BF)
        )
        return carry

    lax.fori_loop(begin, end, block, 0)


def rotate(v, cosr, sinr):
    return v * cosr + swap_halves(v) * sinr


def rotated(R):
    low = lane_low((LEN, 128))
    R.q[...] = rotate(R.pq[...], R.cosr[...], R.sinr[...]).astype(BF)
    pkv = R.pkv[...]
    k = rotate(pkv, R.cosr[...], R.sinr[...])
    R.kk[...] = jnp.where(low, k, roll(k, 64, 1)).astype(BF)
    R.vv[...] = jnp.where(low, roll(pkv, 64, 1), pkv).astype(BF)


def half_only(v, e):
    low = lane_low(v.shape)
    return jnp.where(low if e == 0 else ~low, v, jnp.zeros_like(v))


def attend(R, begin, end):
    low = lane_low((ROWS, 128))
    for i in range(begin, end):
        rows = slice(i * ROWS, i * ROWS + ROWS)
        n = (i + 1) * ROWS
        seg_row = R.segr[0:1, 0:n]
        seg_col = jnp.broadcast_to(R.segc[rows, 0:1], (ROWS, n))
        allowed = (iota((ROWS, n), 1) <= iota((ROWS, n), 0) + i * ROWS) & (seg_col == seg_row)
        outs = []
        for e in range(2):
            scores = mm_nt(half_only(R.q[rows, :], e), R.kk[0:n, :]) * 0.125
            scores = jnp.where(allowed, scores, -1e30)
            shifted = jnp.exp(scores - jnp.max(scores, axis=-1, keepdims=True))
            probs = (shifted / jnp.sum(shifted, axis=-1, keepdims=True)).astype(BF)
            R.probs[e, rows, 0:n] = probs
            outs.append(mm(probs, R.vv[0:n, :]))
        R.left[rows, 384:512] = jnp.where(low, outs[0], outs[1]).astype(BF)


def out_project(R, h):
    rows = slice(256 * h, 256 * h + 256)
    gate = R.gate[rows, :]
    R.left[rows, 0:384] = (R.ssm[rows, :] * (gate * sigmoid(gate))).astype(BF)
    left = mm(R.left[rows, :], R.perm5[...]).astype(BF)
    R.left_p[rows, :] = left
    out = mm(left, out_weight(R))
    for j in range(4):
        R.branch[h, j] = out[64 * j : 64 * j + 64, :].astype(BF)


def unit_chunk(R, core, k):
    lo = FIN[0] + FW * (k % 2)
    return R.win[core, k // 2, :, :, :, lo : lo + FW].reshape(256, FW)


def ffn(R, h):
    second = R.secall[h].reshape(256, D)
    cot = R.cotall[2 * h : 2 * h + 2].reshape(256, D)
    rows = slice(256 * h, 256 * h + 256)
    for d in range(2):
        cols = slice(256 * d, 256 * d + 256)
        weights = []
        for core in range(2):
            parts = [unit_chunk(R, core, k)[:, cols] for k in range(4)]
            weights.append(jnp.concatenate(parts, axis=0))
        a = mm(second, weights[0])
        b = mm(second, weights[1])
        down = jnp.concatenate(
            [R.win[core, d, :, :, :, FOUT[0] : PK].reshape(256, 512) for core in range(2)], axis=1
        )
        ghid = mm_nt(cot, down)
        sig = sigmoid(a)
        act = a * sig
        R.hid[rows, cols] = (act * b).astype(BF)
        R.gab[rows, cols] = (ghid * b * (sig + act * (1.0 - sig))).astype(BF)
        R.gab[rows, FW + 256 * d : FW + 256 * d + 256] = (ghid * act).astype(BF)
    for k in range(4):
        weights = jnp.concatenate([unit_chunk(R, core, k) for core in range(2)], axis=1)
        out = mm_nt(R.gab[rows, :], weights)
        for j in range(4):
            R.gsec[h, j, :, 256 * k : 256 * k + 256] = out[64 * j : 64 * j + 64, :].astype(BF)


def ffn_out(R, L):
    out = mm(R.hid[...], out_weight(R, FOUT))
    for b in range(4):
        R.fout[b] = out[b * ROWS : b * ROWS + ROWS, :].astype(BF)
    for h in range(2):
        block, rows = mid_rows(L, h)
        R.fout[block, rows, :] = (
            R.fout[block, rows, :].astype(F32) + R.middle[h]
        ).astype(BF)


def ffn_grads(R):
    second = R.secall[...].reshape(LEN, D)
    for k in range(4):
        out = mm_tn(second[:, 256 * k : 256 * k + 256], R.gab[...]).astype(BF)
        lo = FIN[0] + FW * (k % 2)
        for core in range(2):
            part = out[:, FW * core : FW * core + FW]
            R.win[core, k // 2, :, :, :, lo : lo + FW] = part.reshape(4, 4, 16, FW)
    put_out_grad(R.win, FOUT, mm_tn(R.hid[...], R.cotall[...].reshape(LEN, D)))


def norm_back(x, gain, grad):
    inv = lax.rsqrt(jnp.mean(x * x, axis=-1, keepdims=True) + EPS)
    unit = x * inv
    scaled = grad * gain
    return inv * (scaled - unit * jnp.mean(scaled * unit, axis=-1, keepdims=True))


def mid_rows(L, h):
    return 2 * h + lax.div(L.z, 2), pl.ds(pl.multiple_of(64 * lax.rem(L.z, 2), 64), 64)


def back_out(R, h):
    rows = slice(256 * h, 256 * h + 256)
    raw = mm_nt(R.gball[h].reshape(256, D), out_weight(R))
    perm = R.perm5[...]
    hi = raw.astype(BF)
    rest = raw - hi.astype(F32)
    R.gleft[rows, :] = mm_nt(hi, perm) + mm_nt(rest.astype(BF), perm)


def back_gate(R):
    def block(b, carry):
        rows = pl.ds(pl.multiple_of(b * ROWS, ROWS), ROWS)
        gate = R.gate[rows, :]
        sig = sigmoid(gate)
        grad = R.gleft[rows, 0:384] * R.ssm[rows, :]
        R.gproj[rows, 768:1152] = (grad * (sig + gate * sig * (1.0 - sig))).astype(BF)
        return carry

    lax.fori_loop(0, 4, block, 0)


def back_attend(R, begin, end):
    low = lane_low((ROWS, 128))
    for i in range(begin, end):
        rows = slice(i * ROWS, i * ROWS + ROWS)
        n = (i + 1) * ROWS
        go = R.gleft[rows, 384:512].astype(BF)
        outs = []
        for e in range(2):
            probs = R.probs[e, rows, 0:n]
            pf = probs.astype(F32)
            go_e = half_only(go, e)
            dp = mm_nt(go_e, R.vv[0:n, :])
            ds = (pf * (dp - jnp.sum(pf * dp, axis=-1, keepdims=True))).astype(BF)
            outs.append(mm(ds, R.kk[0:n, :]))
            R.gk[0:n, :] += mm_tn(ds, half_only(R.q[rows, :], e))
            R.gv[0:n, :] += mm_tn(probs, go_e)
        R.gq[rows, :] = jnp.where(low, outs[0], outs[1]) * 0.125


def back_rotated(R):
    cosr, sinr = R.cosr[...], R.sinr[...]
    gq = rotate(R.gq[...], cosr, -sinr)
    R.gproj[:, 1152:1280] = gq.astype(BF)
    gk = R.gk[...] * 0.125
    gk = rotate(gk + roll(gk, 64, 1), cosr, -sinr)
    gv = R.gv[...]
    gv = gv + roll(gv, 64, 1)
    R.gproj[:, 1280:1408] = jnp.where(lane_low((LEN, 128)), gk, gv).astype(BF)
    R.gproj[:, 1408:1536] = jnp.zeros((LEN, 128), BF)


def back_recurrence(R, begin, end):
    low = lane_low((ROWS, 128))
    lane = iota((ROWS, 128), 1)
    sub = iota((ROWS, 128), 0)
    upper = (iota((ROWS, ROWS), 1) >= iota((ROWS, ROWS), 0)).astype(BF)

    def block(i, carry):
        b = 3 - i
        s = span(R, b)
        state = R.state[b]
        state_low = state.astype(BF)
        gstate = R.gstate[...]
        gstate_low = gstate.astype(BF)
        gate = R.gate[s.rows, :]
        gy = R.gleft[s.rows, 0:384] * (gate * sigmoid(gate))
        gy_low = gy.astype(BF)
        step_x = R.step_x[s.rows, :]
        tail_x = R.tail_x[s.rows, :]
        xstep = step_x * s.xs
        xstep_low = xstep.astype(BF)
        skip = R.cpar[5:6, 0:384]
        gcross = jnp.zeros((ROWS, ROWS), F32)
        tiles = []
        for pair in range(HEADS // 2):
            cols = slice(128 * pair, 128 * pair + 128)
            gp = gy_low[:, cols]
            both = []
            for e in range(2):
                h = 2 * pair + e
                both.append(mm_tn(R.weights[b, h], gp))
                gm = mm_nt(half_only(gp, e), xstep_low[:, cols])
                gcross = gcross + gm * R.mix[b, h].astype(F32)
            tiles.append(jnp.where(low, both[0], both[1]))
        inside = jnp.concatenate(tiles, axis=1)
        outflow = tail_x * mm(s.wr_low, gstate_low)
        flow_low = (R.inlet_x[s.rows, :] * gy).astype(BF)
        gcross_low = gcross.astype(BF)
        R.gmix[s.rows, 0:384] = (inside + outflow) * step_x + skip * gy
        R.gmix[s.rows, 384:512] = mm_tn(gcross_low, s.rd_low) + mm_nt(
            (tail_x * xstep).astype(BF), gstate_low
        )
        R.gmix[s.rows, 512:640] = mm(gcross_low, s.wr_low) + mm_nt(flow_low, state_low)
        ends = jnp.concatenate(
            [
                jnp.sum(gstate * state, axis=0, keepdims=True),
                jnp.sum(gy * s.xs, axis=0, keepdims=True),
                jnp.zeros((6, XW), F32),
            ],
            axis=0,
        )
        sums = sum_heads(
            jnp.concatenate(
                [
                    gy * (R.ssm[s.rows, :] - skip * s.xs),
                    inside * s.xs,
                    outflow * s.xs,
                    ends,
                ],
                axis=0,
            )
        )
        row_part = sums[0:ROWS, :]
        col_part = sums[ROWS : 2 * ROWS, :]
        through = sums[2 * ROWS : 3 * ROWS, :]
        gfactor = sums[3 * ROWS : 3 * ROWS + 1, :]
        grun = row_part - (col_part + through) * s.step
        at_end = (
            jnp.sum(through * s.step, axis=0, keepdims=True) + gfactor * R.factor[b, 0:1, :]
        )
        grun = grun + jnp.where(sub == ROWS - 1, at_end, 0.0)
        glog = mm_terms(upper, grun, 3)
        decay = -jnp.exp(R.hpar[1:2, :])
        gstep = col_part + through + glog * decay
        drive = R.pm[s.rows, :] + R.hpar[0:1, :]
        gdrive = jnp.where(lane < HEADS, gstep * sigmoid(drive), 0.0)
        R.gproj[s.rows, 640:768] = gdrive.astype(BF)
        R.hsum[0:1, :] += jnp.sum(gdrive, axis=0, keepdims=True)
        R.hsum[1:2, :] += jnp.sum(glog * decay * s.step, axis=0, keepdims=True)
        R.hsum[2:3, :] += sums[3 * ROWS + 1 : 3 * ROWS + 2, :]
        R.gstate[...] = R.factor_x[b, 0:1, :] * gstate + mm_tn(s.rd_low, flow_low)
        return carry

    lax.fori_loop(begin, end, block, 0)


def back_convolve(R):
    masks = [seg_mask(R, k) for k in range(1, 4)]
    for t in range(CW // 128):
        cols = slice(128 * t, 128 * t + 128)
        pre = R.pre[:, cols]
        raw = R.raw[:, cols].astype(F32)
        sig = sigmoid(pre)
        gpre = R.gmix[:, cols] * (sig + pre * sig * (1.0 - sig))
        graw = R.cpar[0:1, cols] * gpre
        R.small[0:1, cols] = jnp.sum(gpre * raw, axis=0, keepdims=True)
        for k in range(1, 4):
            masked = gpre * masks[k - 1]
            graw = graw + R.cpar[k : k + 1, cols] * roll(masked, LEN - k, 0)
            R.small[k : k + 1, cols] = jnp.sum(masked * roll(raw, k, 0), axis=0, keepdims=True)
        R.small[4:5, cols] = jnp.sum(gpre, axis=0, keepdims=True)
        R.gproj[:, cols] = graw.astype(BF)


def back_first(R, L):
    places = ((0, LATE), (1, LATE), (0, EARLY), (1, EARLY))
    gain = R.gain[0:1, :]
    moves = []
    for n, k in enumerate((2, 1, 3, 0)):
        b = L.around("z", k)
        rows = pl.ds(pl.multiple_of(b * ROWS, ROWS), ROWS)
        grads = R.gproj[rows, :]
        for q in range(4):
            weights = jnp.concatenate([chunk(R, core, kind, q) for core, kind in places], axis=1)
            R.gsum[:, 256 * q : 256 * q + 256] = mm_nt(grads, weights)
        R.gfirst[b] = norm_back(R.xall[b].astype(F32), gain, R.gsum[...]).astype(BF)
        for h in range(2):
            block, rows = mid_rows(L, h)

            @pl.when(block == b)
            def _():
                mine = R.gfirst[b, rows, :].astype(F32) + R.gmid[h]
                R.gfirst[b, rows, :] = mine.astype(BF)

        if k:
            moves.append(L.copy(R.gfirst.at[b], R.hrecv.at[n], L.device(z=b)))
        yield
    for one in moves:
        one.wait_recv()
    add_blocks(())(R.gfirst.at[L.z], [R.hrecv.at[n] for n in range(3)])


def put_out_grad(buf, kind, out):
    out = out.astype(BF)
    for core in range(2):
        for d in range(2):
            part = out[256 * d : 256 * d + 256, 512 * core : 512 * core + 512]
            buf[core, d, :, :, :, kind[0] : kind[0] + 512] = part.reshape(4, 4, 16, 512)


def out_grad(R):
    put_out_grad(R.dwin, OUT, mm_tn(R.left_p[...], R.gball[...].reshape(LEN, D)))


def put_grad(R, core, kind, k, value):
    lo = kind[0] + GW * (k % 2)
    R.dwin[core, k // 2, :, :, :, lo : lo + GW] = value.astype(BF).reshape(4, 4, 16, GW)


def early_grads(R):
    for k in range(4):
        out = mm_tn(R.first[:, 256 * k : 256 * k + 256], R.gproj[:, 768:1536])
        for core in range(2):
            put_grad(R, core, EARLY, k, out[:, GW * core : GW * core + GW])


def late_grads(R):
    for k in range(4):
        out = mm_tn(R.first[:, 256 * k : 256 * k + 256], R.gproj[:, 0:768])
        for core in range(2):
            put_grad(R, core, LATE, k, out[:, GW * core : GW * core + GW])


class Move:
    def __init__(self, one):
        self.one, self.came, self.went = one, False, False

    def wait_recv(self):
        if not self.came:
            self.one.wait_recv()
            self.came = True

    def wait_send(self):
        if not self.went:
            self.one.wait_send()
            self.went = True


class Links:
    def __init__(self, send, recv):
        self.send, self.recv, self.moves = send, recv, []
        self.z = lax.axis_index("ctx")
        place = lax.axis_index("fsdp")
        self.c = lax.rem(place, 2)
        self.x = lax.rem(lax.div(place, 2), 4)
        self.y = lax.div(place, 8)
        self.at = {"z": self.z, "y": self.y, "x": self.x}
        self.sibling = self.device(c=1 - self.c)

    def device(self, **moved):
        p = dict(z=self.z, y=self.y, x=self.x, c=self.c)
        p.update(moved)
        return (p["z"], (p["y"] * 4 + p["x"]) * 2 + p["c"])

    def copy(self, src, dst, device):
        k = len(self.moves)
        one = pltpu.make_async_remote_copy(
            src_ref=src,
            dst_ref=dst,
            send_sem=self.send.at[k],
            recv_sem=self.recv.at[k],
            device_id=device,
            device_id_type=MESH,
        )
        one.start()
        self.moves.append(Move(one))
        return self.moves[-1]

    def around(self, axis, k):
        return lax.rem(self.at[axis] + k, 4)

    def slab(self):
        for dz in range(4):
            for flip in range(2):
                if dz or flip:
                    yield self.around("z", dz), self.c if flip == 0 else 1 - self.c

    def greet(self):
        barrier = pltpu.get_barrier_semaphore()
        to = [self.device(z=j, c=h) for j, h in self.slab()]
        for axis in ("x", "y"):
            to += [self.device(**{axis: self.around(axis, k)}) for k in range(1, 4)]
        for one in to:
            pl.semaphore_signal(barrier, inc=1, device_id=one, device_id_type=MESH)
        return lambda: pl.semaphore_wait(barrier, len(to))

    def settle(self):
        for one in self.moves:
            one.wait_send()

    def finish(self):
        for one in self.moves:
            one.wait_recv()
            one.wait_send()


def gather(L, axis, slot, arrived=None, log=None):
    me = L.at[axis]
    moves = [
        (k, L.copy(slot(me), slot(me), L.device(**{axis: L.around(axis, k)}))) for k in (2, 1, 3)
    ]
    if log is not None:
        log.extend(one for _, one in moves)
    if arrived:
        arrived(me)
    yield
    for k, one in moves[1:] + moves[:1]:
        one.wait_recv()
        if arrived:
            arrived(L.around(axis, 4 - k))


def reduce(L, axis, src, bufs, add):
    moves = []
    for buf, k in zip(bufs, (2, 1, 3)):
        j = L.around(axis, k)
        moves.append(L.copy(src(j), buf, L.device(**{axis: j})))
    yield
    for one in moves:
        one.wait_recv()
    add(src(L.at[axis]), bufs)


def add_blocks(lead):
    count = int(np.prod(lead)) if lead else 1

    def add(dst, srcs):
        def body(n, carry):
            where = []
            for size in reversed(lead):
                where.append(lax.rem(n, size))
                n = lax.div(n, size)
            where = tuple(reversed(where)) + (slice(None), slice(None))
            total = dst[where].astype(F32)
            for one in srcs:
                total = total + one[where].astype(F32)
            dst[where] = total.astype(BF)
            return carry

        lax.fori_loop(0, count, body, 0)

    return add


def columns(ref, lead, lo, width):
    return ref.at[(slice(None),) * (lead + 1) + (pl.ds(lo, width),)]


def step(*gens):
    for g in gens:
        next(g, None)


def together(*gens):
    gens = list(gens)
    while gens:
        alive = []
        for g in gens:
            try:
                next(g)
                alive.append(g)
            except StopIteration:
                pass
        gens = alive
        if gens:
            yield


def drain(*gens):
    for _ in together(*gens):
        pass


def mixer_slot(L, buf, sub, stage, lo, width):
    ref = buf.at[L.c, sub]
    axis = ("xy" if sub == 0 else "yx")[stage]

    def slot(j):
        if stage == 0:
            block = ref.at[L.y, j] if axis == "x" else ref.at[j, L.x]
        else:
            block = ref.at[j] if axis == "y" else ref.at[:, j]
        return columns(block, stage, lo, width)

    return axis, slot


def gather_near(L, R, sub, lo, width, log=None):
    axis, slot = mixer_slot(L, R.win, sub, 0, lo, width)
    return gather(L, axis, slot, None, log)


def gather_far(L, R, sub, lo, width, log=None):
    axis, slot = mixer_slot(L, R.win, sub, 1, lo, width)
    sent = []

    def arrived(j):
        sent.append(L.copy(slot(j), slot(j), L.sibling))

    yield from gather(L, axis, slot, arrived, log)
    if log is not None:
        log.extend(sent)
    yield
    for one in sent:
        one.wait_recv()


def gather_mixer(L, R, sub, lo, width, log=None):
    yield from gather_near(L, R, sub, lo, width, log)
    yield from gather_far(L, R, sub, lo, width, log)


def reduce_mixer(L, R, buf, lo, width):
    moves = []
    for sub in range(2):
        theirs = columns(buf.at[1 - L.c, sub], 2, lo, width)
        moves.append(L.copy(theirs, columns(R.wsib.at[sub], 2, lo, width), L.sibling))
    yield
    gens = []
    for sub in range(2):
        moves[sub].wait_recv()
        mine = columns(buf.at[L.c, sub], 2, lo, width)
        add_blocks((4, 4))(mine, [columns(R.wsib.at[sub], 2, lo, width)])
        gens.append(reduce_chips(L, R, buf, sub, lo, width))
        next(gens[-1])
    yield
    yield from together(*gens)


def reduce_chips(L, R, buf, sub, lo, width):
    for stage in (1, 0):
        axis, slot = mixer_slot(L, buf, sub, stage, lo, width)
        bufs = [columns(one.at[sub], stage, lo, width) for one in R.mbufs[stage]]
        yield from reduce(L, axis, slot, bufs, add_blocks((4,) * stage))


def deal_rows(L, buf, kind, width, fin, rfin, place):
    for sub in range(2):
        for k in range(2):
            lo = kind[0] + width * k
            both = buf[L.c, sub, L.y, L.x, :, lo : lo + width].astype(F32)
            for core in range(2):
                fin[2 * sub + k, core, :, place : place + width] = both[8 * core : 8 * core + 8, :]
    cols = pl.ds(place, width)
    moves = [
        L.copy(fin.at[j, h, :, cols], rfin.at[L.z, L.c, :, cols], L.device(z=j, c=h))
        for j, h in L.slab()
    ]
    rfin[L.z, L.c, :, cols] = fin[L.z, L.c, :, cols]
    return moves


def deal_halves(L, buf, kind, fin, rfin):
    for d in range(2):
        fin[d] = buf[L.c, d, L.y, L.x, :, kind[0] : kind[0] + 512].astype(F32)
    return L.copy(fin.at[1 - L.c], rfin, L.sibling)


def reduce_late(L, R):
    yield from reduce_mixer(L, R, R.dwin, *LATE)
    moves = deal_rows(L, R.dwin, LATE, GW, R.fin, R.rfin, 0)
    yield
    for one in moves:
        one.wait_recv()


def reduce_early(L, R):
    yield from reduce_mixer(L, R, R.dwin, EARLY[0], EARLY[1] + OUT[1])
    moves = deal_rows(L, R.dwin, EARLY, GW, R.fin, R.rfin, GW)
    moves.append(deal_halves(L, R.dwin, OUT, R.ofin, R.orfin))
    yield
    for one in moves:
        one.wait_recv()
    lo, hi = in_core_order(L, R.ofin[L.c], R.orfin[...])
    R.o_mo[:, 0:512] = lo[0:12, :]
    R.o_mo[:, 512:1024] = hi[0:12, :]
    R.o_ao[:, 0:512] = lo[12:16, :]
    R.o_ao[:, 512:1024] = hi[12:16, :]
    R.send_out("o_mo", "o_ao")


def reduce_ffn(L, R):
    yield from reduce_mixer(L, R, R.win, *FFN)
    moves = deal_rows(L, R.win, FIN, FW, R.ffin, R.frfin, 0)
    moves.append(deal_halves(L, R.win, FOUT, R.dfin, R.drfin))
    yield
    for one in moves:
        one.wait_recv()
    lo, hi = in_core_order(L, R.dfin[L.c], R.drfin[...])
    R.o_fd[:, 0:512] = lo
    R.o_fd[:, 512:1024] = hi
    turn = (iota((FW, FW), 1) == deal(iota((FW, 1), 0))).astype(BF)
    rows = [R.frfin[j, core] for core in range(2) for j in range(4)]
    out = mm_terms(jnp.concatenate(rows, axis=0), turn, 3)
    for j in range(4):
        R.o_fg[:, FW * j : FW * j + FW] = out[8 * j : 8 * j + 8, :]
        R.o_fu[:, FW * j : FW * j + FW] = out[32 + 8 * j : 40 + 8 * j, :]
    R.gcol[0] = gain_column([(R.w_fg, R.o_fg), (R.w_fu, R.o_fu)], R.gain_mid)
    R.send_out("o_fd", "o_fg", "o_fu")


def reduce_blocks(L, ref, recv):
    return reduce(L, "z", lambda j: ref.at[j], [recv.at[n] for n in range(3)], add_blocks(()))


def gather_blocks(L, ref):
    return gather(L, "z", lambda j: ref.at[j])


def reduce_small(L, R):
    for part in range(3):
        R.small[5:6, 128 * part : 128 * part + 128] = R.hsum[part : part + 1, :]
    R.smc[L.c] = R.small[...]
    move = L.copy(R.smc.at[L.c], R.smc.at[L.c], L.sibling)
    yield
    move.wait_recv()
    R.smx[L.x] = R.smc[0] + R.smc[1]
    yield from gather(L, "x", lambda j: R.smx.at[j])
    R.smy[L.y] = (R.smx[0] + R.smx[1]) + (R.smx[2] + R.smx[3])
    yield from gather(L, "y", lambda j: R.smy.at[j])
    R.smz[L.z] = (R.smy[0] + R.smy[1]) + (R.smy[2] + R.smy[3])
    yield from gather(L, "z", lambda j: R.smz.at[j])
    for j in range(4):
        R.o_conv[:, 384 * j : 384 * j + 384] = R.smz[j, :, 0:384]
    total = (R.smz[0] + R.smz[1]) + (R.smz[2] + R.smz[3])
    R.o_conv[:, 1536:1792] = total[:, 384:640]
    lane = iota((8, 128), 1)
    for part in range(3):
        heads = jnp.zeros((8, 128), F32)
        for j in range(4):
            one = jnp.where(lane < HEADS, R.smz[j, :, 128 * part : 128 * part + 128], 0.0)
            heads = heads + (one if j == 0 else roll(one, HEADS * j, 1))
        R.o_head[part : part + 1, :] = heads[5:6, :]


def setup(L, R):
    lane = iota((1, 128), 1)
    first = HEADS * L.z
    for row, ref in enumerate((R.step_bias, R.decay_log)):
        total = jnp.zeros((1, 128), F32)
        for h in range(HEADS):
            total = jnp.where(lane == h, ref[first + h], total)
        R.hpar[row : row + 1, :] = total
    cols = pl.ds(pl.multiple_of(XW * L.z, 128), XW)
    R.cpar[0:4, 0:384] = R.taps[:, cols]
    R.cpar[0:4, 384:640] = R.taps[:, 1536:1792]
    R.cpar[4:5, 0:384] = R.bias[cols].reshape(1, 384)
    R.cpar[4:5, 384:640] = R.bias[1536:1792].reshape(1, 256)
    lane = iota((1, XW), 1) >> 6
    total = jnp.zeros((1, XW), F32)
    for h in range(HEADS):
        total = jnp.where(lane == h, R.skip_gain[first + h], total)
    R.cpar[5:6, 0:384] = total
    seg = R.seg[...].astype(F32)
    R.segr[0:1, :] = seg
    for b in range(4):
        row = seg[:, b * ROWS : b * ROWS + ROWS]
        R.segc[b * ROWS : b * ROWS + ROWS, :] = jnp.broadcast_to(row, (ROWS, ROWS)).T


def pack_weights(L, R):
    shape8 = (8, 128)
    low = lane_low(shape8)
    lane = iota(shape8, 1)
    sub = iota(shape8, 0)
    k, v = R.w_k[...], R.w_v[...]
    k_up, v_up = roll(k, 64, 1), roll(v, 64, 1)
    R.misc[...] = jnp.zeros(shape8, F32)
    R.misc[:, 0:24] = R.w_step[...]
    misc = R.misc[...]
    for row in range(8):
        misc = jnp.where((lane == 24) & (sub == row), R.gain_in[row], misc)
        misc = jnp.where((lane == 25) & (sub == row), R.gain_mid[row], misc)
    for j in range(4):
        R.pack[j, 0, :, 0:384] = R.w_min[:, 1536 + 384 * j : 1920 + 384 * j]
        R.pack[j, 0, :, 384:768] = R.w_min[:, 384 * j : 384 * j + 384]
        R.pack[j, 1, :, 0:256] = R.w_bc[...]
        mine = misc if j == 0 else roll(misc, 128 - HEADS * j, 1)
        R.pack[j, 1, :, 256:384] = jnp.where(
            lane < HEADS, mine, jnp.where((lane >= 24) & (lane < 26), misc, 0.0)
        )
        R.pack[j, 1, :, 384:512] = R.w_q[:, 128 * j : 128 * j + 128]
        R.pack[j, 1, :, 512:640] = jnp.where(low, k, v_up) if j < 2 else jnp.where(low, k_up, v)
        R.pack[j, 1, :, 640:768] = jnp.zeros(shape8, F32)
    for h in range(2):
        R.opack[h, 0:12, :] = R.w_mo[:, 512 * h : 512 * h + 512]
        R.opack[h, 12:16, :] = R.w_ao[:, 512 * h : 512 * h + 512]


def deal(n):
    return 32 * ((n & 255) >> 4) + 16 * (n >> 8) + (n & 15)


def pack_ffn(L, R):
    turn = (iota((FW, FW), 0) == deal(iota((1, FW), 1))).astype(BF)
    rows = [ref[:, FW * j : FW * j + FW] for ref in (R.w_fg, R.w_fu) for j in range(4)]
    out = mm(jnp.concatenate(rows, axis=0).astype(BF), turn)
    for j in range(4):
        R.fpack[j, 0] = out[8 * j : 8 * j + 8, :]
        R.fpack[j, 1] = out[32 + 8 * j : 40 + 8 * j, :]
    for h in range(2):
        R.dpack[h] = R.w_fd[:, 512 * h : 512 * h + 512]


def gain_column(pairs, scalars):
    total = jnp.zeros((8, 1), F32)
    for weight, grad in pairs:
        weight = weight[...].astype(BF).astype(F32)
        total = total + jnp.sum(weight * grad[...], axis=1, keepdims=True)
    sub = iota((8, 128), 0)
    gain = jnp.ones((8, 128), F32)
    for row in range(8):
        gain = jnp.where(sub == row, scalars[row], gain)
    return total / gain.astype(BF).astype(F32)


def unpack_early(R):
    low = lane_low((8, 128))
    for j in range(4):
        R.o_min[:, 384 * j : 384 * j + 384] = R.rfin[j, 0, :, 384:768]
        R.o_q[:, 128 * j : 128 * j + 128] = R.rfin[j, 1, :, 384:512]
    kv0 = R.rfin[0, 1, :, 512:640] + R.rfin[1, 1, :, 512:640]
    kv1 = R.rfin[2, 1, :, 512:640] + R.rfin[3, 1, :, 512:640]
    R.o_k[...] = jnp.where(low, kv0, roll(kv1, 64, 1))
    R.o_v[...] = jnp.where(low, roll(kv0, 64, 1), kv1)
    pairs = [(R.w_min.at[:, 0:1536], R.o_min.at[:, 0:1536])]
    pairs += [(R.w_q, R.o_q), (R.w_k, R.o_k), (R.w_v, R.o_v)]
    R.gcol[1] = gain_column(pairs, R.gain_in)
    R.send_out("o_q", "o_k", "o_v")


def unpack_late(R):
    lane = iota((8, 128), 1)
    misc = jnp.zeros((8, 128), F32)
    for j in range(4):
        R.o_min[:, 1536 + 384 * j : 1920 + 384 * j] = R.rfin[j, 0, :, 0:384]
        own = jnp.where(lane < HEADS, R.rfin[j, 1, :, 256:384], 0.0)
        misc = misc + (own if j == 0 else roll(own, HEADS * j, 1))
    R.o_misc[...] = misc
    R.o_bc[...] = (R.rfin[0, 1, :, 0:256] + R.rfin[1, 1, :, 0:256]) + (
        R.rfin[2, 1, :, 0:256] + R.rfin[3, 1, :, 0:256]
    )
    R.send_out("o_min", "o_bc", "o_misc")
    pairs = [(R.w_min.at[:, 1536:3072], R.o_min.at[:, 1536:3072])]
    pairs += [(R.w_bc, R.o_bc), (R.w_step, R.o_misc.at[:, 0:24])]
    first = R.gcol[1] + gain_column(pairs, R.gain_in)
    both = jnp.where(iota((8, 128), 1) == 0, first, R.gcol[0])
    turned = jnp.concatenate([both, jnp.zeros((120, 128), F32)], axis=0).T
    R.o_head[3:5, :] = turned[0:2, :]
    R.send_out("o_head")


def in_core_order(L, mine, other):
    first = L.c == 0
    return jnp.where(first, mine, other), jnp.where(first, other, mine)


def own_rows(L, R, exch, kinds, width):
    for sub in range(2):
        for k in range(2):
            both = jnp.concatenate([exch[2 * sub + k, d] for d in range(2)], axis=0).astype(BF)
            for n, kind in enumerate(kinds):
                lo = kind[0] + width * k
                R.win[L.c, sub, L.y, L.x, :, lo : lo + width] = both[:, width * n : width * n + width]


def own_halves(L, R, pack, other, kind):
    for d, part in enumerate(in_core_order(L, pack[L.c], other[...])):
        R.win[L.c, d, L.y, L.x, :, kind[0] : kind[0] + 512] = part.astype(BF)


def to_slab(L, pack, exch):
    moves = [L.copy(pack.at[j, h], exch.at[L.z, L.c], L.device(z=j, c=h)) for j, h in L.slab()]
    exch[L.z, L.c] = pack[L.z, L.c]
    return moves


def come(*moves):
    for one in moves:
        one.wait_recv()


def middle_rows(L, R, h):
    block, rows = mid_rows(L, h)
    total = R.xall[block, rows, :].astype(F32) + R.branch[h, L.z].astype(F32)
    for n in range(3):
        total = total + R.zrecv[h, n].astype(F32)
    R.middle[h] = total
    inv = lax.rsqrt(jnp.mean(total * total, axis=-1, keepdims=True) + EPS)
    R.secall[h, L.z] = (total * inv * R.gain[1:2, :]).astype(BF)


def back_middle(L, R, h):
    block, rows = mid_rows(L, h)
    total = R.gsec[h, L.z].astype(F32)
    for n in range(3):
        total = total + R.zrecv[2 + h, n].astype(F32)
    gmid = norm_back(R.middle[h], R.gain[1:2, :], total)
    gmid = gmid + R.cotall[block, rows, :].astype(F32)
    R.gmid[h] = gmid
    R.gball[h, L.z] = gmid.astype(BF)


def keep(dst, srcs):
    pass


def to_owner(L, R, ref, n):
    return reduce(L, "z", lambda j: ref.at[j], [R.zrecv.at[n, k] for k in range(3)], keep)


def kernel(R):
    L = Links(R.send, R.recv)
    greeted = L.greet()
    R.await_in(*WEIGHTS_IN)
    pack_weights(L, R)
    R.await_in("tok", "cot")
    R.xall[L.z] = R.tok[...]
    R.cotall[L.z] = R.cot[...]
    greeted()

    moves = to_slab(L, R.pack, R.exch)
    wo = L.copy(R.opack.at[1 - L.c], R.exo, L.sibling)
    R.await_in("seg", "taps", "bias")
    setup(L, R)
    R.await_in("w_fg", "w_fu", "w_fd")
    pack_ffn(L, R)
    come(wo)
    own_halves(L, R, R.opack, R.exo, OUT)
    come(*moves)
    own_rows(L, R, R.exch, (LATE, EARLY), GW)
    near = together(*[gather_near(L, R, sub, 0, FIN[0]) for sub in range(2)])
    step(near)
    xgen = gather_blocks(L, R.xall)
    step(xgen)
    fmoves = to_slab(L, R.fpack, R.fexch)
    do = L.copy(R.dpack.at[1 - L.c], R.dexo, L.sibling)
    drain(near)
    late, early, out = [
        together(*[gather_far(L, R, sub, *kind) for sub in range(2)])
        for kind in (LATE, EARLY, OUT)
    ]
    step(late)
    step(early)
    step(out)
    R.small[...] = jnp.zeros((8, CW), F32)
    R.gk[...] = jnp.zeros((LEN, 128), F32)
    R.gv[...] = jnp.zeros((LEN, 128), F32)
    R.state[0] = jnp.zeros((128, XW), F32)
    R.gstate[...] = jnp.zeros((128, XW), F32)
    R.hsum[...] = jnp.zeros((8, 128), F32)
    step(late)
    drain(late)
    gains(R)
    drain(xgen)
    cgen = gather_blocks(L, R.cotall)
    step(cgen)
    norm_first(R)
    project_late(R)
    step(early)
    convolve(R)
    step(out)
    come(do, *fmoves)
    own_rows(L, R, R.fexch, (FIN,), FW)
    own_halves(L, R, R.dpack, R.dexo, FOUT)
    fsent = []
    fgen = together(*[gather_mixer(L, R, sub, *FFN, fsent) for sub in range(2)])
    step(fgen)
    steps(R)
    recurrence(R, 0, 2)
    drain(early)
    project_early(R)
    R.await_in("cosr", "sinr", "perm5")
    rotated(R)
    attend(R, 0, 2)
    step(fgen)
    drain(out)
    out_project(R, 0)
    branch = [to_owner(L, R, R.branch.at[h], h) for h in range(2)]
    step(branch[0])
    recurrence(R, 2, 4)
    attend(R, 2, 4)
    out_project(R, 1)
    step(branch[1])
    second = [gather_blocks(L, R.secall.at[h]) for h in range(2)]
    for h in range(2):
        drain(branch[h])
        middle_rows(L, R, h)
        step(second[h])
        step(fgen)
    drain(cgen, fgen)
    gsec = [to_owner(L, R, R.gsec.at[h], 2 + h) for h in range(2)]
    for h in range(2):
        drain(second[h])
        ffn(R, h)
        step(gsec[h])
    gball = [gather_blocks(L, R.gball.at[h]) for h in range(2)]
    for one in fsent:
        one.wait_send()
    ffn_out(R, L)
    drain(gsec[0])
    back_middle(L, R, 0)
    step(gball[0])
    ffn_grads(R)
    wgen = reduce_ffn(L, R)
    step(wgen)
    drain(gsec[1])
    back_middle(L, R, 1)
    step(gball[1])
    step(wgen)
    drain(gball[0])
    back_out(R, 0)
    back_attend(R, 0, 2)
    drain(gball[1])
    fout = reduce_blocks(L, R.fout, R.frecv)
    step(fout)
    back_out(R, 1)
    back_gate(R)
    back_attend(R, 2, 4)
    back_rotated(R)
    step(wgen)
    out_grad(R)
    early_grads(R)
    egen = reduce_early(L, R)
    step(egen)
    back_recurrence(R, 0, 2)
    step(egen)
    step(wgen)
    back_recurrence(R, 2, 4)
    back_convolve(R)
    late_grads(R)
    lgen = reduce_late(L, R)
    step(lgen)
    mgen = reduce_small(L, R)
    step(mgen)
    hgen = back_first(R, L)
    step(hgen)
    step(lgen, mgen)
    step(hgen)
    step(hgen)
    step(hgen)
    step(mgen)
    step(egen)
    step(lgen)
    step(mgen)
    step(egen)
    step(lgen)
    drain(wgen, fout)
    R.o_out[...] = R.fout[L.z]
    R.send_out("o_out")
    drain(egen)
    unpack_early(R)
    drain(mgen)
    R.send_out("o_conv")
    drain(hgen)
    R.o_tok[...] = R.gfirst[L.z]
    R.send_out("o_tok")
    drain(lgen)
    unpack_late(R)
    L.finish()
    R.finish_out()


INS = dict(
    w_min=((8, 3072), F32),
    w_bc=((8, 256), F32),
    w_step=((8, 24), F32),
    w_q=((8, 512), F32),
    w_k=((8, 128), F32),
    w_v=((8, 128), F32),
    w_mo=((12, D), F32),
    w_ao=((4, D), F32),
    tok=((ROWS, D), BF),
    cot=((ROWS, D), BF),
    w_fg=((8, 2048), F32),
    w_fu=((8, 2048), F32),
    w_fd=((16, D), F32),
    seg=((1, LEN), jnp.int32),
    taps=((4, 1792), F32),
    bias=((1792,), F32),
    cosr=((LEN, 128), F32),
    sinr=((LEN, 128), F32),
    perm5=((512, 512), BF),
)
WEIGHTS_IN = list(INS)[:8]
SCALARS = ("gain_in", "gain_mid", "step_bias", "decay_log", "skip_gain")
OUTS = dict(
    o_out=((ROWS, D), BF),
    o_tok=((ROWS, D), BF),
    o_min=((8, 3072), F32),
    o_bc=((8, 256), F32),
    o_misc=((8, 128), F32),
    o_q=((8, 512), F32),
    o_k=((8, 128), F32),
    o_v=((8, 128), F32),
    o_mo=((12, D), F32),
    o_ao=((4, D), F32),
    o_fg=((8, 2048), F32),
    o_fu=((8, 2048), F32),
    o_fd=((16, D), F32),
    o_conv=((8, 1792), F32),
    o_head=((8, 128), F32),
)
SCRATCH = dict(
    xall=((4, ROWS, D), BF),
    segc=((LEN, 128), F32),
    segr=((8, LEN), F32),
    cpar=((8, CW), F32),
    hpar=((8, 128), F32),
    misc=((8, 128), F32),
    pack=((4, 2, 8, 768), F32),
    exch=((4, 2, 8, 768), F32),
    opack=((2, 16, 512), F32),
    exo=((16, 512), F32),
    fpack=((4, 2, 8, FW), F32),
    fexch=((4, 2, 8, FW), F32),
    dpack=((2, 16, 512), F32),
    dexo=((16, 512), F32),
    win=((2, 2, 4, 4, 16, PK), BF),
    dwin=((2, 2, 4, 4, 16, FIN[0]), BF),
    cotall=((4, ROWS, D), BF),
    secall=((2, 4, 64, D), BF),
    hid=((LEN, FW), BF),
    gab=((LEN, 2 * FW), BF),
    gsec=((2, 4, 64, D), BF),
    fout=((4, ROWS, D), BF),
    gain=((8, D), F32),
    gcol=((2, 8, 128), F32),
    first=((LEN, D), BF),
    gate=((LEN, XW), F32),
    raw=((LEN, CW), BF),
    pq=((LEN, 128), F32),
    pkv=((LEN, 128), F32),
    pm=((LEN, 128), F32),
    pre=((LEN, CW), F32),
    mixed=((LEN, CW), F32),
    step=((LEN, 128), F32),
    run=((LEN, 128), F32),
    state=((5, 128, XW), F32),
    ssm=((LEN, XW), F32),
    q=((LEN, 128), BF),
    kk=((LEN, 128), BF),
    vv=((LEN, 128), BF),
    probs=((2, LEN, LEN), BF),
    left=((LEN, 512), BF),
    left_p=((LEN, 512), BF),
    branch=((2, 4, 64, D), BF),
    zrecv=((4, 3, 64, D), BF),
    frecv=((3, ROWS, D), BF),
    hrecv=((3, ROWS, D), BF),
    middle=((2, 64, D), F32),
    gmid=((2, 64, D), F32),
    gsum=((ROWS, D), F32),
    gball=((2, 4, 64, D), BF),
    gleft=((LEN, 512), F32),
    gq=((LEN, 128), F32),
    gk=((LEN, 128), F32),
    gv=((LEN, 128), F32),
    gstate=((128, XW), F32),
    hsum=((8, 128), F32),
    gmix=((LEN, CW), F32),
    gproj=((LEN, 4 * GW), BF),
    small=((8, CW), F32),
    factor=((4, 8, 128), F32),
    inlet_x=((LEN, XW), F32),
    tail_x=((LEN, XW), F32),
    factor_x=((4, 8, XW), F32),
    step_x=((LEN, XW), F32),
    mix=((4, HEADS, ROWS, ROWS), BF),
    weights=((4, HEADS, ROWS, ROWS), BF),
    gfirst=((4, ROWS, D), BF),
    wsib=((2, 4, 4, 16, PK), BF),
    smc=((2, 8, CW), F32),
    smx=((4, 8, CW), F32),
    smy=((4, 8, CW), F32),
    smz=((4, 8, CW), F32),
    fin=((4, 2, 8, 768), F32),
    rfin=((4, 2, 8, 768), F32),
    ofin=((2, 16, 512), F32),
    orfin=((16, 512), F32),
    ffin=((4, 2, 8, FW), F32),
    frfin=((4, 2, 8, FW), F32),
    dfin=((2, 16, 512), F32),
    drfin=((16, 512), F32),
)
COPIES = 250


def ring_buffers(parts, width, stages):
    shapes = {}
    for stage in range(stages):
        for n in range(3):
            shapes[(stage, n)] = ((parts,) + (4,) * stage + (16, width), BF)
    return shapes


MBUFS = ring_buffers(2, PK, 2)


def entry(*refs):
    refs = list(refs)
    take = lambda names: [(name, refs.pop(0)) for name in names]
    given, scalars, results = dict(take(INS)), take(SCALARS), dict(take(OUTS))
    inside = take(INS)
    R = types.SimpleNamespace(**dict(scalars + inside + take(OUTS) + take(SCRATCH)))
    bufs = dict(take(MBUFS))
    R.mbufs = [[bufs[key] for key in MBUFS if key[0] == stage] for stage in range(2)]
    R.send, R.recv, came, left = refs
    loads = {}
    for n, name in enumerate(INS):
        loads[name] = pltpu.make_async_copy(given[name], getattr(R, name), came.at[n])
        loads[name].start()
    stores = []

    def await_in(*names):
        for name in names:
            loads[name].wait()

    def send_out(*names):
        for name in names:
            n = len(stores)
            stores.append(pltpu.make_async_copy(getattr(R, name), results[name], left.at[n]))
            stores[-1].start()

    def finish_out():
        for one in stores:
            one.wait()

    R.await_in, R.send_out, R.finish_out = await_in, send_out, finish_out
    kernel(R)


def layer(*args):
    anywhere = pl.BlockSpec(memory_space=pl.ANY)
    smem = pl.BlockSpec(memory_space=pltpu.SMEM)
    shapes = [*INS.values(), *OUTS.values(), *SCRATCH.values(), *MBUFS.values()]
    scratch = [pltpu.VMEM(shape, kind) for shape, kind in shapes]
    scratch += [pltpu.SemaphoreType.DMA((n,)) for n in (COPIES, COPIES, len(INS), len(OUTS))]
    return pl.pallas_call(
        entry,
        out_shape=[jax.ShapeDtypeStruct(shape, kind) for shape, kind in OUTS.values()],
        in_specs=[anywhere] * len(INS) + [smem] * len(SCALARS),
        out_specs=[anywhere] * len(OUTS),
        scratch_shapes=scratch,
        compiler_params=pltpu.CompilerParams(
            collective_id=0, has_side_effects=True, vmem_limit_bytes=63 * 2**20
        ),
    )(*args)


SAME = [name for name in OUTS if name not in ("o_misc", "o_conv", "o_head")]
RESULTS = {name: OUTS[name] for name in SAME}
RESULTS.update(
    step=((8, 24), F32),
    taps=((4, 1792), F32),
    bias=((1792,), F32),
    gain_in=((8,), F32),
    gain_mid=((8,), F32),
    step_bias=((24,), F32),
    decay_log=((24,), F32),
    skip_gain=((24,), F32),
)


def deliver_kernel(*refs):
    given = dict(zip(OUTS, refs))
    result = dict(zip(RESULTS, refs[len(OUTS) :]))
    for name in SAME:
        result[name][...] = given[name][...]
    result["step"][...] = given["o_misc"][:, 0:24]
    result["taps"][...] = given["o_conv"][0:4, :]
    result["bias"][...] = given["o_conv"][4, :]
    head = given["o_head"]
    for row, name in enumerate(("step_bias", "decay_log", "skip_gain")):
        result[name][...] = head[row, 0:24]
    result["gain_in"][...] = head[3, 0:8]
    result["gain_mid"][...] = head[4, 0:8]


def deliver(outs):
    vmem = pl.BlockSpec(memory_space=pltpu.VMEM)
    results = pl.pallas_call(
        deliver_kernel,
        out_shape=[jax.ShapeDtypeStruct(shape, kind) for shape, kind in RESULTS.values()],
        in_specs=[vmem] * len(OUTS),
        out_specs=[vmem] * len(RESULTS),
    )(*outs)
    return dict(zip(RESULTS, results))


def rotary_tables():
    lane = np.arange(128)
    power = (-2.0 * (lane % 32).astype(np.float32) / np.float32(64)).astype(np.float32)
    frequency = np.power(np.float32(ROPE), power).astype(np.float32)
    angles = np.arange(LEN, dtype=np.float32)[:, None] * frequency[None, :]
    sign = np.where(lane % 64 < 32, -1.0, 1.0)
    cosine = np.cos(angles.astype(np.float64)).astype(np.float32)
    sine = (np.sin(angles.astype(np.float64)) * sign).astype(np.float32)
    return cosine, sine


def out_order():
    n = np.arange(512)
    device = np.where(n < 384, n // 12, (n - 384) // 4)
    row = np.where(n < 384, n % 12, 12 + (n - 384) % 4)
    to = (device % 2) * 256 + (device // 2) * 16 + row
    table = np.zeros((512, 512), np.float32)
    table[n, to] = 1.0
    return table


def shards(
    tokens,
    segments,
    cotangent,
    gain_in,
    mamba_in,
    mamba_bc,
    mamba_step,
    in_query,
    in_key,
    in_value,
    mamba_out,
    attn_out,
    gain_mid,
    ffn_gate,
    ffn_up,
    ffn_down,
    conv_taps,
    conv_bias,
    step_bias,
    decay_log,
    skip_gain,
):
    cosine, sine = rotary_tables()
    outs = layer(
        mamba_in,
        mamba_bc,
        mamba_step,
        in_query,
        in_key,
        in_value,
        mamba_out,
        attn_out,
        tokens[0],
        cotangent[0],
        ffn_gate,
        ffn_up,
        ffn_down,
        segments,
        conv_taps,
        conv_bias,
        jnp.asarray(cosine),
        jnp.asarray(sine),
        jnp.asarray(out_order(), BF),
        gain_in,
        gain_mid,
        step_bias,
        decay_log,
        skip_gain,
    )
    r = deliver(outs)
    return (
        r["o_out"][None],
        r["o_tok"][None],
        r["gain_in"],
        r["o_min"],
        r["o_bc"],
        r["step"],
        r["o_q"],
        r["o_k"],
        r["o_v"],
        r["o_mo"],
        r["o_ao"],
        r["gain_mid"],
        r["o_fg"],
        r["o_fu"],
        r["o_fd"],
        r["taps"],
        r["bias"],
        r["step_bias"],
        r["decay_log"],
        r["skip_gain"],
    )


def solution(mesh):
    one = P(("ctx", "fsdp"))
    rows = P(("ctx", "fsdp"), None)
    block = P("fsdp", "ctx", None)
    return jax.shard_map(
        shards,
        mesh=mesh,
        in_specs=(block, P("fsdp", None), block, one)
        + (rows,) * 8
        + (one,)
        + (rows,) * 3
        + (P(),) * 5,
        out_specs=(block, block, one) + (rows,) * 8 + (one,) + (rows,) * 3 + (P(),) * 5,
        check_vma=False,
    )
```

```python
import types

import jax
import jax.numpy as jnp
import numpy as np
from jax import lax
from jax.experimental import pallas as pl
from jax.experimental.pallas import tpu as pltpu
from jax.sharding import PartitionSpec as P

BF = jnp.bfloat16
F32 = jnp.float32
MESH = pl.DeviceIdType.MESH
EPS = 1e-06
ROPE = 100000000000.0

D = 1024
LEN = 512
ROWS = 128
HEADS = 6
XW = 384
CW = 640
GW = 384
PK = 3584
FW = 512


def mm(a, b):
    return lax.dot_general(a, b, (((1,), (0,)), ((), ())), preferred_element_type=F32)


def mm_nt(a, b):
    return lax.dot_general(a, b, (((1,), (1,)), ((), ())), preferred_element_type=F32)


def mm_tn(a, b):
    return lax.dot_general(a, b, (((0,), (0,)), ((), ())), preferred_element_type=F32)


def iota(shape, dim):
    return lax.broadcasted_iota(jnp.int32, shape, dim)


def lane_low(shape):
    return iota(shape, 1) & 64 == 0


def roll(v, shift, axis):
    size = v.shape[axis]
    return pltpu.roll(v, shift % size, axis)


def swap_halves(v):
    lanes = v.shape[1]
    first = iota(v.shape, 1) & 32 == 0
    return jnp.where(first, roll(v, lanes - 32, 1), roll(v, 32, 1))


def sigmoid(v):
    return 1.0 / (1.0 + jnp.exp(-v))


def softplus(v):
    return jnp.maximum(v, 0.0) + jnp.log1p(jnp.exp(-jnp.abs(v)))


def spread_heads(v):
    rows = v.shape[0]
    low = lane_low((rows, 128))
    tiles = []
    for pair in range(HEADS // 2):
        a = jnp.broadcast_to(v[:, 2 * pair : 2 * pair + 1], (rows, 128))
        b = jnp.broadcast_to(v[:, 2 * pair + 1 : 2 * pair + 2], (rows, 128))
        tiles.append(jnp.where(low, a, b))
    return jnp.concatenate(tiles, axis=1)


def mm_terms(a, b, count):
    side = 0 if a.dtype == F32 else 1
    rest, total = (a, b)[side], None
    for _ in range(count):
        term = rest.astype(BF)
        rest = rest - term.astype(F32)
        one = mm(term, b) if side == 0 else mm(a, term)
        total = one if total is None else total + one
    return total


def sum_heads(v):
    pick = (iota((XW, 128), 0) >> 6 == iota((XW, 128), 1)).astype(BF)
    return mm_terms(v, pick, 2)


def lower_ones():
    return (iota((ROWS, ROWS), 1) <= iota((ROWS, ROWS), 0)).astype(BF)


LATE, EARLY, OUT = (0, 2 * GW), (2 * GW, 2 * GW), (4 * GW, 512)
FIN, FOUT = (2048, 2 * FW), (2048 + 2 * FW, 512)
FFN = (FIN[0], FIN[1] + FOUT[1])


def chunk(R, core, kind, k, lo=0, width=GW):
    v = R.win[core, k // 2, :, :, :, pl.ds(kind[0] + GW * (k % 2) + lo, width)]
    return v.reshape(256, width)


def group_weight(R, core, kind):
    return jnp.concatenate([chunk(R, core, kind, k) for k in range(4)], axis=0)


def out_weight(R, kind=OUT):
    parts = []
    for core in range(2):
        rows = [R.win[core, d, :, :, :, pl.ds(kind[0], 512)].reshape(256, 512) for d in range(2)]
        parts.append(jnp.concatenate(rows, axis=0))
    return jnp.concatenate(parts, axis=1)


def seg_mask(R, k):
    seg = R.segc[...]
    return jnp.where(
        (seg == roll(seg, k, 0)) & (iota((LEN, 128), 0) >= k), 1.0, 0.0
    ).astype(F32)


def gains(R):
    pick = (iota((8, 128), 1) == iota((8, 128), 0) + 24).astype(BF)
    for k in range(4):
        R.gain[:, pl.ds(256 * k, 256)] = mm_nt(pick, chunk(R, 1, LATE, k, 256, 128))


def norm_first(R):
    gain = R.gain[0:1, :]

    def block(b, carry):
        x = R.xall[b].astype(F32)
        inv = lax.rsqrt(jnp.mean(x * x, axis=-1, keepdims=True) + EPS)
        R.first[pl.ds(pl.multiple_of(b * ROWS, ROWS), ROWS), :] = (x * inv * gain).astype(BF)
        return carry

    lax.fori_loop(0, 4, block, 0)


def project_late(R):
    first = R.first[...]
    out = mm(first, group_weight(R, 0, LATE))
    R.raw[:, 0:384] = out.astype(BF)
    out = mm(first, group_weight(R, 1, LATE))
    R.raw[:, 384:640] = out[:, 0:256].astype(BF)
    R.pm[...] = out[:, 256:384]


def project_early(R):
    first = R.first[...]
    out = mm(first, group_weight(R, 1, EARLY))
    R.pq[...] = out[:, 0:128]
    R.pkv[...] = out[:, 128:256]
    R.gate[...] = mm(first, group_weight(R, 0, EARLY))


def convolve(R):
    masks = [seg_mask(R, k) for k in range(1, 4)]
    for t in range(CW // 128):
        cols = slice(128 * t, 128 * t + 128)
        raw = R.raw[:, cols].astype(F32)
        total = R.cpar[4:5, cols] + R.cpar[0:1, cols] * raw
        for k in range(1, 4):
            total = total + R.cpar[k : k + 1, cols] * (roll(raw, k, 0) * masks[k - 1])
        R.pre[:, cols] = total
        R.mixed[:, cols] = total * sigmoid(total)


def steps(R):
    step = softplus(R.pm[...] + R.hpar[0:1, :])
    R.step[...] = step
    decay = -jnp.exp(R.hpar[1:2, :])
    ones = lower_ones()
    for b in range(4):
        rows = slice(b * ROWS, b * ROWS + ROWS)
        R.run[rows, :] = mm_terms(ones, decay * step[rows, :], 3)


def span(R, b):
    s = types.SimpleNamespace()
    s.at = pl.multiple_of(b * ROWS, ROWS)
    s.rows = pl.ds(s.at, ROWS)
    s.xs = R.mixed[s.rows, 0:384]
    s.xs_low = s.xs.astype(BF)
    s.wr_low = R.mixed[s.rows, 384:512].astype(BF)
    s.rd_low = R.mixed[s.rows, 512:640].astype(BF)
    s.step = R.step[s.rows, :]
    return s


def recurrence(R, begin, end):
    low = lane_low((ROWS, 128))

    def block(b, carry):
        s = span(R, b)
        run = R.run[s.rows, :]
        run_t = run.T
        seg = R.segc[s.rows, :]
        last = jnp.broadcast_to(seg[ROWS - 1 : ROWS, :], (ROWS, ROWS))
        earlier = R.segc[pl.ds(pl.multiple_of(jnp.maximum(s.at - 8, 0), 8), 8), :][7:8, :]
        earlier = jnp.where(jnp.broadcast_to(b, (1, 128)) == 0, -1.0, earlier)
        causal = (iota((ROWS, ROWS), 1) <= iota((ROWS, ROWS), 0)) & (
            seg == R.segr[0:1, s.rows]
        )
        inlet = jnp.where(seg == earlier, jnp.exp(run), 0.0)
        stop = run[ROWS - 1 : ROWS, :]
        tail0 = jnp.where(seg == last, jnp.exp(stop - run), 0.0)
        factor = jnp.where(last[0:1, :] == earlier, jnp.exp(stop), 0.0)
        inlet_x = spread_heads(inlet)
        step_x = spread_heads(s.step)
        tail_x = spread_heads(tail0)
        xstep = step_x * s.xs
        xstep_low = xstep.astype(BF)
        factor_x = spread_heads(jnp.broadcast_to(factor, (8, 128)))
        R.step_x[s.rows, :] = step_x
        R.factor[b] = jnp.broadcast_to(factor, (8, 128))
        R.inlet_x[s.rows, :] = inlet_x
        R.tail_x[s.rows, :] = tail_x
        R.factor_x[b] = factor_x
        cross = mm_nt(s.rd_low, s.wr_low)
        state = R.state[b]
        inflow = mm(s.rd_low, state.astype(BF))
        tiles = []
        for pair in range(HEADS // 2):
            xp = xstep_low[:, 128 * pair : 128 * pair + 128]
            both = []
            for h in (2 * pair, 2 * pair + 1):
                spread = run[:, h : h + 1] - run_t[h : h + 1, :]
                mix = jnp.exp(jnp.where(causal, spread, -10000.0))
                weights = (mix * cross).astype(BF)
                R.mix[b, h] = mix.astype(BF)
                R.weights[b, h] = weights
                both.append(mm(weights, xp))
            tiles.append(jnp.where(low, both[0], both[1]))
        R.ssm[s.rows, :] = (
            jnp.concatenate(tiles, axis=1) + inlet_x * inflow + R.cpar[5:6, 0:384] * s.xs
        )
        R.state[b + 1] = factor_x[0:1, :] * state + mm_tn(
            s.wr_low, (tail_x * xstep).astype(BF)
        )
        return carry

    lax.fori_loop(begin, end, block, 0)


def rotate(v, cosr, sinr):
    return v * cosr + swap_halves(v) * sinr


def rotated(R):
    low = lane_low((LEN, 128))
    R.q[...] = rotate(R.pq[...], R.cosr[...], R.sinr[...]).astype(BF)
    pkv = R.pkv[...]
    k = rotate(pkv, R.cosr[...], R.sinr[...])
    R.kk[...] = jnp.where(low, k, roll(k, 64, 1)).astype(BF)
    R.vv[...] = jnp.where(low, roll(pkv, 64, 1), pkv).astype(BF)


def half_only(v, e):
    low = lane_low(v.shape)
    return jnp.where(low if e == 0 else ~low, v, jnp.zeros_like(v))


def attend(R, begin, end):
    low = lane_low((ROWS, 128))
    for i in range(begin, end):
        rows = slice(i * ROWS, i * ROWS + ROWS)
        n = (i + 1) * ROWS
        seg_row = R.segr[0:1, 0:n]
        seg_col = jnp.broadcast_to(R.segc[rows, 0:1], (ROWS, n))
        allowed = (iota((ROWS, n), 1) <= iota((ROWS, n), 0) + i * ROWS) & (seg_col == seg_row)
        outs = []
        for e in range(2):
            scores = mm_nt(half_only(R.q[rows, :], e), R.kk[0:n, :]) * 0.125
            scores = jnp.where(allowed, scores, -1e30)
            shifted = jnp.exp(scores - jnp.max(scores, axis=-1, keepdims=True))
            probs = (shifted / jnp.sum(shifted, axis=-1, keepdims=True)).astype(BF)
            R.probs[e, rows, 0:n] = probs
            outs.append(mm(probs, R.vv[0:n, :]))
        R.left[rows, 384:512] = jnp.where(low, outs[0], outs[1]).astype(BF)


def out_project(R, h):
    rows = slice(256 * h, 256 * h + 256)
    gate = R.gate[rows, :]
    R.left[rows, 0:384] = (R.ssm[rows, :] * (gate * sigmoid(gate))).astype(BF)
    left = mm(R.left[rows, :], R.perm5[...]).astype(BF)
    R.left_p[rows, :] = left
    out = mm(left, out_weight(R))
    for j in range(4):
        R.branch[h, j] = out[64 * j : 64 * j + 64, :].astype(BF)


def unit_chunk(R, core, k):
    lo = FIN[0] + FW * (k % 2)
    return R.win[core, k // 2, :, :, :, lo : lo + FW].reshape(256, FW)


def ffn(R, h):
    second = R.secall[h].reshape(256, D)
    cot = R.cotall[2 * h : 2 * h + 2].reshape(256, D)
    rows = slice(256 * h, 256 * h + 256)
    for d in range(2):
        cols = slice(256 * d, 256 * d + 256)
        weights = []
        for core in range(2):
            parts = [unit_chunk(R, core, k)[:, cols] for k in range(4)]
            weights.append(jnp.concatenate(parts, axis=0))
        a = mm(second, weights[0])
        b = mm(second, weights[1])
        down = jnp.concatenate(
            [R.win[core, d, :, :, :, FOUT[0] : PK].reshape(256, 512) for core in range(2)], axis=1
        )
        ghid = mm_nt(cot, down)
        sig = sigmoid(a)
        act = a * sig
        R.hid[rows, cols] = (act * b).astype(BF)
        R.gab[rows, cols] = (ghid * b * (sig + act * (1.0 - sig))).astype(BF)
        R.gab[rows, FW + 256 * d : FW + 256 * d + 256] = (ghid * act).astype(BF)
    for k in range(4):
        weights = jnp.concatenate([unit_chunk(R, core, k) for core in range(2)], axis=1)
        out = mm_nt(R.gab[rows, :], weights)
        for j in range(4):
            R.gsec[h, j, :, 256 * k : 256 * k + 256] = out[64 * j : 64 * j + 64, :].astype(BF)


def ffn_out(R, L):
    out = mm(R.hid[...], out_weight(R, FOUT))
    for b in range(4):
        R.fout[b] = out[b * ROWS : b * ROWS + ROWS, :].astype(BF)
    for h in range(2):
        block, rows = mid_rows(L, h)
        R.fout[block, rows, :] = (
            R.fout[block, rows, :].astype(F32) + R.middle[h]
        ).astype(BF)


def ffn_grads(R):
    second = R.secall[...].reshape(LEN, D)
    for k in range(4):
        out = mm_tn(second[:, 256 * k : 256 * k + 256], R.gab[...]).astype(BF)
        lo = FIN[0] + FW * (k % 2)
        for core in range(2):
            part = out[:, FW * core : FW * core + FW]
            R.win[core, k // 2, :, :, :, lo : lo + FW] = part.reshape(4, 4, 16, FW)
    put_out_grad(R.win, FOUT, mm_tn(R.hid[...], R.cotall[...].reshape(LEN, D)))


def norm_back(x, gain, grad):
    inv = lax.rsqrt(jnp.mean(x * x, axis=-1, keepdims=True) + EPS)
    unit = x * inv
    scaled = grad * gain
    return inv * (scaled - unit * jnp.mean(scaled * unit, axis=-1, keepdims=True))


def mid_rows(L, h):
    return 2 * h + lax.div(L.z, 2), pl.ds(pl.multiple_of(64 * lax.rem(L.z, 2), 64), 64)


def back_out(R, h):
    rows = slice(256 * h, 256 * h + 256)
    raw = mm_nt(R.gball[h].reshape(256, D), out_weight(R))
    perm = R.perm5[...]
    hi = raw.astype(BF)
    rest = raw - hi.astype(F32)
    R.gleft[rows, :] = mm_nt(hi, perm) + mm_nt(rest.astype(BF), perm)


def back_gate(R):
    def block(b, carry):
        rows = pl.ds(pl.multiple_of(b * ROWS, ROWS), ROWS)
        gate = R.gate[rows, :]
        sig = sigmoid(gate)
        grad = R.gleft[rows, 0:384] * R.ssm[rows, :]
        R.gproj[rows, 768:1152] = (grad * (sig + gate * sig * (1.0 - sig))).astype(BF)
        return carry

    lax.fori_loop(0, 4, block, 0)


def back_attend(R, begin, end):
    low = lane_low((ROWS, 128))
    for i in range(begin, end):
        rows = slice(i * ROWS, i * ROWS + ROWS)
        n = (i + 1) * ROWS
        go = R.gleft[rows, 384:512].astype(BF)
        outs = []
        for e in range(2):
            probs = R.probs[e, rows, 0:n]
            pf = probs.astype(F32)
            go_e = half_only(go, e)
            dp = mm_nt(go_e, R.vv[0:n, :])
            ds = (pf * (dp - jnp.sum(pf * dp, axis=-1, keepdims=True))).astype(BF)
            outs.append(mm(ds, R.kk[0:n, :]))
            R.gk[0:n, :] += mm_tn(ds, half_only(R.q[rows, :], e))
            R.gv[0:n, :] += mm_tn(probs, go_e)
        R.gq[rows, :] = jnp.where(low, outs[0], outs[1]) * 0.125


def back_rotated(R):
    cosr, sinr = R.cosr[...], R.sinr[...]
    gq = rotate(R.gq[...], cosr, -sinr)
    R.gproj[:, 1152:1280] = gq.astype(BF)
    gk = R.gk[...] * 0.125
    gk = rotate(gk + roll(gk, 64, 1), cosr, -sinr)
    gv = R.gv[...]
    gv = gv + roll(gv, 64, 1)
    R.gproj[:, 1280:1408] = jnp.where(lane_low((LEN, 128)), gk, gv).astype(BF)
    R.gproj[:, 1408:1536] = jnp.zeros((LEN, 128), BF)


def back_recurrence(R, begin, end):
    low = lane_low((ROWS, 128))
    lane = iota((ROWS, 128), 1)
    sub = iota((ROWS, 128), 0)
    upper = (iota((ROWS, ROWS), 1) >= iota((ROWS, ROWS), 0)).astype(BF)

    def block(i, carry):
        b = 3 - i
        s = span(R, b)
        state = R.state[b]
        state_low = state.astype(BF)
        gstate = R.gstate[...]
        gstate_low = gstate.astype(BF)
        gate = R.gate[s.rows, :]
        gy = R.gleft[s.rows, 0:384] * (gate * sigmoid(gate))
        gy_low = gy.astype(BF)
        step_x = R.step_x[s.rows, :]
        tail_x = R.tail_x[s.rows, :]
        xstep = step_x * s.xs
        xstep_low = xstep.astype(BF)
        skip = R.cpar[5:6, 0:384]
        gcross = jnp.zeros((ROWS, ROWS), F32)
        tiles = []
        for pair in range(HEADS // 2):
            cols = slice(128 * pair, 128 * pair + 128)
            gp = gy_low[:, cols]
            both = []
            for e in range(2):
                h = 2 * pair + e
                both.append(mm_tn(R.weights[b, h], gp))
                gm = mm_nt(half_only(gp, e), xstep_low[:, cols])
                gcross = gcross + gm * R.mix[b, h].astype(F32)
            tiles.append(jnp.where(low, both[0], both[1]))
        inside = jnp.concatenate(tiles, axis=1)
        outflow = tail_x * mm(s.wr_low, gstate_low)
        flow_low = (R.inlet_x[s.rows, :] * gy).astype(BF)
        gcross_low = gcross.astype(BF)
        R.gmix[s.rows, 0:384] = (inside + outflow) * step_x + skip * gy
        R.gmix[s.rows, 384:512] = mm_tn(gcross_low, s.rd_low) + mm_nt(
            (tail_x * xstep).astype(BF), gstate_low
        )
        R.gmix[s.rows, 512:640] = mm(gcross_low, s.wr_low) + mm_nt(flow_low, state_low)
        ends = jnp.concatenate(
            [
                jnp.sum(gstate * state, axis=0, keepdims=True),
                jnp.sum(gy * s.xs, axis=0, keepdims=True),
                jnp.zeros((6, XW), F32),
            ],
            axis=0,
        )
        sums = sum_heads(
            jnp.concatenate(
                [
                    gy * (R.ssm[s.rows, :] - skip * s.xs),
                    inside * s.xs,
                    outflow * s.xs,
                    ends,
                ],
                axis=0,
            )
        )
        row_part = sums[0:ROWS, :]
        col_part = sums[ROWS : 2 * ROWS, :]
        through = sums[2 * ROWS : 3 * ROWS, :]
        gfactor = sums[3 * ROWS : 3 * ROWS + 1, :]
        grun = row_part - (col_part + through) * s.step
        at_end = (
            jnp.sum(through * s.step, axis=0, keepdims=True) + gfactor * R.factor[b, 0:1, :]
        )
        grun = grun + jnp.where(sub == ROWS - 1, at_end, 0.0)
        glog = mm_terms(upper, grun, 3)
        decay = -jnp.exp(R.hpar[1:2, :])
        gstep = col_part + through + glog * decay
        drive = R.pm[s.rows, :] + R.hpar[0:1, :]
        gdrive = jnp.where(lane < HEADS, gstep * sigmoid(drive), 0.0)
        R.gproj[s.rows, 640:768] = gdrive.astype(BF)
        R.hsum[0:1, :] += jnp.sum(gdrive, axis=0, keepdims=True)
        R.hsum[1:2, :] += jnp.sum(glog * decay * s.step, axis=0, keepdims=True)
        R.hsum[2:3, :] += sums[3 * ROWS + 1 : 3 * ROWS + 2, :]
        R.gstate[...] = R.factor_x[b, 0:1, :] * gstate + mm_tn(s.rd_low, flow_low)
        return carry

    lax.fori_loop(begin, end, block, 0)


def back_convolve(R):
    masks = [seg_mask(R, k) for k in range(1, 4)]
    for t in range(CW // 128):
        cols = slice(128 * t, 128 * t + 128)
        pre = R.pre[:, cols]
        raw = R.raw[:, cols].astype(F32)
        sig = sigmoid(pre)
        gpre = R.gmix[:, cols] * (sig + pre * sig * (1.0 - sig))
        graw = R.cpar[0:1, cols] * gpre
        R.small[0:1, cols] = jnp.sum(gpre * raw, axis=0, keepdims=True)
        for k in range(1, 4):
            masked = gpre * masks[k - 1]
            graw = graw + R.cpar[k : k + 1, cols] * roll(masked, LEN - k, 0)
            R.small[k : k + 1, cols] = jnp.sum(masked * roll(raw, k, 0), axis=0, keepdims=True)
        R.small[4:5, cols] = jnp.sum(gpre, axis=0, keepdims=True)
        R.gproj[:, cols] = graw.astype(BF)


def back_first(R, L):
    places = ((0, LATE), (1, LATE), (0, EARLY), (1, EARLY))
    gain = R.gain[0:1, :]
    moves = []
    for n, k in enumerate((2, 1, 3, 0)):
        b = L.around("z", k)
        rows = pl.ds(pl.multiple_of(b * ROWS, ROWS), ROWS)
        grads = R.gproj[rows, :]
        for q in range(4):
            weights = jnp.concatenate([chunk(R, core, kind, q) for core, kind in places], axis=1)
            R.gsum[:, 256 * q : 256 * q + 256] = mm_nt(grads, weights)
        R.gfirst[b] = norm_back(R.xall[b].astype(F32), gain, R.gsum[...]).astype(BF)
        for h in range(2):
            block, rows = mid_rows(L, h)

            @pl.when(block == b)
            def _():
                mine = R.gfirst[b, rows, :].astype(F32) + R.gmid[h]
                R.gfirst[b, rows, :] = mine.astype(BF)

        if k:
            moves.append(L.copy(R.gfirst.at[b], R.hrecv.at[n], L.device(z=b)))
        yield
    for one in moves:
        one.wait_recv()
    add_blocks(())(R.gfirst.at[L.z], [R.hrecv.at[n] for n in range(3)])


def put_out_grad(buf, kind, out):
    out = out.astype(BF)
    for core in range(2):
        for d in range(2):
            part = out[256 * d : 256 * d + 256, 512 * core : 512 * core + 512]
            buf[core, d, :, :, :, kind[0] : kind[0] + 512] = part.reshape(4, 4, 16, 512)


def out_grad(R):
    put_out_grad(R.dwin, OUT, mm_tn(R.left_p[...], R.gball[...].reshape(LEN, D)))


def put_grad(R, core, kind, k, value):
    lo = kind[0] + GW * (k % 2)
    R.dwin[core, k // 2, :, :, :, lo : lo + GW] = value.astype(BF).reshape(4, 4, 16, GW)


def early_grads(R):
    for k in range(4):
        out = mm_tn(R.first[:, 256 * k : 256 * k + 256], R.gproj[:, 768:1536])
        for core in range(2):
            put_grad(R, core, EARLY, k, out[:, GW * core : GW * core + GW])


def late_grads(R, sub):
    for k in (2 * sub, 2 * sub + 1):
        out = mm_tn(R.first[:, 256 * k : 256 * k + 256], R.gproj[:, 0:768])
        for core in range(2):
            put_grad(R, core, LATE, k, out[:, GW * core : GW * core + GW])


class Move:
    def __init__(self, one):
        self.one, self.came, self.went = one, False, False

    def wait_recv(self):
        if not self.came:
            self.one.wait_recv()
            self.came = True

    def wait_send(self):
        if not self.went:
            self.one.wait_send()
            self.went = True


class Links:
    def __init__(self, send, recv):
        self.send, self.recv, self.moves = send, recv, []
        self.z = lax.axis_index("ctx")
        place = lax.axis_index("fsdp")
        self.c = lax.rem(place, 2)
        self.x = lax.rem(lax.div(place, 2), 4)
        self.y = lax.div(place, 8)
        self.at = {"z": self.z, "y": self.y, "x": self.x}
        self.sibling = self.device(c=1 - self.c)

    def device(self, **moved):
        p = dict(z=self.z, y=self.y, x=self.x, c=self.c)
        p.update(moved)
        return (p["z"], (p["y"] * 4 + p["x"]) * 2 + p["c"])

    def copy(self, src, dst, device):
        k = len(self.moves)
        one = pltpu.make_async_remote_copy(
            src_ref=src,
            dst_ref=dst,
            send_sem=self.send.at[k],
            recv_sem=self.recv.at[k],
            device_id=device,
            device_id_type=MESH,
        )
        one.start()
        self.moves.append(Move(one))
        return self.moves[-1]

    def around(self, axis, k):
        return lax.rem(self.at[axis] + k, 4)

    def slab(self):
        for dz in range(4):
            for flip in range(2):
                if dz or flip:
                    yield self.around("z", dz), self.c if flip == 0 else 1 - self.c

    def greet(self):
        barrier = pltpu.get_barrier_semaphore()
        to = [self.device(z=j, c=h) for j, h in self.slab()]
        for axis in ("x", "y"):
            to += [self.device(**{axis: self.around(axis, k)}) for k in range(1, 4)]
        for one in to:
            pl.semaphore_signal(barrier, inc=1, device_id=one, device_id_type=MESH)
        return lambda: pl.semaphore_wait(barrier, len(to))

    def settle(self):
        for one in self.moves:
            one.wait_send()

    def finish(self):
        for one in self.moves:
            one.wait_recv()
            one.wait_send()


def gather(L, axis, slot, arrived=None, log=None):
    me = L.at[axis]
    moves = [
        (k, L.copy(slot(me), slot(me), L.device(**{axis: L.around(axis, k)}))) for k in (2, 1, 3)
    ]
    if log is not None:
        log.extend(one for _, one in moves)
    if arrived:
        arrived(me)
    yield
    for k, one in moves[1:] + moves[:1]:
        one.wait_recv()
        if arrived:
            arrived(L.around(axis, 4 - k))


def reduce(L, axis, src, bufs, add):
    moves = []
    for buf, k in zip(bufs, (2, 1, 3)):
        j = L.around(axis, k)
        moves.append(L.copy(src(j), buf, L.device(**{axis: j})))
    yield
    for one in moves:
        one.wait_recv()
    add(src(L.at[axis]), bufs)


def add_blocks(lead):
    count = int(np.prod(lead)) if lead else 1

    def add(dst, srcs):
        def body(n, carry):
            where = []
            for size in reversed(lead):
                where.append(lax.rem(n, size))
                n = lax.div(n, size)
            where = tuple(reversed(where)) + (slice(None), slice(None))
            total = dst[where].astype(F32)
            for one in srcs:
                total = total + one[where].astype(F32)
            dst[where] = total.astype(BF)
            return carry

        lax.fori_loop(0, count, body, 0, unroll=min(count, 4))

    return add


def columns(ref, lead, lo, width):
    return ref.at[(slice(None),) * (lead + 1) + (pl.ds(lo, width),)]


def step(*gens):
    for g in gens:
        next(g, None)


def together(*gens):
    gens = list(gens)
    while gens:
        alive = []
        for g in gens:
            try:
                next(g)
                alive.append(g)
            except StopIteration:
                pass
        gens = alive
        if gens:
            yield


def drain(*gens):
    for _ in together(*gens):
        pass


def mixer_slot(L, buf, sub, stage, lo, width):
    ref = buf.at[L.c, sub]
    axis = ("xy" if sub == 0 else "yx")[stage]

    def slot(j):
        if stage == 0:
            block = ref.at[L.y, j] if axis == "x" else ref.at[j, L.x]
        else:
            block = ref.at[j] if axis == "y" else ref.at[:, j]
        return columns(block, stage, lo, width)

    return axis, slot


def gather_near(L, R, sub, lo, width, log=None):
    axis, slot = mixer_slot(L, R.win, sub, 0, lo, width)
    return gather(L, axis, slot, None, log)


def gather_far(L, R, sub, lo, width, log=None):
    axis, slot = mixer_slot(L, R.win, sub, 1, lo, width)
    sent = []

    def arrived(j):
        sent.append(L.copy(slot(j), slot(j), L.sibling))

    yield from gather(L, axis, slot, arrived, log)
    if log is not None:
        log.extend(sent)
    yield
    for one in sent:
        one.wait_recv()


def gather_mixer(L, R, sub, lo, width, log=None):
    yield from gather_near(L, R, sub, lo, width, log)
    yield from gather_far(L, R, sub, lo, width, log)


def reduce_mixer(L, R, buf, lo, width, fill=None):
    moves = []
    for sub in range(2):
        if fill:
            fill(R, sub)
        theirs = columns(buf.at[1 - L.c, sub], 2, lo, width)
        moves.append(L.copy(theirs, columns(R.wsib.at[sub], 2, lo, width), L.sibling))
    yield
    gens = []
    for sub in range(2):
        moves[sub].wait_recv()
        mine = columns(buf.at[L.c, sub], 2, lo, width)
        add_blocks((4, 4))(mine, [columns(R.wsib.at[sub], 2, lo, width)])
        gens.append(reduce_chips(L, R, buf, sub, lo, width))
        next(gens[-1])
    yield
    yield from together(*gens)


def reduce_chips(L, R, buf, sub, lo, width):
    for stage in (1, 0):
        axis, slot = mixer_slot(L, buf, sub, stage, lo, width)
        bufs = [columns(one.at[sub], stage, lo, width) for one in R.mbufs[stage]]
        yield from reduce(L, axis, slot, bufs, add_blocks((4,) * stage))


def deal_rows(L, buf, kind, width, fin, rfin, place):
    for sub in range(2):
        for k in range(2):
            lo = kind[0] + width * k
            both = buf[L.c, sub, L.y, L.x, :, lo : lo + width].astype(F32)
            for core in range(2):
                fin[2 * sub + k, core, :, place : place + width] = both[8 * core : 8 * core + 8, :]
    cols = pl.ds(place, width)
    moves = [
        L.copy(fin.at[j, h, :, cols], rfin.at[L.z, L.c, :, cols], L.device(z=j, c=h))
        for j, h in L.slab()
    ]
    rfin[L.z, L.c, :, cols] = fin[L.z, L.c, :, cols]
    return moves


def deal_halves(L, buf, kind, fin, rfin):
    for d in range(2):
        fin[d] = buf[L.c, d, L.y, L.x, :, kind[0] : kind[0] + 512].astype(F32)
    return L.copy(fin.at[1 - L.c], rfin, L.sibling)


def reduce_late(L, R):
    yield from reduce_mixer(L, R, R.dwin, *LATE, fill=late_grads)
    moves = deal_rows(L, R.dwin, LATE, GW, R.fin, R.rfin, 0)
    yield
    for one in moves:
        one.wait_recv()


def reduce_early(L, R):
    yield from reduce_mixer(L, R, R.dwin, EARLY[0], EARLY[1] + OUT[1])
    moves = deal_rows(L, R.dwin, EARLY, GW, R.fin, R.rfin, GW)
    moves.append(deal_halves(L, R.dwin, OUT, R.ofin, R.orfin))
    yield
    for one in moves:
        one.wait_recv()
    lo, hi = in_core_order(L, R.ofin[L.c], R.orfin[...])
    R.o_mo[:, 0:512] = lo[0:12, :]
    R.o_mo[:, 512:1024] = hi[0:12, :]
    R.o_ao[:, 0:512] = lo[12:16, :]
    R.o_ao[:, 512:1024] = hi[12:16, :]
    R.send_out("o_mo", "o_ao")


def reduce_ffn(L, R):
    yield from reduce_mixer(L, R, R.win, *FFN)
    moves = deal_rows(L, R.win, FIN, FW, R.ffin, R.frfin, 0)
    moves.append(deal_halves(L, R.win, FOUT, R.dfin, R.drfin))
    yield
    for one in moves:
        one.wait_recv()
    lo, hi = in_core_order(L, R.dfin[L.c], R.drfin[...])
    R.o_fd[:, 0:512] = lo
    R.o_fd[:, 512:1024] = hi
    turn = (iota((FW, FW), 1) == deal(iota((FW, 1), 0))).astype(BF)
    rows = [R.frfin[j, core] for core in range(2) for j in range(4)]
    out = mm_terms(jnp.concatenate(rows, axis=0), turn, 3)
    for j in range(4):
        R.o_fg[:, FW * j : FW * j + FW] = out[8 * j : 8 * j + 8, :]
        R.o_fu[:, FW * j : FW * j + FW] = out[32 + 8 * j : 40 + 8 * j, :]
    R.gcol[0] = gain_column([(R.w_fg, R.o_fg), (R.w_fu, R.o_fu)], R.gain_mid)
    R.send_out("o_fd", "o_fg", "o_fu")


def reduce_blocks(L, ref, recv):
    return reduce(L, "z", lambda j: ref.at[j], [recv.at[n] for n in range(3)], add_blocks(()))


def gather_blocks(L, ref):
    return gather(L, "z", lambda j: ref.at[j])


def reduce_small(L, R):
    for part in range(3):
        R.small[5:6, 128 * part : 128 * part + 128] = R.hsum[part : part + 1, :]
    R.smc[L.c] = R.small[...]
    move = L.copy(R.smc.at[L.c], R.smc.at[L.c], L.sibling)
    yield
    move.wait_recv()
    R.smx[L.x] = R.smc[0] + R.smc[1]
    yield from gather(L, "x", lambda j: R.smx.at[j])
    R.smy[L.y] = (R.smx[0] + R.smx[1]) + (R.smx[2] + R.smx[3])
    yield from gather(L, "y", lambda j: R.smy.at[j])
    R.smz[L.z] = (R.smy[0] + R.smy[1]) + (R.smy[2] + R.smy[3])
    yield from gather(L, "z", lambda j: R.smz.at[j])
    for j in range(4):
        R.o_conv[:, 384 * j : 384 * j + 384] = R.smz[j, :, 0:384]
    total = (R.smz[0] + R.smz[1]) + (R.smz[2] + R.smz[3])
    R.o_conv[:, 1536:1792] = total[:, 384:640]
    lane = iota((8, 128), 1)
    for part in range(3):
        heads = jnp.zeros((8, 128), F32)
        for j in range(4):
            one = jnp.where(lane < HEADS, R.smz[j, :, 128 * part : 128 * part + 128], 0.0)
            heads = heads + (one if j == 0 else roll(one, HEADS * j, 1))
        R.o_head[part : part + 1, :] = heads[5:6, :]


def setup(L, R):
    lane = iota((1, 128), 1)
    first = HEADS * L.z
    for row, ref in enumerate((R.step_bias, R.decay_log)):
        total = jnp.zeros((1, 128), F32)
        for h in range(HEADS):
            total = jnp.where(lane == h, ref[first + h], total)
        R.hpar[row : row + 1, :] = total
    cols = pl.ds(pl.multiple_of(XW * L.z, 128), XW)
    R.cpar[0:4, 0:384] = R.taps[:, cols]
    R.cpar[0:4, 384:640] = R.taps[:, 1536:1792]
    R.cpar[4:5, 0:384] = R.bias[cols].reshape(1, 384)
    R.cpar[4:5, 384:640] = R.bias[1536:1792].reshape(1, 256)
    lane = iota((1, XW), 1) >> 6
    total = jnp.zeros((1, XW), F32)
    for h in range(HEADS):
        total = jnp.where(lane == h, R.skip_gain[first + h], total)
    R.cpar[5:6, 0:384] = total
    seg = R.seg[...].astype(F32)
    R.segr[0:1, :] = seg
    for b in range(4):
        row = seg[:, b * ROWS : b * ROWS + ROWS]
        R.segc[b * ROWS : b * ROWS + ROWS, :] = jnp.broadcast_to(row, (ROWS, ROWS)).T


def pack_weights(L, R):
    shape8 = (8, 128)
    low = lane_low(shape8)
    lane = iota(shape8, 1)
    sub = iota(shape8, 0)
    k, v = R.w_k[...], R.w_v[...]
    k_up, v_up = roll(k, 64, 1), roll(v, 64, 1)
    R.misc[...] = jnp.zeros(shape8, F32)
    R.misc[:, 0:24] = R.w_step[...]
    misc = R.misc[...]
    for row in range(8):
        misc = jnp.where((lane == 24) & (sub == row), R.gain_in[row], misc)
        misc = jnp.where((lane == 25) & (sub == row), R.gain_mid[row], misc)
    for j in range(4):
        R.pack[j, 0, :, 0:384] = R.w_min[:, 1536 + 384 * j : 1920 + 384 * j]
        R.pack[j, 0, :, 384:768] = R.w_min[:, 384 * j : 384 * j + 384]
        R.pack[j, 1, :, 0:256] = R.w_bc[...]
        mine = misc if j == 0 else roll(misc, 128 - HEADS * j, 1)
        R.pack[j, 1, :, 256:384] = jnp.where(
            lane < HEADS, mine, jnp.where((lane >= 24) & (lane < 26), misc, 0.0)
        )
        R.pack[j, 1, :, 384:512] = R.w_q[:, 128 * j : 128 * j + 128]
        R.pack[j, 1, :, 512:640] = jnp.where(low, k, v_up) if j < 2 else jnp.where(low, k_up, v)
        R.pack[j, 1, :, 640:768] = jnp.zeros(shape8, F32)
    for h in range(2):
        R.opack[h, 0:12, :] = R.w_mo[:, 512 * h : 512 * h + 512]
        R.opack[h, 12:16, :] = R.w_ao[:, 512 * h : 512 * h + 512]


def deal(n):
    return 32 * ((n & 255) >> 4) + 16 * (n >> 8) + (n & 15)


def pack_ffn(L, R):
    turn = (iota((FW, FW), 0) == deal(iota((1, FW), 1))).astype(BF)
    rows = [ref[:, FW * j : FW * j + FW] for ref in (R.w_fg, R.w_fu) for j in range(4)]
    out = mm(jnp.concatenate(rows, axis=0).astype(BF), turn)
    for j in range(4):
        R.fpack[j, 0] = out[8 * j : 8 * j + 8, :]
        R.fpack[j, 1] = out[32 + 8 * j : 40 + 8 * j, :]
    for h in range(2):
        R.dpack[h] = R.w_fd[:, 512 * h : 512 * h + 512]


def gain_column(pairs, scalars):
    total = jnp.zeros((8, 1), F32)
    for weight, grad in pairs:
        weight = weight[...].astype(BF).astype(F32)
        total = total + jnp.sum(weight * grad[...], axis=1, keepdims=True)
    sub = iota((8, 128), 0)
    gain = jnp.ones((8, 128), F32)
    for row in range(8):
        gain = jnp.where(sub == row, scalars[row], gain)
    return total / gain.astype(BF).astype(F32)


def unpack_early(R):
    low = lane_low((8, 128))
    for j in range(4):
        R.o_min[:, 384 * j : 384 * j + 384] = R.rfin[j, 0, :, 384:768]
        R.o_q[:, 128 * j : 128 * j + 128] = R.rfin[j, 1, :, 384:512]
    kv0 = R.rfin[0, 1, :, 512:640] + R.rfin[1, 1, :, 512:640]
    kv1 = R.rfin[2, 1, :, 512:640] + R.rfin[3, 1, :, 512:640]
    R.o_k[...] = jnp.where(low, kv0, roll(kv1, 64, 1))
    R.o_v[...] = jnp.where(low, roll(kv0, 64, 1), kv1)
    pairs = [(R.w_min.at[:, 0:1536], R.o_min.at[:, 0:1536])]
    pairs += [(R.w_q, R.o_q), (R.w_k, R.o_k), (R.w_v, R.o_v)]
    R.gcol[1] = gain_column(pairs, R.gain_in)
    R.send_out("o_q", "o_k", "o_v")


def unpack_late(R):
    lane = iota((8, 128), 1)
    misc = jnp.zeros((8, 128), F32)
    for j in range(4):
        R.o_min[:, 1536 + 384 * j : 1920 + 384 * j] = R.rfin[j, 0, :, 0:384]
        own = jnp.where(lane < HEADS, R.rfin[j, 1, :, 256:384], 0.0)
        misc = misc + (own if j == 0 else roll(own, HEADS * j, 1))
    R.o_misc[...] = misc
    R.o_bc[...] = (R.rfin[0, 1, :, 0:256] + R.rfin[1, 1, :, 0:256]) + (
        R.rfin[2, 1, :, 0:256] + R.rfin[3, 1, :, 0:256]
    )
    R.send_out("o_min", "o_bc", "o_misc")
    pairs = [(R.w_min.at[:, 1536:3072], R.o_min.at[:, 1536:3072])]
    pairs += [(R.w_bc, R.o_bc), (R.w_step, R.o_misc.at[:, 0:24])]
    first = R.gcol[1] + gain_column(pairs, R.gain_in)
    both = jnp.where(iota((8, 128), 1) == 0, first, R.gcol[0])
    turned = jnp.concatenate([both, jnp.zeros((120, 128), F32)], axis=0).T
    R.o_head[3:5, :] = turned[0:2, :]
    R.send_out("o_head")


def in_core_order(L, mine, other):
    first = L.c == 0
    return jnp.where(first, mine, other), jnp.where(first, other, mine)


def own_rows(L, R, exch, kinds, width):
    for sub in range(2):
        for k in range(2):
            both = jnp.concatenate([exch[2 * sub + k, d] for d in range(2)], axis=0).astype(BF)
            for n, kind in enumerate(kinds):
                lo = kind[0] + width * k
                R.win[L.c, sub, L.y, L.x, :, lo : lo + width] = both[:, width * n : width * n + width]


def own_halves(L, R, pack, other, kind):
    for d, part in enumerate(in_core_order(L, pack[L.c], other[...])):
        R.win[L.c, d, L.y, L.x, :, kind[0] : kind[0] + 512] = part.astype(BF)


def to_slab(L, pack, exch):
    moves = [L.copy(pack.at[j, h], exch.at[L.z, L.c], L.device(z=j, c=h)) for j, h in L.slab()]
    exch[L.z, L.c] = pack[L.z, L.c]
    return moves


def come(*moves):
    for one in moves:
        one.wait_recv()


def middle_rows(L, R, h):
    block, rows = mid_rows(L, h)
    total = R.xall[block, rows, :].astype(F32) + R.branch[h, L.z].astype(F32)
    for n in range(3):
        total = total + R.zrecv[h, n].astype(F32)
    R.middle[h] = total
    inv = lax.rsqrt(jnp.mean(total * total, axis=-1, keepdims=True) + EPS)
    R.secall[h, L.z] = (total * inv * R.gain[1:2, :]).astype(BF)


def back_middle(L, R, h):
    block, rows = mid_rows(L, h)
    total = R.gsec[h, L.z].astype(F32)
    for n in range(3):
        total = total + R.zrecv[2 + h, n].astype(F32)
    gmid = norm_back(R.middle[h], R.gain[1:2, :], total)
    gmid = gmid + R.cotall[block, rows, :].astype(F32)
    R.gmid[h] = gmid
    R.gball[h, L.z] = gmid.astype(BF)


def keep(dst, srcs):
    pass


def to_owner(L, R, ref, n):
    return reduce(L, "z", lambda j: ref.at[j], [R.zrecv.at[n, k] for k in range(3)], keep)


def kernel(R):
    L = Links(R.send, R.recv)
    greeted = L.greet()
    R.await_in(*WEIGHTS_IN)
    pack_weights(L, R)
    R.await_in("tok", "cot")
    R.xall[L.z] = R.tok[...]
    R.cotall[L.z] = R.cot[...]
    greeted()

    moves = to_slab(L, R.pack, R.exch)
    wo = L.copy(R.opack.at[1 - L.c], R.exo, L.sibling)
    R.await_in("seg", "taps", "bias")
    setup(L, R)
    R.await_in("w_fg", "w_fu", "w_fd")
    pack_ffn(L, R)
    come(wo)
    own_halves(L, R, R.opack, R.exo, OUT)
    come(*moves)
    own_rows(L, R, R.exch, (LATE, EARLY), GW)
    near = together(*[gather_near(L, R, sub, 0, FIN[0]) for sub in range(2)])
    step(near)
    xgen = gather_blocks(L, R.xall)
    step(xgen)
    fmoves = to_slab(L, R.fpack, R.fexch)
    do = L.copy(R.dpack.at[1 - L.c], R.dexo, L.sibling)
    drain(near)
    late, early, out = [
        together(*[gather_far(L, R, sub, *kind) for sub in range(2)])
        for kind in (LATE, EARLY, OUT)
    ]
    step(late)
    step(early)
    step(out)
    R.small[...] = jnp.zeros((8, CW), F32)
    R.gk[...] = jnp.zeros((LEN, 128), F32)
    R.gv[...] = jnp.zeros((LEN, 128), F32)
    R.state[0] = jnp.zeros((128, XW), F32)
    R.gstate[...] = jnp.zeros((128, XW), F32)
    R.hsum[...] = jnp.zeros((8, 128), F32)
    step(late)
    drain(late)
    gains(R)
    drain(xgen)
    cgen = gather_blocks(L, R.cotall)
    step(cgen)
    norm_first(R)
    project_late(R)
    step(early)
    convolve(R)
    step(out)
    come(do, *fmoves)
    own_rows(L, R, R.fexch, (FIN,), FW)
    own_halves(L, R, R.dpack, R.dexo, FOUT)
    fsent = []
    fgen = together(*[gather_mixer(L, R, sub, *FFN, fsent) for sub in range(2)])
    step(fgen)
    steps(R)
    recurrence(R, 0, 2)
    drain(early)
    project_early(R)
    R.await_in("cosr", "sinr", "perm5")
    rotated(R)
    attend(R, 0, 2)
    step(fgen)
    drain(out)
    out_project(R, 0)
    branch = [to_owner(L, R, R.branch.at[h], h) for h in range(2)]
    step(branch[0])
    recurrence(R, 2, 4)
    attend(R, 2, 4)
    out_project(R, 1)
    step(branch[1])
    second = [gather_blocks(L, R.secall.at[h]) for h in range(2)]
    for h in range(2):
        drain(branch[h])
        middle_rows(L, R, h)
        step(second[h])
        step(fgen)
    drain(cgen, fgen)
    gsec = [to_owner(L, R, R.gsec.at[h], 2 + h) for h in range(2)]
    for h in range(2):
        drain(second[h])
        ffn(R, h)
        step(gsec[h])
    gball = [gather_blocks(L, R.gball.at[h]) for h in range(2)]
    for one in fsent:
        one.wait_send()
    ffn_out(R, L)
    drain(gsec[0])
    back_middle(L, R, 0)
    step(gball[0])
    ffn_grads(R)
    wgen = reduce_ffn(L, R)
    step(wgen)
    drain(gsec[1])
    back_middle(L, R, 1)
    step(gball[1])
    step(wgen)
    drain(gball[0])
    back_out(R, 0)
    back_attend(R, 0, 2)
    drain(gball[1])
    fout = reduce_blocks(L, R.fout, R.frecv)
    step(fout)
    back_out(R, 1)
    back_gate(R)
    back_attend(R, 2, 4)
    back_rotated(R)
    step(wgen)
    out_grad(R)
    early_grads(R)
    egen = reduce_early(L, R)
    step(egen)
    back_recurrence(R, 0, 2)
    step(egen)
    step(wgen)
    back_recurrence(R, 2, 4)
    back_convolve(R)
    lgen = reduce_late(L, R)
    step(lgen)
    mgen = reduce_small(L, R)
    step(mgen)
    hgen = back_first(R, L)
    step(hgen)
    step(lgen, mgen)
    step(hgen)
    step(hgen)
    step(hgen)
    step(mgen)
    step(egen)
    step(lgen)
    step(mgen)
    step(egen)
    step(lgen)
    drain(wgen, fout)
    R.o_out[...] = R.fout[L.z]
    R.send_out("o_out")
    drain(egen)
    unpack_early(R)
    drain(mgen)
    R.send_out("o_conv")
    drain(hgen)
    R.o_tok[...] = R.gfirst[L.z]
    R.send_out("o_tok")
    drain(lgen)
    unpack_late(R)
    L.finish()
    R.finish_out()


INS = dict(
    w_min=((8, 3072), F32),
    w_bc=((8, 256), F32),
    w_step=((8, 24), F32),
    w_q=((8, 512), F32),
    w_k=((8, 128), F32),
    w_v=((8, 128), F32),
    w_mo=((12, D), F32),
    w_ao=((4, D), F32),
    tok=((ROWS, D), BF),
    cot=((ROWS, D), BF),
    w_fg=((8, 2048), F32),
    w_fu=((8, 2048), F32),
    w_fd=((16, D), F32),
    seg=((1, LEN), jnp.int32),
    taps=((4, 1792), F32),
    bias=((1792,), F32),
    cosr=((LEN, 128), F32),
    sinr=((LEN, 128), F32),
    perm5=((512, 512), BF),
)
WEIGHTS_IN = list(INS)[:8]
SCALARS = ("gain_in", "gain_mid", "step_bias", "decay_log", "skip_gain")
OUTS = dict(
    o_out=((ROWS, D), BF),
    o_tok=((ROWS, D), BF),
    o_min=((8, 3072), F32),
    o_bc=((8, 256), F32),
    o_misc=((8, 128), F32),
    o_q=((8, 512), F32),
    o_k=((8, 128), F32),
    o_v=((8, 128), F32),
    o_mo=((12, D), F32),
    o_ao=((4, D), F32),
    o_fg=((8, 2048), F32),
    o_fu=((8, 2048), F32),
    o_fd=((16, D), F32),
    o_conv=((8, 1792), F32),
    o_head=((8, 128), F32),
)
SCRATCH = dict(
    xall=((4, ROWS, D), BF),
    segc=((LEN, 128), F32),
    segr=((8, LEN), F32),
    cpar=((8, CW), F32),
    hpar=((8, 128), F32),
    misc=((8, 128), F32),
    pack=((4, 2, 8, 768), F32),
    exch=((4, 2, 8, 768), F32),
    opack=((2, 16, 512), F32),
    exo=((16, 512), F32),
    fpack=((4, 2, 8, FW), F32),
    fexch=((4, 2, 8, FW), F32),
    dpack=((2, 16, 512), F32),
    dexo=((16, 512), F32),
    win=((2, 2, 4, 4, 16, PK), BF),
    dwin=((2, 2, 4, 4, 16, FIN[0]), BF),
    cotall=((4, ROWS, D), BF),
    secall=((2, 4, 64, D), BF),
    hid=((LEN, FW), BF),
    gab=((LEN, 2 * FW), BF),
    gsec=((2, 4, 64, D), BF),
    fout=((4, ROWS, D), BF),
    gain=((8, D), F32),
    gcol=((2, 8, 128), F32),
    first=((LEN, D), BF),
    gate=((LEN, XW), F32),
    raw=((LEN, CW), BF),
    pq=((LEN, 128), F32),
    pkv=((LEN, 128), F32),
    pm=((LEN, 128), F32),
    pre=((LEN, CW), F32),
    mixed=((LEN, CW), F32),
    step=((LEN, 128), F32),
    run=((LEN, 128), F32),
    state=((5, 128, XW), F32),
    ssm=((LEN, XW), F32),
    q=((LEN, 128), BF),
    kk=((LEN, 128), BF),
    vv=((LEN, 128), BF),
    probs=((2, LEN, LEN), BF),
    left=((LEN, 512), BF),
    left_p=((LEN, 512), BF),
    branch=((2, 4, 64, D), BF),
    zrecv=((4, 3, 64, D), BF),
    frecv=((3, ROWS, D), BF),
    hrecv=((3, ROWS, D), BF),
    middle=((2, 64, D), F32),
    gmid=((2, 64, D), F32),
    gsum=((ROWS, D), F32),
    gball=((2, 4, 64, D), BF),
    gleft=((LEN, 512), F32),
    gq=((LEN, 128), F32),
    gk=((LEN, 128), F32),
    gv=((LEN, 128), F32),
    gstate=((128, XW), F32),
    hsum=((8, 128), F32),
    gmix=((LEN, CW), F32),
    gproj=((LEN, 4 * GW), BF),
    small=((8, CW), F32),
    factor=((4, 8, 128), F32),
    inlet_x=((LEN, XW), F32),
    tail_x=((LEN, XW), F32),
    factor_x=((4, 8, XW), F32),
    step_x=((LEN, XW), F32),
    mix=((4, HEADS, ROWS, ROWS), BF),
    weights=((4, HEADS, ROWS, ROWS), BF),
    gfirst=((4, ROWS, D), BF),
    wsib=((2, 4, 4, 16, PK), BF),
    smc=((2, 8, CW), F32),
    smx=((4, 8, CW), F32),
    smy=((4, 8, CW), F32),
    smz=((4, 8, CW), F32),
    fin=((4, 2, 8, 768), F32),
    rfin=((4, 2, 8, 768), F32),
    ofin=((2, 16, 512), F32),
    orfin=((16, 512), F32),
    ffin=((4, 2, 8, FW), F32),
    frfin=((4, 2, 8, FW), F32),
    dfin=((2, 16, 512), F32),
    drfin=((16, 512), F32),
)
COPIES = 250


def ring_buffers(parts, width, stages):
    shapes = {}
    for stage in range(stages):
        for n in range(3):
            shapes[(stage, n)] = ((parts,) + (4,) * stage + (16, width), BF)
    return shapes


MBUFS = ring_buffers(2, PK, 2)


def entry(*refs):
    refs = list(refs)
    take = lambda names: [(name, refs.pop(0)) for name in names]
    given, scalars, results = dict(take(INS)), take(SCALARS), dict(take(OUTS))
    inside = take(INS)
    R = types.SimpleNamespace(**dict(scalars + inside + take(OUTS) + take(SCRATCH)))
    bufs = dict(take(MBUFS))
    R.mbufs = [[bufs[key] for key in MBUFS if key[0] == stage] for stage in range(2)]
    R.send, R.recv, came, left = refs
    loads = {}
    for n, name in enumerate(INS):
        loads[name] = pltpu.make_async_copy(given[name], getattr(R, name), came.at[n])
        loads[name].start()
    stores = []

    def await_in(*names):
        for name in names:
            loads[name].wait()

    def send_out(*names):
        for name in names:
            n = len(stores)
            stores.append(pltpu.make_async_copy(getattr(R, name), results[name], left.at[n]))
            stores[-1].start()

    def finish_out():
        for one in stores:
            one.wait()

    R.await_in, R.send_out, R.finish_out = await_in, send_out, finish_out
    kernel(R)


def layer(*args):
    anywhere = pl.BlockSpec(memory_space=pl.ANY)
    smem = pl.BlockSpec(memory_space=pltpu.SMEM)
    shapes = [*INS.values(), *OUTS.values(), *SCRATCH.values(), *MBUFS.values()]
    scratch = [pltpu.VMEM(shape, kind) for shape, kind in shapes]
    scratch += [pltpu.SemaphoreType.DMA((n,)) for n in (COPIES, COPIES, len(INS), len(OUTS))]
    return pl.pallas_call(
        entry,
        out_shape=[jax.ShapeDtypeStruct(shape, kind) for shape, kind in OUTS.values()],
        in_specs=[anywhere] * len(INS) + [smem] * len(SCALARS),
        out_specs=[anywhere] * len(OUTS),
        scratch_shapes=scratch,
        compiler_params=pltpu.CompilerParams(
            collective_id=0, has_side_effects=True, vmem_limit_bytes=63 * 2**20
        ),
    )(*args)


SAME = [name for name in OUTS if name not in ("o_misc", "o_conv", "o_head")]
RESULTS = {name: OUTS[name] for name in SAME}
RESULTS.update(
    step=((8, 24), F32),
    taps=((4, 1792), F32),
    bias=((1792,), F32),
    gain_in=((8,), F32),
    gain_mid=((8,), F32),
    step_bias=((24,), F32),
    decay_log=((24,), F32),
    skip_gain=((24,), F32),
)


def deliver_kernel(*refs):
    given = dict(zip(OUTS, refs))
    result = dict(zip(RESULTS, refs[len(OUTS) :]))
    for name in SAME:
        result[name][...] = given[name][...]
    result["step"][...] = given["o_misc"][:, 0:24]
    result["taps"][...] = given["o_conv"][0:4, :]
    result["bias"][...] = given["o_conv"][4, :]
    head = given["o_head"]
    for row, name in enumerate(("step_bias", "decay_log", "skip_gain")):
        result[name][...] = head[row, 0:24]
    result["gain_in"][...] = head[3, 0:8]
    result["gain_mid"][...] = head[4, 0:8]


def deliver(outs):
    vmem = pl.BlockSpec(memory_space=pltpu.VMEM)
    results = pl.pallas_call(
        deliver_kernel,
        out_shape=[jax.ShapeDtypeStruct(shape, kind) for shape, kind in RESULTS.values()],
        in_specs=[vmem] * len(OUTS),
        out_specs=[vmem] * len(RESULTS),
    )(*outs)
    return dict(zip(RESULTS, results))


def rotary_tables():
    lane = np.arange(128)
    power = (-2.0 * (lane % 32).astype(np.float32) / np.float32(64)).astype(np.float32)
    frequency = np.power(np.float32(ROPE), power).astype(np.float32)
    angles = np.arange(LEN, dtype=np.float32)[:, None] * frequency[None, :]
    sign = np.where(lane % 64 < 32, -1.0, 1.0)
    cosine = np.cos(angles.astype(np.float64)).astype(np.float32)
    sine = (np.sin(angles.astype(np.float64)) * sign).astype(np.float32)
    return cosine, sine


def out_order():
    n = np.arange(512)
    device = np.where(n < 384, n // 12, (n - 384) // 4)
    row = np.where(n < 384, n % 12, 12 + (n - 384) % 4)
    to = (device % 2) * 256 + (device // 2) * 16 + row
    table = np.zeros((512, 512), np.float32)
    table[n, to] = 1.0
    return table


def shards(
    tokens,
    segments,
    cotangent,
    gain_in,
    mamba_in,
    mamba_bc,
    mamba_step,
    in_query,
    in_key,
    in_value,
    mamba_out,
    attn_out,
    gain_mid,
    ffn_gate,
    ffn_up,
    ffn_down,
    conv_taps,
    conv_bias,
    step_bias,
    decay_log,
    skip_gain,
):
    cosine, sine = rotary_tables()
    outs = layer(
        mamba_in,
        mamba_bc,
        mamba_step,
        in_query,
        in_key,
        in_value,
        mamba_out,
        attn_out,
        tokens[0],
        cotangent[0],
        ffn_gate,
        ffn_up,
        ffn_down,
        segments,
        conv_taps,
        conv_bias,
        jnp.asarray(cosine),
        jnp.asarray(sine),
        jnp.asarray(out_order(), BF),
        gain_in,
        gain_mid,
        step_bias,
        decay_log,
        skip_gain,
    )
    r = deliver(outs)
    return (
        r["o_out"][None],
        r["o_tok"][None],
        r["gain_in"],
        r["o_min"],
        r["o_bc"],
        r["step"],
        r["o_q"],
        r["o_k"],
        r["o_v"],
        r["o_mo"],
        r["o_ao"],
        r["gain_mid"],
        r["o_fg"],
        r["o_fu"],
        r["o_fd"],
        r["taps"],
        r["bias"],
        r["step_bias"],
        r["decay_log"],
        r["skip_gain"],
    )


def solution(mesh):
    one = P(("ctx", "fsdp"))
    rows = P(("ctx", "fsdp"), None)
    block = P("fsdp", "ctx", None)
    return jax.shard_map(
        shards,
        mesh=mesh,
        in_specs=(block, P("fsdp", None), block, one)
        + (rows,) * 8
        + (one,)
        + (rows,) * 3
        + (P(),) * 5,
        out_specs=(block, block, one) + (rows,) * 8 + (one,) + (rows,) * 3 + (P(),) * 5,
        check_vma=False,
    )
```
